128 devices in a mesh: dom: 64 (over x, y, z_hi, core), feat: 2 (over z_lo).
Axes of the slice: x: 4, y: 4, z: 4 (z_hi: 2, z_lo: 2; z = z_hi * 2 + z_lo), core: 2. Of those that a mesh axis runs over, the one named last changes fastest.
Arguments:
- features: bfloat16 [65536, 128], P('dom', 'feat'), may hold values from -6 to 6
- weight: bfloat16 [128, 256], P('feat'), may hold values from -0.5 to 0.5
- stale_cache: bfloat16 [65536, 256], P(None, 'feat'), may hold values from -6 to 6
- adj_tiles: bfloat16 [49152, 128, 128], P('dom'), may hold values from -0.0546875 to 0.0546875
- tile_src: int32 [49152], P('dom'), may hold values from 0 to 511
- tile_dst: int32 [49152], P('dom'), may hold values from 0 to 7
- tile_count: int32 [64], P('dom'), may hold values from 153 to 768, as said below
- refresh: int32 [64, 256], replicated, may hold values from 0 to 1023, as said below
- train_mask: int32 [65536], P('dom'), may hold values 0 or 1
- grad_hidden: bfloat16 [65536, 256], P('dom', 'feat'), may hold values from -6 to 6
Outputs:
- hidden: bfloat16 [65536, 256], P('dom', 'feat')
- grad_features: bfloat16 [65536, 128], P('dom', 'feat')
- grad_weight: float32 [128, 256], P('feat')
The draws below stay inside these ranges and needn't reach their ends.
Inputs may be any that keep to these rules, and one draw needn't show every extreme that they name: `tile_count`: some partition has all 768 slots live. `refresh`: the 256 entries of one partition are distinct.
All inputs are finite; a program needn't handle non-finite values. No bound on the sum of `train_mask` on one device may be relied on, other than what follows from the above.
Results may differ from the reference program's by a relative error of at most 0.027.
Values may be sent and summed in bfloat16 or wider, within the bound.
A program may use at most 256 MiB of HBM per device.

```python
import jax
import jax.numpy as jnp
from jax import lax

F = 128
HID = 256
TILE = 128
TILE_DEG = 96
ROWS = 1024
REF = 256
NT = 768
NODES = 65536
N_DOM = 64


def draw_tile_count(key, part):
    key = jax.random.fold_in(key, 11)
    first_key, second_key = jax.random.split(key)
    divisor = jax.random.randint(first_key, (N_DOM,), 1, 6)
    counts = NT // divisor
    busiest = jax.random.randint(second_key, (), 0, N_DOM)
    return jnp.where(jnp.arange(N_DOM) == busiest, NT, counts).astype(jnp.int32)


def one_order(sub_key):
    return jax.random.permutation(sub_key, ROWS)


def draw_refresh(key, part):
    key = jax.random.fold_in(key, 23)
    sub_keys = jax.random.split(key, N_DOM)
    orders = jax.vmap(one_order)(sub_keys)
    return orders[:, :REF].astype(jnp.int32)


def set_ends(values, rng, least, largest):
    longest = values.shape.index(max(values.shape))
    spots = []
    for shift in (0, 1):
        where = [jax.random.randint(jax.random.fold_in(rng, axis), (), 0, length) for axis, length in enumerate(values.shape)]
        where[longest] = (where[longest] + shift) % values.shape[longest]
        spots.append(tuple(where))
    return values.at[spots[0]].set(least).at[spots[1]].set(largest)


def steps_of(rng, extent, cuts, low, top_value):
    loudness = 1.0
    for dim, parts in cuts:
        draws = jax.random.uniform(jax.random.fold_in(jax.random.fold_in(rng, 6), dim), (parts,), jnp.float32, low / len(cuts), top_value / len(cuts))
        loudness = loudness * jnp.repeat(jnp.exp(draws), extent[dim] // parts).reshape((-1,) + (1,) * (len(extent) - 1 - dim))
    return loudness


def gaussian(rng, dims, spread, bound, cuts=(), kind=jnp.bfloat16):
    array = jax.random.normal(rng, dims, jnp.float32) * spread
    if len(cuts) > 0:
        array = steps_of(rng, dims, cuts, -0.22, 0.18) * array
    return jnp.clip(array, min=-bound, max=bound).astype(kind)


def setup_inputs(seed: int = 0) -> dict:
    splits = jax.random.split(jax.random.key(seed), 11)
    features = gaussian(splits[0], (NODES, F), 1.0, 6.0, ((0, 64), (1, 2)))
    weight = gaussian(splits[1], (F, HID), F ** -0.5, 0.5, ((0, 2),))
    stale_cache = gaussian(splits[2], (NODES, HID), 1.0, 6.0, ((1, 2),))
    adj_tiles = gaussian(splits[3], (N_DOM * NT, TILE, TILE), (TILE * TILE_DEG) ** -0.5, 0.0546875, ((0, 64),))
    tile_src = set_ends(jax.random.randint(splits[4], (N_DOM * NT,), 0, NODES // TILE), jax.random.fold_in(splits[4], 1), 0, (NODES // TILE) - 1).astype(jnp.int32)
    tile_dst = set_ends(jax.random.randint(splits[5], (N_DOM * NT,), 0, ROWS // TILE), jax.random.fold_in(splits[5], 1), 0, (ROWS // TILE) - 1).astype(jnp.int32)
    tile_count = draw_tile_count(jax.random.fold_in(splits[10], 71), 0)
    refresh = draw_refresh(jax.random.fold_in(splits[10], 71), 0)
    train_mask = set_ends((jax.random.randint(splits[8], (NODES,), 0, 2) < 1).astype(jnp.int32), jax.random.fold_in(splits[8], 1), 0, 1)
    grad_hidden = gaussian(splits[9], (NODES, HID), 1.0, 6.0, ((0, 64), (1, 2)))
    return dict(features=features, weight=weight, stale_cache=stale_cache, adj_tiles=adj_tiles, tile_src=tile_src, tile_dst=tile_dst, tile_count=tile_count, refresh=refresh, train_mask=train_mask, grad_hidden=grad_hidden)


def reference(features, weight, stale_cache, adj_tiles, tile_src, tile_dst, tile_count, refresh, train_mask, grad_hidden):
    highest = lax.Precision.HIGHEST
    per_part = ROWS // TILE
    all_blocks = N_DOM * per_part
    fresh_rows = jnp.dot(features, weight, preferred_element_type=jnp.float32).astype(jnp.bfloat16)
    offsets = jnp.arange(N_DOM, dtype=jnp.int32)[:, None] * ROWS
    global_rows = (offsets + refresh.astype(jnp.int32)).reshape(-1).astype(jnp.int32)
    stale_rows = stale_cache.at[global_rows].set(fresh_rows[global_rows])
    fresh_blocks = fresh_rows.reshape(all_blocks, TILE, HID)
    stale_blocks = stale_rows.reshape(all_blocks, TILE, HID)
    tiles_by_part = adj_tiles.reshape(N_DOM, NT, TILE, TILE)
    sources = tile_src.reshape(N_DOM, NT)
    targets = tile_dst.reshape(N_DOM, NT)
    slot_ids = jnp.arange(NT, dtype=jnp.int32)
    local_blocks = jnp.arange(per_part, dtype=jnp.int32)
    owners = jnp.arange(N_DOM, dtype=jnp.int32)

    def forward_part(packed):
        owner_id, tiles_here, src_here, dst_here, live_count = packed
        live_mask = (slot_ids < live_count).astype(jnp.float32)
        inside = (src_here // per_part) == owner_id
        source = jnp.where(inside[:, None, None], fresh_blocks[src_here], stale_blocks[src_here])
        product = jnp.einsum("tij,tjc->tic", tiles_here.astype(jnp.float32), source.astype(jnp.float32), precision=highest)
        onehot = (dst_here[:, None] == local_blocks[None, :]).astype(jnp.float32) * live_mask[:, None]
        return jnp.einsum("tb,tic->bic", onehot, product, precision=highest).reshape(ROWS, HID)

    pre_act = lax.map(forward_part, (owners, tiles_by_part, sources, targets, tile_count)).reshape(N_DOM * ROWS, HID)
    hidden = jnp.maximum(pre_act, 0.0).astype(jnp.bfloat16)
    pass_mask = train_mask.astype(jnp.float32)[:, None] * (pre_act > 0).astype(jnp.float32)
    delta_rows = (grad_hidden.astype(jnp.float32) * pass_mask).astype(jnp.bfloat16)
    delta_blocks = delta_rows.reshape(N_DOM, per_part, TILE, HID)

    def backward_part(carried, packed):
        own_acc, other_acc = carried
        owner_id, tiles_here, src_here, dst_here, live_count, delta_here = packed
        live_mask = (slot_ids < live_count).astype(jnp.float32)
        inside = ((src_here // per_part) == owner_id).astype(jnp.float32)
        contrib = jnp.einsum("tji,tjc->tic", tiles_here.astype(jnp.float32), delta_here[dst_here].astype(jnp.float32), precision=highest)
        contrib = contrib * live_mask[:, None, None]
        own_acc = own_acc.at[src_here].add(contrib * inside[:, None, None])
        other_acc = other_acc.at[src_here].add(contrib * (1.0 - inside)[:, None, None])
        return (own_acc, other_acc), None

    zero_acc = jnp.zeros((all_blocks, TILE, HID), jnp.float32)
    (own_acc, other_acc), unused = lax.scan(backward_part, (zero_acc, zero_acc), (owners, tiles_by_part, sources, targets, tile_count, delta_blocks))
    chosen = jnp.zeros((N_DOM * ROWS,), jnp.float32).at[global_rows].set(1.0)
    grad_fresh = (own_acc.reshape(-1, HID) + other_acc.reshape(-1, HID) * chosen[:, None]).astype(jnp.bfloat16)
    grad_weight = jnp.dot(features.T, grad_fresh, preferred_element_type=jnp.float32)
    grad_features = jnp.dot(grad_fresh, weight.T, preferred_element_type=jnp.float32).astype(jnp.bfloat16)
    return (hidden, grad_features, grad_weight)
```

```python
import jax
import jax.numpy as jnp
from jax import lax
from jax.experimental import pallas as pl
from jax.experimental.pallas import tpu as pltpu
from jax.sharding import PartitionSpec as P

MESH = pl.DeviceIdType.MESH
BF16 = jnp.bfloat16
F32 = jnp.float32
I32 = jnp.int32

ROWS = 1024
REF = 256
TILE = 128
NT = 768
PARTS = 64
BLOCKS = PARTS * ROWS // TILE
PER = ROWS // TILE
RING = 4
CLASS = PARTS // 2
MIB = 1024 * 1024


def dot(lhs, rhs):
    return jnp.dot(lhs, rhs, preferred_element_type=F32)


class Place:
    def __init__(self):
        self.dom = lax.axis_index("dom")
        self.feat = lax.axis_index("feat")
        self.core = self.dom % 2
        self.z = (self.dom // 2) % 2
        self.y = (self.dom // 4) % RING
        self.x = self.dom // 16
        self.a = self.x * (1 - self.core) + self.y * self.core
        self.b = self.y * (1 - self.core) + self.x * self.core
        self.sibling = self.dom + 1 - 2 * self.core
        self.z_pair = self.dom + 2 - 4 * self.z
        self.a_next = self.at(self.a + 1, self.b)
        self.a_prev = self.at(self.a + 3, self.b)
        self.b_next = self.at(self.a, self.b + 1)
        self.b_prev = self.at(self.a, self.b + 3)

    def at(self, a, b):
        a, b = a % RING, b % RING
        x = a * (1 - self.core) + b * self.core
        y = b * (1 - self.core) + a * self.core
        return ((x * RING + y) * 2 + self.z) * 2 + self.core

    def xy(self, x, y):
        return (((x % RING) * RING + y % RING) * 2 + self.z) * 2 + self.core

    def slot(self, a, b, z):
        return self.core * CLASS + (b % RING) * 8 + (a % RING) * 2 + z

    def greet(self):
        barrier = pltpu.get_barrier_semaphore()
        near = (self.sibling, self.z_pair, self.a_next, self.a_prev, self.b_next, self.b_prev)
        for device in near:
            pl.semaphore_signal(barrier, inc=1, device_id=(device, self.feat), device_id_type=MESH)
        pl.semaphore_signal(
            barrier, inc=1, device_id=(self.dom, 1 - self.feat), device_id_type=MESH
        )
        return lambda: pl.semaphore_wait(barrier, len(near) + 1)


def slot_part(slot):
    core, b, a, z = slot // CLASS, (slot // 8) % RING, (slot // 2) % RING, slot % 2
    x = a * (1 - core) + b * core
    y = b * (1 - core) + a * core
    return ((x * RING + y) * 2 + z) * 2 + core


def part_slot(part):
    core, z, y, x = part % 2, (part // 2) % 2, (part // 4) % RING, part // 16
    a = x * (1 - core) + y * core
    b = y * (1 - core) + x * core
    return core * CLASS + b * 8 + a * 2 + z


def rows_by_refresh(row):
    column = jnp.transpose(jnp.broadcast_to(row, (TILE, REF)))
    lanes = lax.broadcasted_iota(I32, (REF, TILE), 1)
    parts = [(column == lanes + k * TILE).astype(F32).astype(BF16) for k in range(PER)]
    return jnp.concatenate(parts, axis=1)


def refresh_by_rows(row):
    rows = lax.broadcasted_iota(I32, (ROWS, REF), 0)
    return (rows == row).astype(F32).astype(BF16)


def gather_kernel(
    feat_ref,
    w_ref,
    refresh_ref,
    arr_out,
    fx_out,
    wcol_out,
    arr,
    pick,
    pick_in,
    wide,
    wide_in,
    wcol,
    send_sem,
    recv_sem,
    pair_send,
    pair_recv,
    out_sem,
):
    me = Place()
    ready = me.greet()
    f = me.feat
    spread_to = lax.broadcasted_iota(I32, (64, TILE), 1)
    spread_from = lax.broadcasted_iota(I32, (64, TILE), 0)
    spread = (spread_to == spread_from + f * 64).astype(F32).astype(BF16)
    wide[...] = dot(feat_ref[...], spread).astype(BF16)
    chosen = rows_by_refresh(refresh_ref[pl.ds(me.dom, 1), :])
    pick[...] = dot(chosen, wide[...]).astype(BF16)
    ready()

    def to_pair(k, src, dst):
        return pltpu.make_async_remote_copy(
            src_ref=src,
            dst_ref=dst,
            send_sem=pair_send.at[k],
            recv_sem=pair_recv.at[k],
            device_id=(me.dom, 1 - f),
            device_id_type=MESH,
        )

    own_columns = pl.ds(pl.multiple_of(f * TILE, TILE), TILE)
    pair_columns = pl.ds(pl.multiple_of((1 - f) * TILE, TILE), TILE)
    own_rows = pl.ds(pl.multiple_of(f * 64, 64), 64)
    pick_copy = to_pair(0, pick, pick_in)
    pick_copy.start()
    w_copy = to_pair(1, w_ref.at[:, pair_columns], wcol.at[own_rows, :])
    w_copy.start()
    wide_copy = to_pair(2, wide, wide_in)
    wide_copy.start()
    wcol_out[own_rows, :] = w_ref[:, own_columns]

    sends = []

    def send(slot, target):
        copy = pltpu.make_async_remote_copy(
            src_ref=arr.at[slot],
            dst_ref=arr.at[slot],
            send_sem=send_sem.at[len(sends)],
            recv_sem=recv_sem.at[slot],
            device_id=(target, f),
            device_id_type=MESH,
        )
        copy.start()
        sends.append(copy)

    def arrive(slot):
        pltpu.make_async_remote_copy(
            src_ref=arr.at[slot],
            dst_ref=arr.at[slot],
            send_sem=send_sem.at[0],
            recv_sem=recv_sem.at[slot],
            device_id=(me.sibling, f),
            device_id_type=MESH,
        ).wait_recv()

    a, b, z, o = me.a, me.b, me.z, 1 - me.z
    mine = me.slot(a, b, z)
    pick_copy.wait_recv()
    arr[pl.ds(mine, 1)] = (pick[...] + pick_in[...])[None]

    def spread_b(slot):
        send(slot, me.b_next)
        send(slot, me.b_prev)
        send(slot, me.sibling)

    send(mine, me.z_pair)
    send(mine, me.a_next)
    send(mine, me.a_prev)
    spread_b(mine)

    slot = me.slot(a, b, o)
    arrive(slot)
    send(slot, me.a_next)
    send(slot, me.a_prev)
    spread_b(slot)

    slot = me.slot(a + 3, b, z)
    arrive(slot)
    send(slot, me.a_next)
    spread_b(slot)
    slot = me.slot(a + 1, b, z)
    arrive(slot)
    spread_b(slot)

    def ring_b(aa, zz):
        slot = me.slot(aa, b + 3, zz)
        arrive(slot)
        if zz is z:
            send(slot, me.b_next)
        send(slot, me.sibling)
        slot = me.slot(aa, b + 1, zz)
        arrive(slot)
        if zz is not z:
            send(slot, me.b_prev)
        send(slot, me.sibling)

    ring_b(a, z)
    slot = me.slot(a + 3, b, o)
    arrive(slot)
    spread_b(slot)
    slot = me.slot(a + 1, b, o)
    arrive(slot)
    send(slot, me.a_prev)
    spread_b(slot)
    ring_b(a, o)
    slot = me.slot(a + 2, b, z)
    arrive(slot)
    spread_b(slot)
    slot = me.slot(a + 2, b, o)
    arrive(slot)
    spread_b(slot)
    ring_b(a + 3, z)
    ring_b(a + 1, z)
    ring_b(a + 3, o)
    ring_b(a + 1, o)
    ring_b(a + 2, z)
    ring_b(a + 2, o)
    for aa, zz in (
        (a, z),
        (a, o),
        (a + 3, z),
        (a + 1, z),
        (a + 3, o),
        (a + 1, o),
        (a + 2, z),
        (a + 2, o),
    ):
        slot = me.slot(aa, b + 2, zz)
        arrive(slot)
        send(slot, me.sibling)

    def keep(k, first):
        part = pl.ds(first, CLASS)
        return pltpu.make_async_copy(arr.at[part], arr_out.at[part], out_sem.at[k])

    keep_own = keep(0, me.core * CLASS)
    keep_own.start()
    wide_copy.wait_recv()
    fx_out[...] = wide[...] + wide_in[...]
    w_copy.wait_recv()
    wcol_out[pl.ds(pl.multiple_of((1 - f) * 64, 64), 64), :] = wcol[
        pl.ds(pl.multiple_of((1 - f) * 64, 64), 64), :
    ]
    other = (1 - me.core) * CLASS
    for k in range(CLASS):
        arrive(other + k)
    keep_other = keep(1, other)
    keep_other.start()
    for copy in sends:
        copy.wait_send()
    pick_copy.wait_send()
    w_copy.wait_send()
    wide_copy.wait_send()
    keep_own.wait()
    keep_other.wait()


CHUNK = 12
AHEAD = 10
UNROLL = 8


def forward_kernel(
    src_ref,
    dst_ref,
    count_ref,
    refresh_ref,
    fx_ref,
    wcol_ref,
    mask_ref,
    gh_ref,
    arr_hbm,
    stale_hbm,
    tiles_hbm,
    hidden_ref,
    delta_ref,
    source,
    tiles,
    arr,
    acc,
    stale_sem,
    arr_sem,
    tile_sem,
):
    me = lax.axis_index("dom")
    live = count_ref[0]

    def stale_copy(slot):
        rows = pl.ds(pl.multiple_of(slot_part(slot) * ROWS, ROWS), ROWS)
        return pltpu.make_async_copy(stale_hbm.at[rows], source.at[rows], stale_sem.at[slot])

    def arr_copy(slot):
        return pltpu.make_async_copy(arr_hbm.at[slot], arr.at[slot], arr_sem.at[slot])

    def tile_copy(chunk):
        part = pl.ds(chunk * CHUNK, CHUNK)
        return pltpu.make_async_copy(tiles_hbm.at[part], tiles.at[part], tile_sem.at[chunk])

    def first(slot, carry):
        stale_copy(slot).start()
        arr_copy(slot).start()
        return carry

    lax.fori_loop(0, AHEAD, first, 0)
    acc[...] = jnp.zeros_like(acc)
    wcol = wcol_ref[...]
    ones = jnp.ones((REF, TILE), BF16)

    def merge(slot, carry):
        @pl.when(slot + AHEAD < PARTS)
        def _():
            stale_copy(slot + AHEAD).start()
            arr_copy(slot + AHEAD).start()

        @pl.when(slot * CHUNK < live)
        def _():
            tile_copy(slot).start()

        part = slot_part(slot)
        arr_copy(slot).wait()
        fresh = dot(arr[pl.ds(slot, 1)][0], wcol).astype(BF16)
        chosen = refresh_by_rows(refresh_ref[pl.ds(part, 1), :])
        placed = dot(chosen, jnp.concatenate([fresh, ones], axis=1))
        stale_copy(slot).wait()
        rows = pl.ds(pl.multiple_of(part * ROWS, ROWS), ROWS)
        old = source[rows, :].astype(F32)
        source[rows, :] = jnp.where(placed[:, TILE:] > 0, placed[:, :TILE], old).astype(BF16)
        return carry

    lax.fori_loop(0, PARTS, merge, 0)
    own = pl.ds(pl.multiple_of(me * ROWS, ROWS), ROWS)
    source[own, :] = dot(fx_ref[...], wcol).astype(BF16)

    def wait_chunk(chunk, carry):
        tile_copy(chunk).wait()
        return carry

    lax.fori_loop(0, (live + CHUNK - 1) // CHUNK, wait_chunk, 0)

    def step(index, carry):
        for k in range(UNROLL):
            t = index * UNROLL + k
            rows = pl.ds(pl.multiple_of(src_ref[t] * TILE, TILE), TILE)
            product = dot(tiles[t], source[rows, :])
            d = jnp.where(t < live, dst_ref[t], PER)
            acc[pl.ds(d, 1)] = acc[pl.ds(d, 1)] + product[None]
        return carry

    lax.fori_loop(0, (live + UNROLL - 1) // UNROLL, step, 0)

    for d in range(PER):
        pre = acc[d]
        rows = pl.ds(d * TILE, TILE)
        hidden_ref[rows, :] = jnp.maximum(pre, 0.0).astype(BF16)
        passed = jnp.where(pre > 0, gh_ref[rows, :].astype(F32), 0.0)
        kept = mask_ref[pl.ds(d, 1), :].astype(F32)
        delta_ref[d] = (jnp.transpose(passed) * kept).astype(BF16)


B_CHUNK = 32
B_RING = 4


def backward_kernel(
    src_ref,
    dst_ref,
    count_ref,
    refresh_ref,
    fx_ref,
    delta_ref,
    arr_hbm,
    tiles_hbm,
    picked_hbm,
    own_ref,
    gw_ref,
    acc,
    tiles,
    arr,
    picked,
    gw_total,
    tile_sem,
    arr_sem,
    out_sem,
):
    me = lax.axis_index("dom")
    live = count_ref[0]
    chunks = (live + B_CHUNK - 1) // B_CHUNK

    def tile_copy(chunk):
        part = pl.ds(chunk * B_CHUNK, B_CHUNK)
        place = chunk % B_RING
        return pltpu.make_async_copy(tiles_hbm.at[part], tiles.at[place], tile_sem.at[place])

    for k in range(B_RING - 1):

        @pl.when(k < chunks)
        def _():
            tile_copy(k).start()

    arr_copy = pltpu.make_async_copy(arr_hbm, arr, arr_sem)
    arr_copy.start()

    def clear(block, carry):
        acc[pl.ds(block, 1)] = jnp.zeros((1, TILE, TILE), F32)
        return carry

    lax.fori_loop(0, BLOCKS + 1, clear, 0)

    def take_chunk(chunk, carry):
        @pl.when(chunk + B_RING - 1 < chunks)
        def _():
            tile_copy(chunk + B_RING - 1).start()

        tile_copy(chunk).wait()
        place = chunk % B_RING

        def step(index, carry):
            for k in range(UNROLL):
                local = index * UNROLL + k
                t = chunk * B_CHUNK + local
                product = dot(delta_ref[dst_ref[t]], tiles[place, local])
                s = jnp.where(t < live, src_ref[t], BLOCKS)
                acc[pl.ds(s, 1)] = acc[pl.ds(s, 1)] + product[None]
            return carry

        return lax.fori_loop(0, B_CHUNK // UNROLL, step, carry)

    lax.fori_loop(0, chunks, take_chunk, 0)
    arr_copy.wait()
    gw_total[...] = jnp.zeros_like(gw_total)

    def out_copy(slot):
        return pltpu.make_async_copy(picked.at[slot], picked_hbm.at[slot], out_sem.at[slot])

    def pick(slot, carry):
        part = slot_part(slot)
        chosen = refresh_by_rows(refresh_ref[pl.ds(part, 1), :])
        blocks = [acc[part * PER + k].astype(BF16) for k in range(PER)]
        grads = dot(jnp.concatenate(blocks, axis=1), chosen)
        grads = jnp.where(part == me, 0.0, grads).astype(BF16)
        picked[pl.ds(slot, 1)] = grads[None]
        out_copy(slot).start()
        gw_total[...] += dot(grads, arr[pl.ds(slot, 1)][0])
        return carry

    lax.fori_loop(0, PARTS, pick, 0)
    for k in range(PER):
        own_ref[:, pl.ds(k * TILE, TILE)] = acc[me * PER + k]
    gw = gw_total[...] + dot(own_ref[...].astype(BF16), fx_ref[...])
    gw_ref[...] = jnp.transpose(gw)

    def wait_out(slot, carry):
        out_copy(slot).wait()
        return carry

    lax.fori_loop(0, PARTS, wait_out, 0)


def scatter_kernel(
    refresh_ref,
    w_ref,
    own_ref,
    gw_ref,
    picked_hbm,
    gf_out,
    gw_out,
    work,
    sib,
    from_b1,
    from_b2,
    from_a1,
    from_a2,
    from_z,
    sums,
    sums_in,
    gw_in,
    grad,
    grad_in,
    load_sem,
    send_sem,
    recv_sem,
):
    me = Place()
    ready = me.greet()
    f, a, b, z = me.feat, me.a, me.b, me.z
    loads = []
    for k, chunk in enumerate((b + 2, b + 1, b + 3, b)):
        first = (chunk % RING) * 8
        copy = pltpu.make_async_copy(
            picked_hbm.at[pl.ds(me.core * CLASS + first, 8)],
            work.at[pl.ds(first, 8)],
            load_sem.at[k],
        )
        copy.start()
        loads.append(copy)
    sums[0] = gw_ref[...]
    ready()
    sends = []

    def send(src, dst, target, feat=None):
        k = len(sends)
        copy = pltpu.make_async_remote_copy(
            src_ref=src,
            dst_ref=dst,
            send_sem=send_sem.at[k],
            recv_sem=recv_sem.at[k],
            device_id=(target, f if feat is None else feat),
            device_id_type=MESH,
        )
        copy.start()
        sends.append(copy)
        return copy

    y_one = me.xy(me.x, me.y + 1 + 2 * (me.y % 2))
    y_two = me.xy(me.x, me.y + 3 - 2 * (me.y % 2))
    x_one = me.xy(me.x + 1 + 2 * (me.x % 2), me.y)
    x_two = me.xy(me.x + 3 - 2 * (me.x % 2), me.y)
    partners = (me.sibling, y_one, y_two, x_one, x_two, me.z_pair)

    def sum_send(k):
        return send(sums.at[k], sums_in.at[k], partners[k])

    def sum_take(k, copy):
        copy.wait_recv()
        sums[k + 1] = sums[k] + sums_in[k]

    def add(ref, first, size, *others):
        part = pl.ds(first, size)
        total = ref[part].astype(F32)
        for other in others:
            total = total + other.astype(F32)
        ref[part] = total.astype(BF16)

    gw_copy = sum_send(0)
    to_sib = []
    for chunk in (a + 2, a + 1, a + 3, a):
        first = (chunk % RING) * 8
        src = picked_hbm.at[pl.ds((1 - me.core) * CLASS + first, 8)]
        to_sib.append(send(src, sib.at[pl.ds(first, 8)], me.sibling))

    def fold(k, chunk):
        first = (chunk % RING) * 8
        loads[k].wait()
        to_sib[k].wait_recv()
        add(work, first, 8, sib[pl.ds(first, 8)])
        return first

    across = fold(0, b + 2)
    b1_up = send(work.at[pl.ds(across, 4)], from_b1.at[pl.ds(0, 4)], me.b_next)
    b1_down = send(work.at[pl.ds(across + 4, 4)], from_b1.at[pl.ds(4, 4)], me.b_prev)
    up = fold(1, b + 1)
    b2_up_late = send(work.at[pl.ds(up + 4, 4)], from_b2.at[0, pl.ds(4, 4)], me.b_next)
    down = fold(2, b + 3)
    b2_down_early = send(work.at[pl.ds(down, 4)], from_b2.at[1, pl.ds(0, 4)], me.b_prev)
    sum_take(0, gw_copy)
    gw_copy = sum_send(1)
    here = fold(3, b)
    b1_up.wait_recv()
    add(work, up, 4, from_b1[pl.ds(0, 4)])
    b2_up_early = send(work.at[pl.ds(up, 4)], from_b2.at[0, pl.ds(0, 4)], me.b_next)
    b1_down.wait_recv()
    add(work, down + 4, 4, from_b1[pl.ds(4, 4)])
    b2_down_late = send(work.at[pl.ds(down + 4, 4)], from_b2.at[1, pl.ds(4, 4)], me.b_prev)
    sum_take(1, gw_copy)
    gw_copy = sum_send(2)
    sum_take(2, gw_copy)
    gw_copy = sum_send(3)
    b2_up_late.wait_recv()
    b2_down_early.wait_recv()
    b2_up_early.wait_recv()
    b2_down_late.wait_recv()
    add(work, here, 8, from_b2[0], from_b2[1])

    across = here + ((a + 2) % RING) * 2
    up = here + ((a + 1) % RING) * 2
    down = here + ((a + 3) % RING) * 2
    mine = here + a * 2
    a1_up = send(work.at[pl.ds(across, 1)], from_a1.at[pl.ds(0, 1)], me.a_next)
    a1_down = send(work.at[pl.ds(across + 1, 1)], from_a1.at[pl.ds(1, 1)], me.a_prev)
    a2_up_late = send(work.at[pl.ds(up + 1, 1)], from_a2.at[0, pl.ds(1, 1)], me.a_next)
    a2_down_early = send(work.at[pl.ds(down, 1)], from_a2.at[1, pl.ds(0, 1)], me.a_prev)
    sum_take(3, gw_copy)
    gw_copy = sum_send(4)
    a1_up.wait_recv()
    add(work, up, 1, from_a1[pl.ds(0, 1)])
    a2_up_early = send(work.at[pl.ds(up, 1)], from_a2.at[0, pl.ds(0, 1)], me.a_next)
    a1_down.wait_recv()
    add(work, down + 1, 1, from_a1[pl.ds(1, 1)])
    a2_down_late = send(work.at[pl.ds(down + 1, 1)], from_a2.at[1, pl.ds(1, 1)], me.a_prev)
    chosen = rows_by_refresh(refresh_ref[pl.ds(me.dom, 1), :])
    sum_take(4, gw_copy)
    gw_copy = sum_send(5)
    a2_up_late.wait_recv()
    a2_down_early.wait_recv()
    a2_up_early.wait_recv()
    a2_down_late.wait_recv()
    add(work, mine, 2, from_a2[0], from_a2[1])
    z_copy = send(work.at[pl.ds(mine + 1 - z, 1)], from_z, me.z_pair)
    sum_take(5, gw_copy)
    other_rows = pl.ds(pl.multiple_of((1 - f) * 64, 64), 64)
    own_rows = pl.ds(pl.multiple_of(f * 64, 64), 64)
    swap = send(sums.at[6, other_rows, :], gw_in, me.dom, 1 - f)
    z_copy.wait_recv()
    carried = work[pl.ds(mine + z, 1)][0].astype(F32) + from_z[0].astype(F32)
    grad[...] = (own_ref[...] + dot(carried.astype(BF16), chosen)).astype(BF16)
    grad_copy = send(grad, grad_in, me.dom, 1 - f)
    own_columns = pl.ds(pl.multiple_of(f * TILE, TILE), TILE)
    other_columns = pl.ds(pl.multiple_of((1 - f) * TILE, TILE), TILE)
    half = dot(w_ref[:, own_columns], grad[...])
    swap.wait_recv()
    gw_out[:, own_columns] = sums[6, own_rows, :]
    gw_out[:, other_columns] = gw_in[...]
    grad_copy.wait_recv()
    half = half + dot(w_ref[:, other_columns], grad_in[...])
    gf_out[...] = jnp.transpose(half).astype(BF16)
    for copy in sends:
        copy.wait_send()


VMEM = pl.BlockSpec(memory_space=pltpu.VMEM)
SMEM = pl.BlockSpec(memory_space=pltpu.SMEM)
ANY = pl.BlockSpec(memory_space=pl.ANY)
DMA = pltpu.SemaphoreType.DMA


def shape(dims, kind):
    return jax.ShapeDtypeStruct(dims, kind)


def shards(
    features,
    weight,
    stale_cache,
    adj_tiles,
    tile_src,
    tile_dst,
    tile_count,
    refresh,
    train_mask,
    grad_hidden,
):
    arr, fx, wcol = pl.pallas_call(
        gather_kernel,
        out_shape=(
            shape((PARTS, REF, TILE), BF16),
            shape((ROWS, TILE), BF16),
            shape((TILE, TILE), BF16),
        ),
        in_specs=[VMEM, VMEM, VMEM],
        out_specs=(ANY, VMEM, VMEM),
        scratch_shapes=[
            pltpu.VMEM((PARTS, REF, TILE), BF16),
            pltpu.VMEM((REF, TILE), BF16),
            pltpu.VMEM((REF, TILE), BF16),
            pltpu.VMEM((ROWS, TILE), BF16),
            pltpu.VMEM((ROWS, TILE), BF16),
            pltpu.VMEM((TILE, TILE), BF16),
            DMA((63,)),
            DMA((PARTS,)),
            DMA((3,)),
            DMA((3,)),
            DMA((2,)),
        ],
        compiler_params=pltpu.CompilerParams(
            collective_id=0, has_side_effects=True, vmem_limit_bytes=32 * MIB
        ),
        name="gather_refreshed",
    )(features, weight, refresh)
    hidden, delta = pl.pallas_call(
        forward_kernel,
        out_shape=(shape((ROWS, TILE), BF16), shape((PER, TILE, TILE), BF16)),
        in_specs=[SMEM, SMEM, SMEM, VMEM, VMEM, VMEM, VMEM, VMEM, ANY, ANY, ANY],
        out_specs=(VMEM, VMEM),
        scratch_shapes=[
            pltpu.VMEM((PARTS * ROWS, TILE), BF16),
            pltpu.VMEM((NT, TILE, TILE), BF16),
            pltpu.VMEM((PARTS, REF, TILE), BF16),
            pltpu.VMEM((PER + 1, TILE, TILE), F32),
            DMA((PARTS,)),
            DMA((PARTS,)),
            DMA((NT // CHUNK,)),
        ],
        compiler_params=pltpu.CompilerParams(vmem_limit_bytes=60 * MIB),
        name="forward_tiles",
    )(
        tile_src,
        tile_dst,
        tile_count,
        refresh,
        fx,
        wcol,
        train_mask.reshape(PER, TILE),
        grad_hidden,
        arr,
        stale_cache,
        adj_tiles,
    )
    picked, own, gw = pl.pallas_call(
        backward_kernel,
        out_shape=(
            shape((PARTS, TILE, REF), BF16),
            shape((TILE, ROWS), F32),
            shape((TILE, TILE), F32),
        ),
        in_specs=[SMEM, SMEM, SMEM, VMEM, VMEM, VMEM, ANY, ANY],
        out_specs=(ANY, VMEM, VMEM),
        scratch_shapes=[
            pltpu.VMEM((BLOCKS + 1, TILE, TILE), F32),
            pltpu.VMEM((B_RING, B_CHUNK, TILE, TILE), BF16),
            pltpu.VMEM((PARTS, REF, TILE), BF16),
            pltpu.VMEM((PARTS, TILE, REF), BF16),
            pltpu.VMEM((TILE, TILE), F32),
            DMA((B_RING,)),
            DMA,
            DMA((PARTS,)),
        ],
        compiler_params=pltpu.CompilerParams(vmem_limit_bytes=60 * MIB),
        name="backward_tiles",
    )(tile_src, tile_dst, tile_count, refresh, fx, delta, arr, adj_tiles)
    grad_features, grad_weight = pl.pallas_call(
        scatter_kernel,
        out_shape=(shape((ROWS, 64), BF16), shape((64, 2 * TILE), F32)),
        in_specs=[VMEM, VMEM, VMEM, VMEM, ANY],
        out_specs=(VMEM, VMEM),
        scratch_shapes=[
            pltpu.VMEM((CLASS, TILE, REF), BF16),
            pltpu.VMEM((CLASS, TILE, REF), BF16),
            pltpu.VMEM((8, TILE, REF), BF16),
            pltpu.VMEM((2, 8, TILE, REF), BF16),
            pltpu.VMEM((2, TILE, REF), BF16),
            pltpu.VMEM((2, 2, TILE, REF), BF16),
            pltpu.VMEM((1, TILE, REF), BF16),
            pltpu.VMEM((7, TILE, TILE), F32),
            pltpu.VMEM((6, TILE, TILE), F32),
            pltpu.VMEM((64, TILE), F32),
            pltpu.VMEM((TILE, ROWS), BF16),
            pltpu.VMEM((TILE, ROWS), BF16),
            DMA((4,)),
            DMA((32,)),
            DMA((32,)),
        ],
        compiler_params=pltpu.CompilerParams(
            collective_id=1, has_side_effects=True, vmem_limit_bytes=32 * MIB
        ),
        name="scatter_gradients",
    )(refresh, weight, own, gw, picked)
    return hidden, grad_features, grad_weight


def solution(mesh):
    placed = (
        P("dom", "feat"),
        P("feat", None),
        P(None, "feat"),
        P("dom", None, None),
        P("dom"),
        P("dom"),
        P("dom"),
        P(),
        P("dom"),
        P("dom", "feat"),
    )
    return jax.shard_map(
        shards,
        mesh=mesh,
        in_specs=placed,
        out_specs=(P("dom", "feat"), P("dom", "feat"), P("feat", None)),
        check_vma=False,
    )
```

```python
import jax
import jax.numpy as jnp
from jax import lax
from jax.experimental import pallas as pl
from jax.experimental.pallas import tpu as pltpu
from jax.sharding import PartitionSpec as P

MESH = pl.DeviceIdType.MESH
BF16 = jnp.bfloat16
F32 = jnp.float32
I32 = jnp.int32

ROWS = 1024
REF = 256
TILE = 128
NT = 768
PARTS = 64
BLOCKS = PARTS * ROWS // TILE
PER = ROWS // TILE
RING = 4
CLASS = PARTS // 2
MIB = 1024 * 1024


def dot(lhs, rhs):
    return jnp.dot(lhs, rhs, preferred_element_type=F32)


class Place:
    def __init__(self):
        self.dom = lax.axis_index("dom")
        self.feat = lax.axis_index("feat")
        self.core = self.dom % 2
        self.z = (self.dom // 2) % 2
        self.y = (self.dom // 4) % RING
        self.x = self.dom // 16
        self.a = self.x * (1 - self.core) + self.y * self.core
        self.b = self.y * (1 - self.core) + self.x * self.core
        self.sibling = self.dom + 1 - 2 * self.core
        self.z_pair = self.dom + 2 - 4 * self.z
        self.a_next = self.at(self.a + 1, self.b)
        self.a_prev = self.at(self.a + 3, self.b)
        self.b_next = self.at(self.a, self.b + 1)
        self.b_prev = self.at(self.a, self.b + 3)

    def at(self, a, b):
        a, b = a % RING, b % RING
        x = a * (1 - self.core) + b * self.core
        y = b * (1 - self.core) + a * self.core
        return ((x * RING + y) * 2 + self.z) * 2 + self.core

    def xy(self, x, y):
        return (((x % RING) * RING + y % RING) * 2 + self.z) * 2 + self.core

    def slot(self, a, b, z):
        return self.core * CLASS + (b % RING) * 8 + (a % RING) * 2 + z

    def greet(self):
        barrier = pltpu.get_barrier_semaphore()
        near = (self.sibling, self.z_pair, self.a_next, self.a_prev, self.b_next, self.b_prev)
        for device in near:
            pl.semaphore_signal(barrier, inc=1, device_id=(device, self.feat), device_id_type=MESH)
        pl.semaphore_signal(
            barrier, inc=1, device_id=(self.dom, 1 - self.feat), device_id_type=MESH
        )
        return lambda: pl.semaphore_wait(barrier, len(near) + 1)


def slot_part(slot):
    core, b, a, z = slot // CLASS, (slot // 8) % RING, (slot // 2) % RING, slot % 2
    x = a * (1 - core) + b * core
    y = b * (1 - core) + a * core
    return ((x * RING + y) * 2 + z) * 2 + core


def part_slot(part):
    core, z, y, x = part % 2, (part // 2) % 2, (part // 4) % RING, part // 16
    a = x * (1 - core) + y * core
    b = y * (1 - core) + x * core
    return core * CLASS + b * 8 + a * 2 + z


def rows_by_refresh(row):
    column = jnp.transpose(jnp.broadcast_to(row, (TILE, REF)))
    lanes = lax.broadcasted_iota(I32, (REF, TILE), 1)
    parts = [(column == lanes + k * TILE).astype(F32).astype(BF16) for k in range(PER)]
    return jnp.concatenate(parts, axis=1)


def refresh_by_rows(row):
    rows = lax.broadcasted_iota(I32, (ROWS, REF), 0)
    return (rows == row).astype(F32).astype(BF16)


def fetch(sems, *pairs):
    copies = [pltpu.make_async_copy(src, dst, sems.at[k]) for k, (src, dst) in enumerate(pairs)]
    for copy in copies:
        copy.start()
    return copies


def half_rows(index):
    return pl.ds(pl.multiple_of(index * 64, 64), 64)


def column_block(index):
    return pl.ds(pl.multiple_of(index * TILE, TILE), TILE)


def gather_kernel(
    feat_hbm,
    w_hbm,
    refresh_hbm,
    arr_out,
    fx_out,
    wcol_out,
    arr,
    pick,
    fx,
    weight,
    wcol,
    refresh,
    send_sem,
    recv_sem,
    pair_send,
    pair_recv,
    load_sem,
    out_sem,
):
    me = Place()
    f = me.feat
    own_rows, pair_rows = half_rows(f), half_rows(1 - f)
    own_columns, pair_columns = column_block(f), column_block(1 - f)
    loads = fetch(
        load_sem, (feat_hbm, fx.at[own_rows, :]), (w_hbm, weight), (refresh_hbm, refresh)
    )
    ready = me.greet()
    loads[2].wait()
    chosen = refresh_by_rows(refresh[pl.ds(me.dom, 1), :])
    loads[0].wait()
    pick[own_rows, :] = dot(fx[own_rows, :], chosen).astype(BF16)
    loads[1].wait()
    wcol[own_rows, :] = weight[:, own_columns]
    ready()

    def to_pair(k, src, dst):
        return pltpu.make_async_remote_copy(
            src_ref=src,
            dst_ref=dst,
            send_sem=pair_send.at[k],
            recv_sem=pair_recv.at[k],
            device_id=(me.dom, 1 - f),
            device_id_type=MESH,
        )

    pick_copy = to_pair(0, pick.at[own_rows, :], pick.at[own_rows, :])
    pick_copy.start()
    w_copy = to_pair(1, weight.at[:, pair_columns], wcol.at[own_rows, :])
    w_copy.start()
    fx_copy = to_pair(2, fx.at[own_rows, :], fx.at[own_rows, :])
    fx_copy.start()

    sends = []

    def send(slot, target):
        copy = pltpu.make_async_remote_copy(
            src_ref=arr.at[slot],
            dst_ref=arr.at[slot],
            send_sem=send_sem.at[len(sends)],
            recv_sem=recv_sem.at[slot],
            device_id=(target, f),
            device_id_type=MESH,
        )
        copy.start()
        sends.append(copy)

    def arrive(slot):
        pltpu.make_async_remote_copy(
            src_ref=arr.at[slot],
            dst_ref=arr.at[slot],
            send_sem=send_sem.at[0],
            recv_sem=recv_sem.at[slot],
            device_id=(me.sibling, f),
            device_id_type=MESH,
        ).wait_recv()

    a, b, z, o = me.a, me.b, me.z, 1 - me.z
    mine = me.slot(a, b, z)
    pick_copy.wait_recv()
    arr[pl.ds(mine, 1)] = jnp.transpose(pick[...].astype(F32)).astype(BF16)[None]

    def spread_b(slot):
        send(slot, me.b_next)
        send(slot, me.b_prev)
        send(slot, me.sibling)

    send(mine, me.z_pair)
    send(mine, me.a_next)
    send(mine, me.a_prev)
    spread_b(mine)

    slot = me.slot(a, b, o)
    arrive(slot)
    send(slot, me.a_next)
    send(slot, me.a_prev)
    spread_b(slot)

    slot = me.slot(a + 3, b, z)
    arrive(slot)
    send(slot, me.a_next)
    spread_b(slot)
    slot = me.slot(a + 1, b, z)
    arrive(slot)
    spread_b(slot)

    def ring_b(aa, zz):
        slot = me.slot(aa, b + 3, zz)
        arrive(slot)
        if zz is z:
            send(slot, me.b_next)
        send(slot, me.sibling)
        slot = me.slot(aa, b + 1, zz)
        arrive(slot)
        if zz is not z:
            send(slot, me.b_prev)
        send(slot, me.sibling)

    ring_b(a, z)
    slot = me.slot(a + 3, b, o)
    arrive(slot)
    spread_b(slot)
    slot = me.slot(a + 1, b, o)
    arrive(slot)
    send(slot, me.a_prev)
    spread_b(slot)
    ring_b(a, o)
    slot = me.slot(a + 2, b, z)
    arrive(slot)
    spread_b(slot)
    slot = me.slot(a + 2, b, o)
    arrive(slot)
    spread_b(slot)
    ring_b(a + 3, z)
    ring_b(a + 1, z)
    ring_b(a + 3, o)
    ring_b(a + 1, o)
    ring_b(a + 2, z)
    ring_b(a + 2, o)
    for aa, zz in (
        (a, z),
        (a, o),
        (a + 3, z),
        (a + 1, z),
        (a + 3, o),
        (a + 1, o),
        (a + 2, z),
        (a + 2, o),
    ):
        slot = me.slot(aa, b + 2, zz)
        arrive(slot)
        send(slot, me.sibling)

    def keep(k, first):
        part = pl.ds(first, CLASS)
        return pltpu.make_async_copy(arr.at[part], arr_out.at[part], out_sem.at[k])

    keep_own = keep(0, me.core * CLASS)
    keep_own.start()
    w_copy.wait_recv()
    keep_w = pltpu.make_async_copy(wcol, wcol_out, out_sem.at[2])
    keep_w.start()
    fx_copy.wait_recv()
    keep_fx = pltpu.make_async_copy(fx, fx_out, out_sem.at[3])
    keep_fx.start()
    other = (1 - me.core) * CLASS
    for k in range(CLASS):
        arrive(other + k)
    keep_other = keep(1, other)
    keep_other.start()
    for copy in sends:
        copy.wait_send()
    pick_copy.wait_send()
    w_copy.wait_send()
    fx_copy.wait_send()
    keep_own.wait()
    keep_other.wait()
    keep_w.wait()
    keep_fx.wait()


CHUNK = 12
GROUP = 8
AHEAD = 2
F_UNROLL = 64


def forward_kernel(
    src_ref,
    dst_ref,
    count_ref,
    refresh_hbm,
    fx_hbm,
    wcol_hbm,
    mask_hbm,
    gh_hbm,
    arr_hbm,
    stale_hbm,
    tiles_hbm,
    hidden_ref,
    delta_ref,
    source,
    tiles,
    arr,
    fresh,
    acc,
    refresh,
    fx,
    wcol,
    mask,
    gh,
    stale_sem,
    arr_sem,
    tile_sem,
    load_sem,
):
    me = lax.axis_index("dom")
    live = count_ref[0]
    groups = PARTS // GROUP

    def stale_copy(slot):
        rows = pl.ds(pl.multiple_of(slot_part(slot) * ROWS, ROWS), ROWS)
        return pltpu.make_async_copy(stale_hbm.at[rows], source.at[rows], stale_sem.at[slot])

    def arr_copy(group):
        part = pl.ds(group * GROUP, GROUP)
        return pltpu.make_async_copy(arr_hbm.at[part], arr.at[part], arr_sem.at[group])

    def tile_copy(chunk):
        part = pl.ds(chunk * CHUNK, CHUNK)
        return pltpu.make_async_copy(tiles_hbm.at[part], tiles.at[part], tile_sem.at[chunk])

    def start_group(group):
        arr_copy(group).start()
        for k in range(GROUP):
            stale_copy(group * GROUP + k).start()

    loads = fetch(load_sem, (wcol_hbm, wcol), (refresh_hbm, refresh))
    for group in range(AHEAD):
        start_group(group)
    late = fetch(load_sem.at[pl.ds(2, 3)], (fx_hbm, fx), (mask_hbm, mask), (gh_hbm, gh))
    acc[...] = jnp.zeros_like(acc)
    ones = jnp.ones((REF, TILE), BF16)

    def make_fresh(group):
        rows = arr[pl.ds(group * GROUP, GROUP)].reshape(GROUP * REF, TILE)
        fresh[group % 2] = dot(rows, wcol[...]).astype(BF16)

    for copy in loads:
        copy.wait()
    arr_copy(0).wait()
    make_fresh(0)

    def merge(group, carry):
        @pl.when(group + AHEAD < groups)
        def _():
            start_group(group + AHEAD)

        for k in range(GROUP):

            @pl.when((group * GROUP + k) * CHUNK < live)
            def _():
                tile_copy(group * GROUP + k).start()

        @pl.when(group + 1 < groups)
        def _():
            arr_copy(group + 1).wait()

        for k in range(GROUP):
            stale_copy(group * GROUP + k).wait()
        make_fresh(jnp.minimum(group + 1, groups - 1))
        for k in range(GROUP):
            part = slot_part(group * GROUP + k)
            chosen = refresh_by_rows(refresh[pl.ds(part, 1), :])
            new = fresh[group % 2, pl.ds(k * REF, REF), :]
            placed = dot(chosen, jnp.concatenate([new, ones], axis=1))
            rows = pl.ds(pl.multiple_of(part * ROWS, ROWS), ROWS)
            old = source[rows, :].astype(F32)
            source[rows, :] = jnp.where(placed[:, TILE:] > 0, placed[:, :TILE], old).astype(BF16)
        return carry

    lax.fori_loop(0, groups, merge, 0)
    for copy in late:
        copy.wait()
    own = pl.ds(pl.multiple_of(me * ROWS, ROWS), ROWS)
    source[own, :] = lax.dot_general(
        fx[...], wcol[...], (((0,), (0,)), ((), ())), preferred_element_type=F32
    ).astype(BF16)

    def wait_chunk(chunk, carry):
        tile_copy(chunk).wait()
        return carry

    lax.fori_loop(0, (live + CHUNK - 1) // CHUNK, wait_chunk, 0)

    def step(index, carry):
        for k in range(F_UNROLL):
            t = index * F_UNROLL + k
            rows = pl.ds(pl.multiple_of(src_ref[t] * TILE, TILE), TILE)
            product = dot(tiles[t], source[rows, :])
            d = jnp.where(t < live, dst_ref[t], PER)
            acc[pl.ds(d, 1)] = acc[pl.ds(d, 1)] + product[None]
        return carry

    lax.fori_loop(0, (live + F_UNROLL - 1) // F_UNROLL, step, 0)

    for d in range(PER):
        pre = acc[d]
        rows = pl.ds(d * TILE, TILE)
        hidden_ref[rows, :] = jnp.maximum(pre, 0.0).astype(BF16)
        passed = jnp.where(pre > 0, gh[rows, :].astype(F32), 0.0)
        kept = mask[pl.ds(d, 1), :].astype(F32)
        delta_ref[d] = (jnp.transpose(passed) * kept).astype(BF16)


B_CHUNK = 64
B_RING = 4
B_UNROLL = 64


def backward_kernel(
    src_ref,
    dst_ref,
    count_ref,
    refresh_hbm,
    fx_hbm,
    delta_hbm,
    arr_hbm,
    tiles_hbm,
    picked_hbm,
    own_ref,
    gw_ref,
    acc,
    refresh,
    fx,
    delta,
    tiles,
    arr,
    picked,
    gw_total,
    tile_sem,
    arr_sem,
    load_sem,
    out_sem,
):
    me = lax.axis_index("dom")
    live = count_ref[0]
    chunks = (live + B_CHUNK - 1) // B_CHUNK

    def tile_copy(chunk):
        part = pl.ds(chunk * B_CHUNK, B_CHUNK)
        place = chunk % B_RING
        return pltpu.make_async_copy(tiles_hbm.at[part], tiles.at[place], tile_sem.at[place])

    for k in range(B_RING - 1):

        @pl.when(k < chunks)
        def _():
            tile_copy(k).start()

    loads = fetch(load_sem, (delta_hbm, delta), (refresh_hbm, refresh), (fx_hbm, fx))
    arr_copy = pltpu.make_async_copy(arr_hbm, arr, arr_sem)
    arr_copy.start()

    def clear(index, carry):
        acc[pl.ds(index * PER, PER)] = jnp.zeros((PER, TILE, TILE), F32)
        return carry

    lax.fori_loop(0, BLOCKS // PER, clear, 0)
    acc[BLOCKS] = jnp.zeros((TILE, TILE), F32)
    for copy in loads:
        copy.wait()

    def take_chunk(chunk, carry):
        @pl.when(chunk + B_RING - 1 < chunks)
        def _():
            tile_copy(chunk + B_RING - 1).start()

        tile_copy(chunk).wait()
        place = chunk % B_RING

        def step(index, carry):
            for k in range(B_UNROLL):
                local = index * B_UNROLL + k
                t = chunk * B_CHUNK + local
                product = dot(delta[dst_ref[t]], tiles[place, local])
                s = jnp.where(t < live, src_ref[t], BLOCKS)
                acc[pl.ds(s, 1)] = acc[pl.ds(s, 1)] + product[None]
            return carry

        return lax.fori_loop(0, B_CHUNK // B_UNROLL, step, carry)

    lax.fori_loop(0, chunks, take_chunk, 0)
    arr_copy.wait()
    gw_total[...] = jnp.zeros_like(gw_total)

    def out_copy(slot):
        return pltpu.make_async_copy(picked.at[slot], picked_hbm.at[slot], out_sem.at[slot])

    def pick(group, carry):
        total = gw_total[...]
        for k in range(GROUP):
            slot = group * GROUP + k
            part = slot_part(slot)
            chosen = refresh_by_rows(refresh[pl.ds(part, 1), :])
            blocks = [acc[part * PER + i].astype(BF16) for i in range(PER)]
            grads = dot(jnp.concatenate(blocks, axis=1), chosen)
            grads = jnp.where(part == me, 0.0, grads).astype(BF16)
            picked[pl.ds(slot, 1)] = grads[None]
            out_copy(slot).start()
            total = total + dot(grads, arr[pl.ds(slot, 1)][0])
        gw_total[...] = total
        return carry

    lax.fori_loop(0, PARTS // GROUP, pick, 0)
    for k in range(PER):
        own_ref[:, pl.ds(k * TILE, TILE)] = acc[me * PER + k]
    gw = gw_total[...] + lax.dot_general(
        own_ref[...].astype(BF16), fx[...], (((1,), (1,)), ((), ())), preferred_element_type=F32
    )
    gw_ref[...] = jnp.transpose(gw)

    def wait_out(slot, carry):
        out_copy(slot).wait()
        return carry

    lax.fori_loop(0, PARTS, wait_out, 0)


def scatter_kernel(
    refresh_hbm,
    w_hbm,
    own_hbm,
    gw_hbm,
    picked_hbm,
    gf_out,
    gw_out,
    refresh,
    weight,
    own,
    work,
    sib,
    from_b1,
    from_b2,
    from_a1,
    from_a2,
    from_z,
    sums,
    sums_in,
    gw_in,
    grad,
    grad_in,
    load_sem,
    small_sem,
    send_sem,
    recv_sem,
):
    me = Place()
    ready = me.greet()
    small = fetch(
        small_sem, (gw_hbm, sums.at[0]), (own_hbm, own), (w_hbm, weight), (refresh_hbm, refresh)
    )
    f, a, b, z = me.feat, me.a, me.b, me.z
    loads = []
    for k, chunk in enumerate((b + 2, b + 1, b + 3, b)):
        first = (chunk % RING) * 8
        copy = pltpu.make_async_copy(
            picked_hbm.at[pl.ds(me.core * CLASS + first, 8)],
            work.at[pl.ds(first, 8)],
            load_sem.at[k],
        )
        copy.start()
        loads.append(copy)
    small[0].wait()
    ready()
    sends = []

    def send(src, dst, target, feat=None):
        k = len(sends)
        copy = pltpu.make_async_remote_copy(
            src_ref=src,
            dst_ref=dst,
            send_sem=send_sem.at[k],
            recv_sem=recv_sem.at[k],
            device_id=(target, f if feat is None else feat),
            device_id_type=MESH,
        )
        copy.start()
        sends.append(copy)
        return copy

    y_one = me.xy(me.x, me.y + 1 + 2 * (me.y % 2))
    y_two = me.xy(me.x, me.y + 3 - 2 * (me.y % 2))
    x_one = me.xy(me.x + 1 + 2 * (me.x % 2), me.y)
    x_two = me.xy(me.x + 3 - 2 * (me.x % 2), me.y)
    partners = (me.sibling, y_one, y_two, x_one, x_two, me.z_pair)

    def sum_send(k):
        return send(sums.at[k], sums_in.at[k], partners[k])

    def sum_take(k, copy):
        copy.wait_recv()
        sums[k + 1] = sums[k] + sums_in[k]

    def add(ref, first, size, *others):
        part = pl.ds(first, size)
        total = ref[part].astype(F32)
        for other in others:
            total = total + other.astype(F32)
        ref[part] = total.astype(BF16)

    gw_copy = sum_send(0)
    to_sib = []
    for chunk in (a + 2, a + 1, a + 3, a):
        first = (chunk % RING) * 8
        src = picked_hbm.at[pl.ds((1 - me.core) * CLASS + first, 8)]
        to_sib.append(send(src, sib.at[pl.ds(first, 8)], me.sibling))

    def fold(k, chunk):
        first = (chunk % RING) * 8
        loads[k].wait()
        to_sib[k].wait_recv()
        add(work, first, 8, sib[pl.ds(first, 8)])
        return first

    across = fold(0, b + 2)
    b1_up = send(work.at[pl.ds(across, 4)], from_b1.at[pl.ds(0, 4)], me.b_next)
    b1_down = send(work.at[pl.ds(across + 4, 4)], from_b1.at[pl.ds(4, 4)], me.b_prev)
    up = fold(1, b + 1)
    b2_up_late = send(work.at[pl.ds(up + 4, 4)], from_b2.at[0, pl.ds(4, 4)], me.b_next)
    down = fold(2, b + 3)
    b2_down_early = send(work.at[pl.ds(down, 4)], from_b2.at[1, pl.ds(0, 4)], me.b_prev)
    sum_take(0, gw_copy)
    gw_copy = sum_send(1)
    here = fold(3, b)
    b1_up.wait_recv()
    add(work, up, 4, from_b1[pl.ds(0, 4)])
    b2_up_early = send(work.at[pl.ds(up, 4)], from_b2.at[0, pl.ds(0, 4)], me.b_next)
    b1_down.wait_recv()
    add(work, down + 4, 4, from_b1[pl.ds(4, 4)])
    b2_down_late = send(work.at[pl.ds(down + 4, 4)], from_b2.at[1, pl.ds(4, 4)], me.b_prev)
    sum_take(1, gw_copy)
    gw_copy = sum_send(2)
    sum_take(2, gw_copy)
    gw_copy = sum_send(3)
    b2_up_late.wait_recv()
    b2_down_early.wait_recv()
    b2_up_early.wait_recv()
    b2_down_late.wait_recv()
    add(work, here, 8, from_b2[0], from_b2[1])

    across = here + ((a + 2) % RING) * 2
    up = here + ((a + 1) % RING) * 2
    down = here + ((a + 3) % RING) * 2
    mine = here + a * 2
    a1_up = send(work.at[pl.ds(across, 1)], from_a1.at[pl.ds(0, 1)], me.a_next)
    a1_down = send(work.at[pl.ds(across + 1, 1)], from_a1.at[pl.ds(1, 1)], me.a_prev)
    a2_up_late = send(work.at[pl.ds(up + 1, 1)], from_a2.at[0, pl.ds(1, 1)], me.a_next)
    a2_down_early = send(work.at[pl.ds(down, 1)], from_a2.at[1, pl.ds(0, 1)], me.a_prev)
    sum_take(3, gw_copy)
    gw_copy = sum_send(4)
    a1_up.wait_recv()
    add(work, up, 1, from_a1[pl.ds(0, 1)])
    a2_up_early = send(work.at[pl.ds(up, 1)], from_a2.at[0, pl.ds(0, 1)], me.a_next)
    a1_down.wait_recv()
    add(work, down + 1, 1, from_a1[pl.ds(1, 1)])
    a2_down_late = send(work.at[pl.ds(down + 1, 1)], from_a2.at[1, pl.ds(1, 1)], me.a_prev)
    for copy in small[1:]:
        copy.wait()
    chosen = rows_by_refresh(refresh[pl.ds(me.dom, 1), :])
    sum_take(4, gw_copy)
    gw_copy = sum_send(5)
    a2_up_late.wait_recv()
    a2_down_early.wait_recv()
    a2_up_early.wait_recv()
    a2_down_late.wait_recv()
    add(work, mine, 2, from_a2[0], from_a2[1])
    z_copy = send(work.at[pl.ds(mine + 1 - z, 1)], from_z, me.z_pair)
    sum_take(5, gw_copy)
    other_rows = pl.ds(pl.multiple_of((1 - f) * 64, 64), 64)
    own_rows = pl.ds(pl.multiple_of(f * 64, 64), 64)
    swap = send(sums.at[6, other_rows, :], gw_in, me.dom, 1 - f)
    z_copy.wait_recv()
    carried = work[pl.ds(mine + z, 1)][0].astype(F32) + from_z[0].astype(F32)
    grad[...] = (own[...] + dot(carried.astype(BF16), chosen)).astype(BF16)
    grad_copy = send(grad, grad_in, me.dom, 1 - f)
    own_columns = pl.ds(pl.multiple_of(f * TILE, TILE), TILE)
    other_columns = pl.ds(pl.multiple_of((1 - f) * TILE, TILE), TILE)
    half = dot(weight[:, own_columns], grad[...])
    swap.wait_recv()
    gw_out[:, own_columns] = sums[6, own_rows, :]
    gw_out[:, other_columns] = gw_in[...]
    grad_copy.wait_recv()
    half = half + dot(weight[:, other_columns], grad_in[...])
    gf_out[...] = half.astype(BF16)
    for copy in sends:
        copy.wait_send()


VMEM = pl.BlockSpec(memory_space=pltpu.VMEM)
SMEM = pl.BlockSpec(memory_space=pltpu.SMEM)
ANY = pl.BlockSpec(memory_space=pl.ANY)
DMA = pltpu.SemaphoreType.DMA


def shape(dims, kind):
    return jax.ShapeDtypeStruct(dims, kind)


def scratch(dims, kind):
    return pltpu.VMEM(dims, kind)


def params(**fields):
    return pltpu.CompilerParams(vmem_limit_bytes=62 * MIB, **fields)


def call_gather(features, weight, refresh):
    return pl.pallas_call(
        gather_kernel,
        out_shape=(
            shape((PARTS, REF, TILE), BF16),
            shape((TILE, ROWS), BF16),
            shape((TILE, TILE), BF16),
        ),
        in_specs=[ANY] * 3,
        out_specs=(ANY, ANY, ANY),
        scratch_shapes=[
            scratch((PARTS, REF, TILE), BF16),
            scratch((TILE, REF), BF16),
            scratch((TILE, ROWS), BF16),
            scratch((64, 2 * TILE), BF16),
            scratch((TILE, TILE), BF16),
            scratch((PARTS, REF), I32),
            DMA((63,)),
            DMA((PARTS,)),
            DMA((3,)),
            DMA((3,)),
            DMA((3,)),
            DMA((4,)),
        ],
        compiler_params=params(collective_id=0, has_side_effects=True),
        name="gather_refreshed",
    )(features, weight, refresh)


def call_forward(
    src, dst, count, refresh, fx, wcol, mask, gh, arr, stale, tiles, name="forward_tiles"
):
    return pl.pallas_call(
        forward_kernel,
        out_shape=(shape((ROWS, TILE), BF16), shape((PER, TILE, TILE), BF16)),
        in_specs=[SMEM] * 3 + [ANY] * 8,
        out_specs=(VMEM, VMEM),
        scratch_shapes=[
            scratch((PARTS * ROWS, TILE), BF16),
            scratch((NT, TILE, TILE), BF16),
            scratch((PARTS, REF, TILE), BF16),
            scratch((2, GROUP * REF, TILE), BF16),
            scratch((PER + 1, TILE, TILE), F32),
            scratch((PARTS, REF), I32),
            scratch((TILE, ROWS), BF16),
            scratch((TILE, TILE), BF16),
            scratch((PER, TILE), I32),
            scratch((ROWS, TILE), BF16),
            DMA((PARTS,)),
            DMA((PARTS // GROUP,)),
            DMA((NT // CHUNK,)),
            DMA((5,)),
        ],
        compiler_params=params(),
        name=name,
    )(src, dst, count, refresh, fx, wcol, mask, gh, arr, stale, tiles)


def call_backward(src, dst, count, refresh, fx, delta, arr, tiles, name="backward_tiles"):
    return pl.pallas_call(
        backward_kernel,
        out_shape=(
            shape((PARTS, TILE, REF), BF16),
            shape((TILE, ROWS), F32),
            shape((TILE, TILE), F32),
        ),
        in_specs=[SMEM] * 3 + [ANY] * 5,
        out_specs=(ANY, VMEM, VMEM),
        scratch_shapes=[
            scratch((BLOCKS + 1, TILE, TILE), F32),
            scratch((PARTS, REF), I32),
            scratch((TILE, ROWS), BF16),
            scratch((PER, TILE, TILE), BF16),
            scratch((B_RING, B_CHUNK, TILE, TILE), BF16),
            scratch((PARTS, REF, TILE), BF16),
            scratch((PARTS, TILE, REF), BF16),
            scratch((TILE, TILE), F32),
            DMA((B_RING,)),
            DMA,
            DMA((3,)),
            DMA((PARTS,)),
        ],
        compiler_params=params(),
        name=name,
    )(src, dst, count, refresh, fx, delta, arr, tiles)


def call_scatter(refresh, weight, own, gw, picked):
    return pl.pallas_call(
        scatter_kernel,
        out_shape=(shape((64, ROWS), BF16), shape((64, 2 * TILE), F32)),
        in_specs=[ANY] * 5,
        out_specs=(VMEM, VMEM),
        scratch_shapes=[
            scratch((PARTS, REF), I32),
            scratch((64, 2 * TILE), BF16),
            scratch((TILE, ROWS), F32),
            scratch((CLASS, TILE, REF), BF16),
            scratch((CLASS, TILE, REF), BF16),
            scratch((8, TILE, REF), BF16),
            scratch((2, 8, TILE, REF), BF16),
            scratch((2, TILE, REF), BF16),
            scratch((2, 2, TILE, REF), BF16),
            scratch((1, TILE, REF), BF16),
            scratch((7, TILE, TILE), F32),
            scratch((6, TILE, TILE), F32),
            scratch((64, TILE), F32),
            scratch((TILE, ROWS), BF16),
            scratch((TILE, ROWS), BF16),
            DMA((4,)),
            DMA((4,)),
            DMA((32,)),
            DMA((32,)),
        ],
        compiler_params=params(collective_id=1, has_side_effects=True),
        name="scatter_gradients",
    )(refresh, weight, own, gw, picked)


def shards(
    features,
    weight,
    stale_cache,
    adj_tiles,
    tile_src,
    tile_dst,
    tile_count,
    refresh,
    train_mask,
    grad_hidden,
):
    arr, fx, wcol = call_gather(features.T, weight, refresh)
    mask = train_mask.reshape(PER, TILE)
    hidden, delta = call_forward(
        tile_src,
        tile_dst,
        tile_count,
        refresh,
        fx,
        wcol,
        mask,
        grad_hidden,
        arr,
        stale_cache,
        adj_tiles,
    )
    picked, own, gw = call_backward(
        tile_src, tile_dst, tile_count, refresh, fx, delta, arr, adj_tiles
    )
    grad_features, grad_weight = call_scatter(refresh, weight, own, gw, picked)
    return hidden, grad_features.T, grad_weight


def solution(mesh):
    placed = (
        P("dom", "feat"),
        P("feat", None),
        P(None, "feat"),
        P("dom", None, None),
        P("dom"),
        P("dom"),
        P("dom"),
        P(),
        P("dom"),
        P("dom", "feat"),
    )
    return jax.shard_map(
        shards,
        mesh=mesh,
        in_specs=placed,
        out_specs=(P("dom", "feat"), P("dom", "feat"), P("feat", None)),
        check_vma=False,
    )
```

```python
import jax
import jax.numpy as jnp
from jax import lax
from jax.experimental import pallas as pl
from jax.experimental.pallas import tpu as pltpu
from jax.sharding import PartitionSpec as P

MESH = pl.DeviceIdType.MESH
BF16 = jnp.bfloat16
F32 = jnp.float32
I32 = jnp.int32

ROWS = 1024
REF = 256
TILE = 128
NT = 768
PARTS = 64
BLOCKS = PARTS * ROWS // TILE
PER = ROWS // TILE
RING = 4
CLASS = PARTS // 2
MIB = 1024 * 1024


def dot(lhs, rhs):
    return jnp.dot(lhs, rhs, preferred_element_type=F32)


class Place:
    def __init__(self):
        self.dom = lax.axis_index("dom")
        self.feat = lax.axis_index("feat")
        self.core = self.dom % 2
        self.z = (self.dom // 2) % 2
        self.y = (self.dom // 4) % RING
        self.x = self.dom // 16
        self.a = self.x * (1 - self.core) + self.y * self.core
        self.b = self.y * (1 - self.core) + self.x * self.core
        self.sibling = self.dom + 1 - 2 * self.core
        self.z_pair = self.dom + 2 - 4 * self.z
        self.a_next = self.at(self.a + 1, self.b)
        self.a_prev = self.at(self.a + 3, self.b)
        self.b_next = self.at(self.a, self.b + 1)
        self.b_prev = self.at(self.a, self.b + 3)
        self.a_far = self.at(self.a + 2, self.b)

    def at(self, a, b):
        a, b = a % RING, b % RING
        x = a * (1 - self.core) + b * self.core
        y = b * (1 - self.core) + a * self.core
        return ((x * RING + y) * 2 + self.z) * 2 + self.core

    def xy(self, x, y):
        return (((x % RING) * RING + y % RING) * 2 + self.z) * 2 + self.core

    def slot(self, a, b, z):
        return self.core * CLASS + (b % RING) * 8 + (a % RING) * 2 + z

    def greet(self, *more):
        barrier = pltpu.get_barrier_semaphore()
        near = (self.sibling, self.z_pair, self.a_next, self.a_prev, self.b_next, self.b_prev)
        near = near + more
        for device in near:
            pl.semaphore_signal(barrier, inc=1, device_id=(device, self.feat), device_id_type=MESH)
        pl.semaphore_signal(
            barrier, inc=1, device_id=(self.dom, 1 - self.feat), device_id_type=MESH
        )
        return lambda: pl.semaphore_wait(barrier, len(near) + 1)


def slot_part(slot):
    core, b, a, z = slot // CLASS, (slot // 8) % RING, (slot // 2) % RING, slot % 2
    x = a * (1 - core) + b * core
    y = b * (1 - core) + a * core
    return ((x * RING + y) * 2 + z) * 2 + core


def part_slot(part):
    core, z, y, x = part % 2, (part // 2) % 2, (part // 4) % RING, part // 16
    a = x * (1 - core) + y * core
    b = y * (1 - core) + x * core
    return core * CLASS + b * 8 + a * 2 + z


def rows_by_refresh(row):
    column = jnp.transpose(jnp.broadcast_to(row, (TILE, REF)))
    lanes = lax.broadcasted_iota(I32, (REF, TILE), 1)
    parts = [(column == lanes + k * TILE).astype(F32).astype(BF16) for k in range(PER)]
    return jnp.concatenate(parts, axis=1)


def refresh_by_rows(row):
    rows = lax.broadcasted_iota(I32, (ROWS, REF), 0)
    return (rows == row).astype(F32).astype(BF16)


def fetch(sems, *pairs):
    copies = [pltpu.make_async_copy(src, dst, sems.at[k]) for k, (src, dst) in enumerate(pairs)]
    for copy in copies:
        copy.start()
    return copies


def half_rows(index):
    return pl.ds(pl.multiple_of(index * 64, 64), 64)


def column_block(index):
    return pl.ds(pl.multiple_of(index * TILE, TILE), TILE)


def plane(p):
    h = p // 2
    return (1 - h // 2) * 3 * h + (h // 2) * (h - 1), p % 2


def gather_kernel(
    feat_hbm,
    w_hbm,
    refresh_hbm,
    stale_hbm,
    arr_out,
    fx_out,
    source_out,
    arr,
    source,
    pick,
    fx,
    weight,
    wcol,
    refresh,
    send_sem,
    recv_sem,
    pair_send,
    pair_recv,
    load_sem,
    stale_sem,
    out_sem,
    row_sem,
):
    me = Place()
    f = me.feat
    own_rows, pair_rows = half_rows(f), half_rows(1 - f)
    own_columns, pair_columns = column_block(f), column_block(1 - f)
    loads = fetch(
        load_sem, (feat_hbm, fx.at[own_rows, :]), (w_hbm, weight), (refresh_hbm, refresh)
    )
    stale_copy = pltpu.make_async_copy(stale_hbm, source, stale_sem)
    stale_copy.start()
    ready = me.greet(me.a_far)
    loads[2].wait()
    chosen = refresh_by_rows(refresh[pl.ds(me.dom, 1), :])
    loads[0].wait()
    pick[own_rows, :] = dot(fx[own_rows, :], chosen).astype(BF16)
    loads[1].wait()
    wcol[own_rows, :] = weight[:, own_columns]
    ready()

    def to_pair(k, src, dst):
        return pltpu.make_async_remote_copy(
            src_ref=src,
            dst_ref=dst,
            send_sem=pair_send.at[k],
            recv_sem=pair_recv.at[k],
            device_id=(me.dom, 1 - f),
            device_id_type=MESH,
        )

    pick_copy = to_pair(0, pick.at[own_rows, :], pick.at[own_rows, :])
    pick_copy.start()
    w_copy = to_pair(1, weight.at[:, pair_columns], wcol.at[own_rows, :])
    w_copy.start()
    fx_copy = to_pair(2, fx.at[own_rows, :], fx.at[own_rows, :])
    fx_copy.start()

    def shard(slot, target, kind, p):
        return pltpu.make_async_remote_copy(
            src_ref=arr.at[slot],
            dst_ref=arr.at[slot],
            send_sem=send_sem.at[kind, p],
            recv_sem=recv_sem.at[slot],
            device_id=(target, f),
            device_id_type=MESH,
        )

    def arrive(slot):
        shard(slot, me.sibling, 0, 0).wait_recv()

    def slot_of(p, b_offset):
        a_offset, pair = plane(p)
        return me.slot(me.a + a_offset, me.b + b_offset, (me.z + pair) % 2)

    def pass_on(p):
        slot = slot_of(p, 0)
        shard(slot, me.b_next, 0, p).start()
        shard(slot, me.b_prev, 1, p).start()
        shard(slot, me.sibling, 3, p).start()

    def along_a(p):
        slot = slot_of(p, 0)
        shard(slot, me.a_next, 7, p).start()
        shard(slot, me.a_prev, 8, p).start()
        shard(slot, me.a_far, 9, p).start()

    def take_plane(p):
        slot = slot_of(p, 0)
        arrive(slot)
        return slot

    def take_b(p):
        below, above = slot_of(p, 3), slot_of(p, 1)
        arrive(below)

        @pl.when(p % 2 == 0)
        def _():
            shard(below, me.b_next, 2, p).start()

        shard(below, me.sibling, 4, p).start()
        arrive(above)

        @pl.when(p % 2 == 1)
        def _():
            shard(above, me.b_prev, 2, p).start()

        shard(above, me.sibling, 5, p).start()
        return below, above

    def take_far(p):
        slot = slot_of(p, 2)
        arrive(slot)
        shard(slot, me.sibling, 6, p).start()
        return slot

    ones = jnp.ones((REF, TILE), BF16)

    def rows_of(part):
        return pl.ds(pl.multiple_of(part * ROWS, ROWS), ROWS)

    def row_copy(part):
        rows = rows_of(part)
        return pltpu.make_async_copy(source.at[rows], source_out.at[rows], row_sem.at[part])

    def merge(*slots):
        fresh = [dot(arr[pl.ds(slot, 1)][0], wcol[...]).astype(BF16) for slot in slots]
        for slot, new in zip(slots, fresh):
            part = slot_part(slot)
            chosen = refresh_by_rows(refresh[pl.ds(part, 1), :])
            placed = dot(chosen, jnp.concatenate([new, ones], axis=1))
            rows = rows_of(part)
            old = source[rows, :].astype(F32)
            source[rows, :] = jnp.where(placed[:, TILE:] > 0, placed[:, :TILE], old).astype(BF16)
        for slot in slots:
            row_copy(slot_part(slot)).start()

    mine = slot_of(0, 0)
    pick_copy.wait_recv()
    arr[pl.ds(mine, 1)] = jnp.transpose(pick[...].astype(F32)).astype(BF16)[None]
    pair_sent = shard(mine, me.z_pair, 2, PER)
    pair_sent.start()
    along_a(0)
    pass_on(0)
    first = take_plane(1)
    along_a(1)
    pass_on(1)
    below, above = take_b(0)
    w_copy.wait_recv()
    stale_copy.wait()
    merge(first, below, above)

    def relay(i, carry):
        near = take_plane(i + 1)
        pass_on(i + 1)
        below, above = take_b(i)
        far = take_far(i - 1)
        merge(near, below, above, far)
        return carry

    lax.fori_loop(1, PER - 1, relay, 0)
    below, above = take_b(PER - 1)
    far = take_far(PER - 2)
    last = take_far(PER - 1)
    own_class = pl.ds(me.core * CLASS, CLASS)
    keep_own = pltpu.make_async_copy(arr.at[own_class], arr_out.at[own_class], out_sem.at[0])
    keep_own.start()
    merge(below, above, far, last)
    fx_copy.wait_recv()
    keep_fx = pltpu.make_async_copy(fx, fx_out, out_sem.at[2])
    keep_fx.start()
    source[rows_of(me.dom), :] = lax.dot_general(
        fx[...], wcol[...], (((0,), (0,)), ((), ())), preferred_element_type=F32
    ).astype(BF16)
    row_copy(me.dom).start()

    def take_sibling(p, carry):
        a_offset, pair = plane(p)
        a, z = (me.b + a_offset) % RING, (me.z + pair) % 2
        first = (1 - me.core) * CLASS + a * 2 + z
        slots = [first + ((me.a + offset) % RING) * 8 for offset in (0, 3, 1, 2)]
        for slot in slots:
            arrive(slot)
        merge(*slots)
        return carry

    lax.fori_loop(0, PER, take_sibling, 0)
    other_class = pl.ds((1 - me.core) * CLASS, CLASS)
    keep_other = pltpu.make_async_copy(arr.at[other_class], arr_out.at[other_class], out_sem.at[1])
    keep_other.start()

    def settle(p, carry):
        for kind in range(7):
            shard(mine, me.sibling, kind, p).wait_send()
        return carry

    lax.fori_loop(0, PER, settle, 0)
    for p in range(2):
        for kind in range(7, 10):
            shard(mine, me.sibling, kind, p).wait_send()
    pair_sent.wait_send()
    pick_copy.wait_send()
    w_copy.wait_send()
    fx_copy.wait_send()

    def settle_rows(part, carry):
        row_copy(part).wait()
        return carry

    lax.fori_loop(0, PARTS, settle_rows, 0)
    keep_own.wait()
    keep_fx.wait()
    keep_other.wait()


GROUP = 8
CHUNK = 64


def forward_kernel(
    src_ref,
    dst_ref,
    count_ref,
    mask_hbm,
    gh_hbm,
    source_hbm,
    tiles_hbm,
    hidden_ref,
    delta_ref,
    source,
    tiles,
    acc,
    mask,
    gh,
    source_sem,
    tile_sem,
    load_sem,
):
    live = count_ref[0]
    chunks = (live + CHUNK - 1) // CHUNK
    source_copy = pltpu.make_async_copy(source_hbm, source, source_sem)
    source_copy.start()

    def tile_copy(chunk):
        part = pl.ds(chunk * CHUNK, CHUNK)
        return pltpu.make_async_copy(tiles_hbm.at[part], tiles.at[part], tile_sem.at[chunk])

    def start_chunk(chunk, carry):
        tile_copy(chunk).start()
        return carry

    lax.fori_loop(0, chunks, start_chunk, 0)
    late = fetch(load_sem, (mask_hbm, mask), (gh_hbm, gh))
    acc[...] = jnp.zeros_like(acc)
    source_copy.wait()

    def step(chunk, carry):
        tile_copy(chunk).wait()
        for k in range(CHUNK):
            t = chunk * CHUNK + k
            rows = pl.ds(pl.multiple_of(src_ref[t] * TILE, TILE), TILE)
            product = dot(tiles[t], source[rows, :])
            d = jnp.where(t < live, dst_ref[t], PER)
            acc[pl.ds(d, 1)] = acc[pl.ds(d, 1)] + product[None]
        return carry

    lax.fori_loop(0, chunks, step, 0)
    for copy in late:
        copy.wait()
    for d in range(PER):
        pre = acc[d]
        rows = pl.ds(d * TILE, TILE)
        hidden_ref[rows, :] = jnp.maximum(pre, 0.0).astype(BF16)
        passed = jnp.where(pre > 0, gh[rows, :].astype(F32), 0.0)
        kept = mask[pl.ds(d, 1), :].astype(F32)
        delta_ref[d] = (jnp.transpose(passed) * kept).astype(BF16)


B_CHUNK = 64
B_RING = 4
B_UNROLL = 64


def backward_kernel(
    src_ref,
    dst_ref,
    count_ref,
    refresh_hbm,
    fx_hbm,
    delta_hbm,
    arr_hbm,
    tiles_hbm,
    picked_hbm,
    own_ref,
    gw_ref,
    acc,
    refresh,
    fx,
    delta,
    tiles,
    arr,
    picked,
    gw_total,
    tile_sem,
    arr_sem,
    load_sem,
    out_sem,
):
    me = lax.axis_index("dom")
    live = count_ref[0]
    chunks = (live + B_CHUNK - 1) // B_CHUNK

    def tile_copy(chunk):
        part = pl.ds(chunk * B_CHUNK, B_CHUNK)
        place = chunk % B_RING
        return pltpu.make_async_copy(tiles_hbm.at[part], tiles.at[place], tile_sem.at[place])

    for k in range(B_RING - 1):

        @pl.when(k < chunks)
        def _():
            tile_copy(k).start()

    loads = fetch(load_sem, (delta_hbm, delta), (refresh_hbm, refresh), (fx_hbm, fx))
    arr_copy = pltpu.make_async_copy(arr_hbm, arr, arr_sem)
    arr_copy.start()

    def clear(index, carry):
        acc[pl.ds(index * PER, PER)] = jnp.zeros((PER, TILE, TILE), F32)
        return carry

    lax.fori_loop(0, BLOCKS // PER, clear, 0)
    acc[BLOCKS] = jnp.zeros((TILE, TILE), F32)
    for copy in loads:
        copy.wait()

    def take_chunk(chunk, carry):
        @pl.when(chunk + B_RING - 1 < chunks)
        def _():
            tile_copy(chunk + B_RING - 1).start()

        tile_copy(chunk).wait()
        place = chunk % B_RING

        def step(index, carry):
            for k in range(B_UNROLL):
                local = index * B_UNROLL + k
                t = chunk * B_CHUNK + local
                product = dot(delta[dst_ref[t]], tiles[place, local])
                s = jnp.where(t < live, src_ref[t], BLOCKS)
                acc[pl.ds(s, 1)] = acc[pl.ds(s, 1)] + product[None]
            return carry

        return lax.fori_loop(0, B_CHUNK // B_UNROLL, step, carry)

    lax.fori_loop(0, chunks, take_chunk, 0)
    arr_copy.wait()
    gw_total[...] = jnp.zeros_like(gw_total)

    def out_copy(slot):
        return pltpu.make_async_copy(picked.at[slot], picked_hbm.at[slot], out_sem.at[slot])

    def pick(group, carry):
        total = gw_total[...]
        for k in range(GROUP):
            slot = group * GROUP + k
            part = slot_part(slot)
            chosen = refresh_by_rows(refresh[pl.ds(part, 1), :])
            blocks = [acc[part * PER + i].astype(BF16) for i in range(PER)]
            grads = dot(jnp.concatenate(blocks, axis=1), chosen)
            grads = jnp.where(part == me, 0.0, grads).astype(BF16)
            picked[pl.ds(slot, 1)] = grads[None]
            out_copy(slot).start()
            total = total + dot(grads, arr[pl.ds(slot, 1)][0])
        gw_total[...] = total
        return carry

    lax.fori_loop(0, PARTS // GROUP, pick, 0)
    for k in range(PER):
        own_ref[:, pl.ds(k * TILE, TILE)] = acc[me * PER + k]
    gw = gw_total[...] + lax.dot_general(
        own_ref[...].astype(BF16), fx[...], (((1,), (1,)), ((), ())), preferred_element_type=F32
    )
    gw_ref[...] = jnp.transpose(gw)

    def wait_out(slot, carry):
        out_copy(slot).wait()
        return carry

    lax.fori_loop(0, PARTS, wait_out, 0)


def scatter_kernel(
    refresh_hbm,
    w_hbm,
    own_hbm,
    gw_hbm,
    picked_hbm,
    gf_out,
    gw_out,
    refresh,
    weight,
    own,
    work,
    sib,
    from_b1,
    from_b2,
    from_a1,
    from_a2,
    from_z,
    sums,
    sums_in,
    gw_in,
    grad,
    grad_in,
    load_sem,
    small_sem,
    send_sem,
    recv_sem,
):
    me = Place()
    ready = me.greet()
    small = fetch(
        small_sem, (gw_hbm, sums.at[0]), (own_hbm, own), (w_hbm, weight), (refresh_hbm, refresh)
    )
    f, a, b, z = me.feat, me.a, me.b, me.z
    loads = []
    for k, chunk in enumerate((b + 2, b + 1, b + 3, b)):
        first = (chunk % RING) * 8
        copy = pltpu.make_async_copy(
            picked_hbm.at[pl.ds(me.core * CLASS + first, 8)],
            work.at[pl.ds(first, 8)],
            load_sem.at[k],
        )
        copy.start()
        loads.append(copy)
    small[0].wait()
    ready()
    sends = []

    def send(src, dst, target, feat=None):
        k = len(sends)
        copy = pltpu.make_async_remote_copy(
            src_ref=src,
            dst_ref=dst,
            send_sem=send_sem.at[k],
            recv_sem=recv_sem.at[k],
            device_id=(target, f if feat is None else feat),
            device_id_type=MESH,
        )
        copy.start()
        sends.append(copy)
        return copy

    y_one = me.xy(me.x, me.y + 1 + 2 * (me.y % 2))
    y_two = me.xy(me.x, me.y + 3 - 2 * (me.y % 2))
    x_one = me.xy(me.x + 1 + 2 * (me.x % 2), me.y)
    x_two = me.xy(me.x + 3 - 2 * (me.x % 2), me.y)
    partners = (me.sibling, y_one, y_two, x_one, x_two, me.z_pair)

    def sum_send(k):
        return send(sums.at[k], sums_in.at[k], partners[k])

    def sum_take(k, copy):
        copy.wait_recv()
        sums[k + 1] = sums[k] + sums_in[k]

    def add(ref, first, size, *others):
        part = pl.ds(first, size)
        total = ref[part].astype(F32)
        for other in others:
            total = total + other.astype(F32)
        ref[part] = total.astype(BF16)

    gw_copy = sum_send(0)
    to_sib = []
    for chunk in (a + 2, a + 1, a + 3, a):
        first = (chunk % RING) * 8
        src = picked_hbm.at[pl.ds((1 - me.core) * CLASS + first, 8)]
        to_sib.append(send(src, sib.at[pl.ds(first, 8)], me.sibling))

    def fold(k, chunk):
        first = (chunk % RING) * 8
        loads[k].wait()
        to_sib[k].wait_recv()
        add(work, first, 8, sib[pl.ds(first, 8)])
        return first

    across = fold(0, b + 2)
    b1_up = send(work.at[pl.ds(across, 4)], from_b1.at[pl.ds(0, 4)], me.b_next)
    b1_down = send(work.at[pl.ds(across + 4, 4)], from_b1.at[pl.ds(4, 4)], me.b_prev)
    up = fold(1, b + 1)
    b2_up_late = send(work.at[pl.ds(up + 4, 4)], from_b2.at[0, pl.ds(4, 4)], me.b_next)
    down = fold(2, b + 3)
    b2_down_early = send(work.at[pl.ds(down, 4)], from_b2.at[1, pl.ds(0, 4)], me.b_prev)
    sum_take(0, gw_copy)
    gw_copy = sum_send(1)
    here = fold(3, b)
    b1_up.wait_recv()
    add(work, up, 4, from_b1[pl.ds(0, 4)])
    b2_up_early = send(work.at[pl.ds(up, 4)], from_b2.at[0, pl.ds(0, 4)], me.b_next)
    b1_down.wait_recv()
    add(work, down + 4, 4, from_b1[pl.ds(4, 4)])
    b2_down_late = send(work.at[pl.ds(down + 4, 4)], from_b2.at[1, pl.ds(4, 4)], me.b_prev)
    sum_take(1, gw_copy)
    gw_copy = sum_send(2)
    sum_take(2, gw_copy)
    gw_copy = sum_send(3)
    b2_up_late.wait_recv()
    b2_down_early.wait_recv()
    b2_up_early.wait_recv()
    b2_down_late.wait_recv()
    add(work, here, 8, from_b2[0], from_b2[1])

    across = here + ((a + 2) % RING) * 2
    up = here + ((a + 1) % RING) * 2
    down = here + ((a + 3) % RING) * 2
    mine = here + a * 2
    a1_up = send(work.at[pl.ds(across, 1)], from_a1.at[pl.ds(0, 1)], me.a_next)
    a1_down = send(work.at[pl.ds(across + 1, 1)], from_a1.at[pl.ds(1, 1)], me.a_prev)
    a2_up_late = send(work.at[pl.ds(up + 1, 1)], from_a2.at[0, pl.ds(1, 1)], me.a_next)
    a2_down_early = send(work.at[pl.ds(down, 1)], from_a2.at[1, pl.ds(0, 1)], me.a_prev)
    sum_take(3, gw_copy)
    gw_copy = sum_send(4)
    a1_up.wait_recv()
    add(work, up, 1, from_a1[pl.ds(0, 1)])
    a2_up_early = send(work.at[pl.ds(up, 1)], from_a2.at[0, pl.ds(0, 1)], me.a_next)
    a1_down.wait_recv()
    add(work, down + 1, 1, from_a1[pl.ds(1, 1)])
    a2_down_late = send(work.at[pl.ds(down + 1, 1)], from_a2.at[1, pl.ds(1, 1)], me.a_prev)
    for copy in small[1:]:
        copy.wait()
    chosen = rows_by_refresh(refresh[pl.ds(me.dom, 1), :])
    sum_take(4, gw_copy)
    gw_copy = sum_send(5)
    a2_up_late.wait_recv()
    a2_down_early.wait_recv()
    a2_up_early.wait_recv()
    a2_down_late.wait_recv()
    add(work, mine, 2, from_a2[0], from_a2[1])
    z_copy = send(work.at[pl.ds(mine + 1 - z, 1)], from_z, me.z_pair)
    sum_take(5, gw_copy)
    other_rows = pl.ds(pl.multiple_of((1 - f) * 64, 64), 64)
    own_rows = pl.ds(pl.multiple_of(f * 64, 64), 64)
    swap = send(sums.at[6, other_rows, :], gw_in, me.dom, 1 - f)
    z_copy.wait_recv()
    carried = work[pl.ds(mine + z, 1)][0].astype(F32) + from_z[0].astype(F32)
    grad[...] = (own[...] + dot(carried.astype(BF16), chosen)).astype(BF16)
    grad_copy = send(grad, grad_in, me.dom, 1 - f)
    own_columns = pl.ds(pl.multiple_of(f * TILE, TILE), TILE)
    other_columns = pl.ds(pl.multiple_of((1 - f) * TILE, TILE), TILE)
    half = dot(weight[:, own_columns], grad[...])
    swap.wait_recv()
    gw_out[:, own_columns] = sums[6, own_rows, :]
    gw_out[:, other_columns] = gw_in[...]
    grad_copy.wait_recv()
    half = half + dot(weight[:, other_columns], grad_in[...])
    gf_out[...] = half.astype(BF16)
    for copy in sends:
        copy.wait_send()


VMEM = pl.BlockSpec(memory_space=pltpu.VMEM)
SMEM = pl.BlockSpec(memory_space=pltpu.SMEM)
ANY = pl.BlockSpec(memory_space=pl.ANY)
DMA = pltpu.SemaphoreType.DMA


def shape(dims, kind):
    return jax.ShapeDtypeStruct(dims, kind)


def scratch(dims, kind):
    return pltpu.VMEM(dims, kind)


def params(**fields):
    return pltpu.CompilerParams(vmem_limit_bytes=62 * MIB, **fields)


def call_gather(features, weight, refresh, stale):
    return pl.pallas_call(
        gather_kernel,
        out_shape=(
            shape((PARTS, REF, TILE), BF16),
            shape((TILE, ROWS), BF16),
            shape((PARTS * ROWS, TILE), BF16),
        ),
        in_specs=[ANY] * 4,
        out_specs=(ANY, ANY, ANY),
        scratch_shapes=[
            scratch((PARTS, REF, TILE), BF16),
            scratch((PARTS * ROWS, TILE), BF16),
            scratch((TILE, REF), BF16),
            scratch((TILE, ROWS), BF16),
            scratch((64, 2 * TILE), BF16),
            scratch((TILE, TILE), BF16),
            scratch((PARTS, REF), I32),
            DMA((10, PER + 1)),
            DMA((PARTS,)),
            DMA((3,)),
            DMA((3,)),
            DMA((3,)),
            DMA,
            DMA((3,)),
            DMA((PARTS,)),
        ],
        compiler_params=params(collective_id=0, has_side_effects=True),
        name="gather_refreshed",
    )(features, weight, refresh, stale)


def call_forward(src, dst, count, mask, gh, source, tiles, name="forward_tiles"):
    return pl.pallas_call(
        forward_kernel,
        out_shape=(shape((ROWS, TILE), BF16), shape((PER, TILE, TILE), BF16)),
        in_specs=[SMEM] * 3 + [ANY] * 4,
        out_specs=(VMEM, VMEM),
        scratch_shapes=[
            scratch((PARTS * ROWS, TILE), BF16),
            scratch((NT, TILE, TILE), BF16),
            scratch((PER + 1, TILE, TILE), F32),
            scratch((PER, TILE), I32),
            scratch((ROWS, TILE), BF16),
            DMA,
            DMA((NT // CHUNK,)),
            DMA((2,)),
        ],
        compiler_params=params(),
        name=name,
    )(src, dst, count, mask, gh, source, tiles)


def call_backward(src, dst, count, refresh, fx, delta, arr, tiles, name="backward_tiles"):
    return pl.pallas_call(
        backward_kernel,
        out_shape=(
            shape((PARTS, TILE, REF), BF16),
            shape((TILE, ROWS), F32),
            shape((TILE, TILE), F32),
        ),
        in_specs=[SMEM] * 3 + [ANY] * 5,
        out_specs=(ANY, VMEM, VMEM),
        scratch_shapes=[
            scratch((BLOCKS + 1, TILE, TILE), F32),
            scratch((PARTS, REF), I32),
            scratch((TILE, ROWS), BF16),
            scratch((PER, TILE, TILE), BF16),
            scratch((B_RING, B_CHUNK, TILE, TILE), BF16),
            scratch((PARTS, REF, TILE), BF16),
            scratch((PARTS, TILE, REF), BF16),
            scratch((TILE, TILE), F32),
            DMA((B_RING,)),
            DMA,
            DMA((3,)),
            DMA((PARTS,)),
        ],
        compiler_params=params(),
        name=name,
    )(src, dst, count, refresh, fx, delta, arr, tiles)


def call_scatter(refresh, weight, own, gw, picked):
    return pl.pallas_call(
        scatter_kernel,
        out_shape=(shape((64, ROWS), BF16), shape((64, 2 * TILE), F32)),
        in_specs=[ANY] * 5,
        out_specs=(VMEM, VMEM),
        scratch_shapes=[
            scratch((PARTS, REF), I32),
            scratch((64, 2 * TILE), BF16),
            scratch((TILE, ROWS), F32),
            scratch((CLASS, TILE, REF), BF16),
            scratch((CLASS, TILE, REF), BF16),
            scratch((8, TILE, REF), BF16),
            scratch((2, 8, TILE, REF), BF16),
            scratch((2, TILE, REF), BF16),
            scratch((2, 2, TILE, REF), BF16),
            scratch((1, TILE, REF), BF16),
            scratch((7, TILE, TILE), F32),
            scratch((6, TILE, TILE), F32),
            scratch((64, TILE), F32),
            scratch((TILE, ROWS), BF16),
            scratch((TILE, ROWS), BF16),
            DMA((4,)),
            DMA((4,)),
            DMA((32,)),
            DMA((32,)),
        ],
        compiler_params=params(collective_id=1, has_side_effects=True),
        name="scatter_gradients",
    )(refresh, weight, own, gw, picked)


def shards(
    features,
    weight,
    stale_cache,
    adj_tiles,
    tile_src,
    tile_dst,
    tile_count,
    refresh,
    train_mask,
    grad_hidden,
):
    arr, fx, source = call_gather(features.T, weight, refresh, stale_cache)
    mask = train_mask.reshape(PER, TILE)
    hidden, delta = call_forward(
        tile_src, tile_dst, tile_count, mask, grad_hidden, source, adj_tiles
    )
    picked, own, gw = call_backward(
        tile_src, tile_dst, tile_count, refresh, fx, delta, arr, adj_tiles
    )
    grad_features, grad_weight = call_scatter(refresh, weight, own, gw, picked)
    return hidden, grad_features.T, grad_weight


def solution(mesh):
    placed = (
        P("dom", "feat"),
        P("feat", None),
        P(None, "feat"),
        P("dom", None, None),
        P("dom"),
        P("dom"),
        P("dom"),
        P(),
        P("dom"),
        P("dom", "feat"),
    )
    return jax.shard_map(
        shards,
        mesh=mesh,
        in_specs=placed,
        out_specs=(P("dom", "feat"), P("dom", "feat"), P("feat", None)),
        check_vma=False,
    )
```

```python
import jax
import jax.numpy as jnp
from jax import lax
from jax.experimental import pallas as pl
from jax.experimental.pallas import tpu as pltpu
from jax.sharding import PartitionSpec as P

MESH = pl.DeviceIdType.MESH
BF16 = jnp.bfloat16
F32 = jnp.float32
I32 = jnp.int32

ROWS = 1024
REF = 256
TILE = 128
NT = 768
PARTS = 64
BLOCKS = PARTS * ROWS // TILE
PER = ROWS // TILE
RING = 4
CLASS = PARTS // 2
MIB = 1024 * 1024


def dot(lhs, rhs):
    return jnp.dot(lhs, rhs, preferred_element_type=F32)


class Place:
    def __init__(self):
        self.dom = lax.axis_index("dom")
        self.feat = lax.axis_index("feat")
        self.core = self.dom % 2
        self.z = (self.dom // 2) % 2
        self.y = (self.dom // 4) % RING
        self.x = self.dom // 16
        self.a = self.x * (1 - self.core) + self.y * self.core
        self.b = self.y * (1 - self.core) + self.x * self.core
        self.sibling = self.dom + 1 - 2 * self.core
        self.z_pair = self.dom + 2 - 4 * self.z
        self.a_next = self.at(self.a + 1, self.b)
        self.a_prev = self.at(self.a + 3, self.b)
        self.b_next = self.at(self.a, self.b + 1)
        self.b_prev = self.at(self.a, self.b + 3)
        self.a_far = self.at(self.a + 2, self.b)
        self.b_far = self.at(self.a, self.b + 2)

    def at(self, a, b):
        a, b = a % RING, b % RING
        x = a * (1 - self.core) + b * self.core
        y = b * (1 - self.core) + a * self.core
        return ((x * RING + y) * 2 + self.z) * 2 + self.core

    def xy(self, x, y):
        return (((x % RING) * RING + y % RING) * 2 + self.z) * 2 + self.core

    def slot(self, a, b, z):
        return self.core * CLASS + (a % RING) * 8 + (b % RING) * 2 + z

    def greet(self, *more, cross=False):
        barrier = pltpu.get_barrier_semaphore()
        near = (self.sibling, self.z_pair, self.a_next, self.a_prev, self.b_next, self.b_prev)
        near = near + more
        for device in near:
            pl.semaphore_signal(barrier, inc=1, device_id=(device, self.feat), device_id_type=MESH)
        pairs = (self.dom, self.z_pair) if cross else (self.dom,)
        for device in pairs:
            pl.semaphore_signal(
                barrier, inc=1, device_id=(device, 1 - self.feat), device_id_type=MESH
            )
        return lambda: pl.semaphore_wait(barrier, len(near) + len(pairs))


def slot_part(slot):
    core, a, b, z = slot // CLASS, (slot // 8) % RING, (slot // 2) % RING, slot % 2
    x = a * (1 - core) + b * core
    y = b * (1 - core) + a * core
    return ((x * RING + y) * 2 + z) * 2 + core


def rows_by_refresh(row):
    column = jnp.transpose(jnp.broadcast_to(row, (TILE, REF)))
    lanes = lax.broadcasted_iota(I32, (REF, TILE), 1)
    parts = [(column == lanes + k * TILE).astype(F32).astype(BF16) for k in range(PER)]
    return jnp.concatenate(parts, axis=1)


def refresh_by_rows(row):
    rows = lax.broadcasted_iota(I32, (ROWS, REF), 0)
    return (rows == row).astype(F32).astype(BF16)


def fetch(sems, *pairs):
    copies = [pltpu.make_async_copy(src, dst, sems.at[k]) for k, (src, dst) in enumerate(pairs)]
    for copy in copies:
        copy.start()
    return copies


def half_rows(index):
    return pl.ds(pl.multiple_of(index * 64, 64), 64)


def column_block(index):
    return pl.ds(pl.multiple_of(index * TILE, TILE), TILE)


def plane(p):
    h = p // 2
    return (1 - h // 2) * 3 * h + (h // 2) * (h - 1), p % 2


def gather_kernel(
    feat_hbm,
    w_hbm,
    refresh_hbm,
    stale_hbm,
    arr_out,
    fx_out,
    source_out,
    arr,
    source,
    fresh_own,
    pick,
    fx,
    weight,
    wcol,
    refresh,
    send_sem,
    recv_sem,
    pair_send,
    pair_recv,
    give_sem,
    take_sem,
    load_sem,
    stale_sem,
    out_sem,
    row_sem,
):
    me = Place()
    f = me.feat
    own_rows, pair_rows = half_rows(f), half_rows(1 - f)
    own_columns, pair_columns = column_block(f), column_block(1 - f)
    loads = fetch(
        load_sem, (feat_hbm, fx.at[own_rows, :]), (w_hbm, weight), (refresh_hbm, refresh)
    )
    ready = me.greet(me.a_far)
    loads[2].wait()
    chosen = refresh_by_rows(refresh[pl.ds(me.dom, 1), :])
    loads[0].wait()
    pick[own_rows, :] = dot(fx[own_rows, :], chosen).astype(BF16)
    loads[1].wait()
    wcol[own_rows, :] = weight[:, own_columns]
    ready()

    def to_pair(k, src, dst):
        return pltpu.make_async_remote_copy(
            src_ref=src,
            dst_ref=dst,
            send_sem=pair_send.at[k],
            recv_sem=pair_recv.at[k],
            device_id=(me.dom, 1 - f),
            device_id_type=MESH,
        )

    pick_copy = to_pair(0, pick.at[own_rows, :], pick.at[own_rows, :])
    pick_copy.start()
    w_copy = to_pair(1, weight.at[:, pair_columns], wcol.at[own_rows, :])
    w_copy.start()
    fx_copy = to_pair(2, fx.at[own_rows, :], fx.at[own_rows, :])
    fx_copy.start()

    def shard(slot, target, kind, p):
        return pltpu.make_async_remote_copy(
            src_ref=arr.at[slot],
            dst_ref=arr.at[slot],
            send_sem=send_sem.at[kind, p],
            recv_sem=recv_sem.at[slot],
            device_id=(target, f),
            device_id_type=MESH,
        )

    def arrive(slot):
        shard(slot, me.sibling, 0, 0).wait_recv()

    def slot_of(p, b_offset):
        a_offset, pair = plane(p)
        return me.slot(me.a + a_offset, me.b + b_offset, (me.z + pair) % 2)

    def pass_on(p):
        slot = slot_of(p, 0)
        shard(slot, me.b_next, 0, p).start()
        shard(slot, me.b_prev, 1, p).start()

    def along_a(p):
        slot = slot_of(p, 0)
        shard(slot, me.a_next, 3, p).start()
        shard(slot, me.a_prev, 4, p).start()
        shard(slot, me.a_far, 5, p).start()

    def take_plane(p):
        slot = slot_of(p, 0)
        arrive(slot)
        return slot

    def take_b(p):
        below, above = slot_of(p, 3), slot_of(p, 1)
        arrive(below)

        @pl.when(p % 2 == 0)
        def _():
            shard(below, me.b_next, 2, p).start()

        arrive(above)

        @pl.when(p % 2 == 1)
        def _():
            shard(above, me.b_prev, 2, p).start()

        return below, above

    def take_far(p):
        slot = slot_of(p, 2)
        arrive(slot)
        return slot

    ones = jnp.ones((REF, TILE), BF16)

    class_first = me.core * CLASS

    def held(slot):
        return pl.ds(pl.multiple_of((slot - class_first) * ROWS, ROWS), ROWS)

    def rows_of(part):
        return pl.ds(pl.multiple_of(part * ROWS, ROWS), ROWS)

    def load_rows(slot):
        return pltpu.make_async_copy(
            stale_hbm.at[rows_of(slot_part(slot))], source.at[held(slot)], stale_sem.at[slot]
        )

    def keep_rows(slot):
        return pltpu.make_async_copy(
            source.at[held(slot)], source_out.at[rows_of(slot_part(slot))], row_sem.at[slot]
        )

    def give_rows(slot, src):
        return pltpu.make_async_remote_copy(
            src_ref=src,
            dst_ref=source_out.at[rows_of(slot_part(slot))],
            send_sem=give_sem.at[slot],
            recv_sem=take_sem.at[slot],
            device_id=(me.sibling, f),
            device_id_type=MESH,
        )

    def merge(*slots):
        fresh = [dot(arr[pl.ds(slot, 1)][0], wcol[...]).astype(BF16) for slot in slots]
        for slot, new in zip(slots, fresh):
            chosen = refresh_by_rows(refresh[pl.ds(slot_part(slot), 1), :])
            placed = dot(chosen, jnp.concatenate([new, ones], axis=1))
            rows = held(slot)
            old = source[rows, :].astype(F32)
            source[rows, :] = jnp.where(placed[:, TILE:] > 0, placed[:, :TILE], old).astype(BF16)
        for slot in slots:
            give_rows(slot, source.at[held(slot)]).start()

    def keep(*slots):
        for slot in slots:
            keep_rows(slot).start()

    mine = slot_of(0, 0)
    pick_copy.wait_recv()
    arr[pl.ds(mine, 1)] = jnp.transpose(pick[...].astype(F32)).astype(BF16)[None]
    pair_sent = shard(mine, me.z_pair, 2, PER)
    pair_sent.start()
    along_a(0)
    pass_on(0)

    def start_load(k, carry):
        load_rows(class_first + k).start()
        return carry

    def wait_load(k, carry):
        load_rows(class_first + k).wait()
        return carry

    lax.fori_loop(0, CLASS, start_load, 0)
    first = take_plane(1)
    along_a(1)
    pass_on(1)
    below, above = take_b(0)
    w_copy.wait_recv()
    lax.fori_loop(0, CLASS, wait_load, 0)
    merge(first, below, above, mine)
    keep(first, below, above)

    def relay(i, carry):
        near = take_plane(i + 1)
        pass_on(i + 1)
        below, above = take_b(i)
        far = take_far(i - 1)
        merge(near, below, above, far)
        keep(near, below, above, far)
        return carry

    lax.fori_loop(1, PER - 1, relay, 0)
    below, above = take_b(PER - 1)
    far = take_far(PER - 2)
    last = take_far(PER - 1)
    keep_arr = pltpu.make_async_copy(arr.at[pl.ds(class_first, CLASS)], arr_out, out_sem.at[0])
    keep_arr.start()
    merge(below, above, far, last)
    keep(below, above, far, last)
    fx_copy.wait_recv()
    keep_fx = pltpu.make_async_copy(fx, fx_out, out_sem.at[1])
    keep_fx.start()
    fresh_own[...] = lax.dot_general(
        fx[...], wcol[...], (((0,), (0,)), ((), ())), preferred_element_type=F32
    ).astype(BF16)
    keep_own = pltpu.make_async_copy(fresh_own, source_out.at[rows_of(me.dom)], row_sem.at[mine])
    keep_own.start()

    def settle(p, carry):
        for kind in range(3):
            shard(mine, me.sibling, kind, p).wait_send()
        return carry

    lax.fori_loop(0, PER, settle, 0)
    for p in range(2):
        for kind in range(3, 6):
            shard(mine, me.sibling, kind, p).wait_send()
    pair_sent.wait_send()
    pick_copy.wait_send()
    w_copy.wait_send()
    fx_copy.wait_send()

    def settle_rows(k, carry):
        given, taken = class_first + k, CLASS - class_first + k
        give_rows(given, source.at[held(given)]).wait_send()
        give_rows(taken, source_out.at[rows_of(slot_part(taken))]).wait_recv()
        keep_rows(class_first + k).wait()
        return carry

    lax.fori_loop(0, CLASS, settle_rows, 0)
    keep_fx.wait()
    keep_arr.wait()


GROUP = 8
CHUNK = 64


def forward_kernel(
    src_ref,
    dst_ref,
    count_ref,
    mask_hbm,
    gh_hbm,
    source_hbm,
    tiles_hbm,
    hidden_ref,
    delta_ref,
    source,
    tiles,
    acc,
    mask,
    gh,
    source_sem,
    tile_sem,
    load_sem,
):
    live = count_ref[0]
    chunks = (live + CHUNK - 1) // CHUNK
    source_copy = pltpu.make_async_copy(source_hbm, source, source_sem)
    source_copy.start()

    def tile_copy(chunk):
        part = pl.ds(chunk * CHUNK, CHUNK)
        return pltpu.make_async_copy(tiles_hbm.at[part], tiles.at[part], tile_sem.at[chunk])

    def start_chunk(chunk, carry):
        tile_copy(chunk).start()
        return carry

    lax.fori_loop(0, chunks, start_chunk, 0)
    late = fetch(load_sem, (mask_hbm, mask), (gh_hbm, gh))
    acc[...] = jnp.zeros_like(acc)
    source_copy.wait()

    def step(chunk, carry):
        tile_copy(chunk).wait()
        for k in range(CHUNK):
            t = chunk * CHUNK + k
            rows = pl.ds(pl.multiple_of(src_ref[t] * TILE, TILE), TILE)
            product = dot(tiles[t], source[rows, :])
            d = jnp.where(t < live, dst_ref[t], PER)
            acc[pl.ds(d, 1)] = acc[pl.ds(d, 1)] + product[None]
        return carry

    lax.fori_loop(0, chunks, step, 0)
    for copy in late:
        copy.wait()
    for d in range(PER):
        pre = acc[d]
        rows = pl.ds(d * TILE, TILE)
        hidden_ref[rows, :] = jnp.maximum(pre, 0.0).astype(BF16)
        passed = jnp.where(pre > 0, gh[rows, :].astype(F32), 0.0)
        kept = mask[pl.ds(d, 1), :].astype(F32)
        delta_ref[d] = (jnp.transpose(passed) * kept).astype(BF16)


B_CHUNK = 64
B_RING = 4
B_UNROLL = 64


def backward_kernel(
    src_ref,
    dst_ref,
    count_ref,
    refresh_hbm,
    fx_hbm,
    delta_hbm,
    tiles_hbm,
    picked_hbm,
    own_ref,
    gw_ref,
    acc,
    refresh,
    fx,
    delta,
    tiles,
    picked,
    tile_sem,
    load_sem,
    out_sem,
):
    me = lax.axis_index("dom")
    live = count_ref[0]
    chunks = (live + B_CHUNK - 1) // B_CHUNK

    def tile_copy(chunk):
        part = pl.ds(chunk * B_CHUNK, B_CHUNK)
        place = chunk % B_RING
        return pltpu.make_async_copy(tiles_hbm.at[part], tiles.at[place], tile_sem.at[place])

    for k in range(B_RING - 1):

        @pl.when(k < chunks)
        def _():
            tile_copy(k).start()

    loads = fetch(load_sem, (delta_hbm, delta), (refresh_hbm, refresh), (fx_hbm, fx))

    def clear(index, carry):
        acc[pl.ds(index * PER, PER)] = jnp.zeros((PER, TILE, TILE), F32)
        return carry

    lax.fori_loop(0, BLOCKS // PER, clear, 0)
    acc[BLOCKS] = jnp.zeros((TILE, TILE), F32)
    for copy in loads:
        copy.wait()

    def take_chunk(chunk, carry):
        @pl.when(chunk + B_RING - 1 < chunks)
        def _():
            tile_copy(chunk + B_RING - 1).start()

        tile_copy(chunk).wait()
        place = chunk % B_RING

        def step(index, carry):
            for k in range(B_UNROLL):
                local = index * B_UNROLL + k
                t = chunk * B_CHUNK + local
                product = dot(delta[dst_ref[t]], tiles[place, local])
                s = jnp.where(t < live, src_ref[t], BLOCKS)
                acc[pl.ds(s, 1)] = acc[pl.ds(s, 1)] + product[None]
            return carry

        return lax.fori_loop(0, B_CHUNK // B_UNROLL, step, carry)

    lax.fori_loop(0, chunks, take_chunk, 0)

    def out_copy(slot):
        return pltpu.make_async_copy(picked.at[slot], picked_hbm.at[slot], out_sem.at[slot])

    def pick(group, carry):
        for k in range(GROUP):
            slot = group * GROUP + k
            part = slot_part(slot)
            chosen = refresh_by_rows(refresh[pl.ds(part, 1), :])
            blocks = [acc[part * PER + i].astype(BF16) for i in range(PER)]
            grads = dot(jnp.concatenate(blocks, axis=1), chosen)
            grads = jnp.where(part == me, 0.0, grads).astype(BF16)
            picked[pl.ds(slot, 1)] = grads[None]
            out_copy(slot).start()
        return carry

    lax.fori_loop(0, PARTS // GROUP, pick, 0)
    for k in range(PER):
        own_ref[:, pl.ds(k * TILE, TILE)] = acc[me * PER + k].astype(BF16)
    gw_ref[...] = lax.dot_general(
        own_ref[...], fx[...], (((1,), (1,)), ((), ())), preferred_element_type=F32
    )

    def wait_out(slot, carry):
        out_copy(slot).wait()
        return carry

    lax.fori_loop(0, PARTS, wait_out, 0)


def scatter_kernel(
    refresh_hbm,
    w_hbm,
    own_hbm,
    gw_hbm,
    arr_hbm,
    picked_hbm,
    gf_out,
    gw_out,
    refresh,
    weight,
    own,
    own_in,
    base,
    gw,
    arr,
    work,
    sib,
    from_b1,
    from_b2,
    from_a,
    from_z,
    sum_core,
    sum_y,
    sum_x,
    sum_last,
    load_sem,
    small_sem,
    send_sem,
    recv_sem,
):
    me = Place()
    ready = me.greet(me.a_far, me.b_far, cross=True)
    f, a, b, z = me.feat, me.a, me.b, me.z
    order = (2, 1, 3, 0)

    def first_of(center, h):
        return ((center + order[h]) % RING) * 8

    loads = []
    for h in range(RING):
        first = first_of(a, h)
        copy = pltpu.make_async_copy(
            picked_hbm.at[pl.ds(me.core * CLASS + first, 8)],
            work.at[pl.ds(first, 8)],
            load_sem.at[h],
        )
        copy.start()
        loads.append(copy)
    small = fetch(
        small_sem,
        (arr_hbm, arr),
        (gw_hbm, gw),
        (own_hbm, own),
        (w_hbm, weight),
        (refresh_hbm, refresh),
    )
    ready()
    sends = []

    def send(src, dst, target, feat=None):
        k = len(sends)
        copy = pltpu.make_async_remote_copy(
            src_ref=src,
            dst_ref=dst,
            send_sem=send_sem.at[k],
            recv_sem=recv_sem.at[k],
            device_id=(target, f if feat is None else feat),
            device_id_type=MESH,
        )
        copy.start()
        sends.append(copy)
        return copy

    def add(first, size, *others):
        part = pl.ds(first, size)
        total = work[part].astype(F32)
        for other in others:
            total = total + other.astype(F32)
        work[part] = total.astype(BF16)

    to_sib = []
    for h in range(RING):
        first = first_of(b, h)
        src = picked_hbm.at[pl.ds((1 - me.core) * CLASS + first, 8)]
        to_sib.append(send(src, sib.at[pl.ds(first, 8)], me.sibling))
    own_copy = send(own_hbm, own_in, me.dom, 1 - f)

    def column(h, offset):
        return first_of(a, h) + ((b + offset) % RING) * 2

    b1, b2 = [], []

    def fold(h):
        first = first_of(a, h)
        loads[h].wait()
        to_sib[h].wait_recv()
        add(first, 8, sib[pl.ds(first, 8)])
        far, up, down = column(h, 2), column(h, 1), column(h, 3)
        b1.append(
            (
                send(work.at[pl.ds(far, 1)], from_b1.at[h, pl.ds(0, 1)], me.b_next),
                send(work.at[pl.ds(far + 1, 1)], from_b1.at[h, pl.ds(1, 1)], me.b_prev),
            )
        )
        b2.append(
            [
                send(work.at[pl.ds(up + 1, 1)], from_b2.at[h, 0, pl.ds(1, 1)], me.b_next),
                send(work.at[pl.ds(down, 1)], from_b2.at[h, 1, pl.ds(0, 1)], me.b_prev),
            ]
        )

    def weigh(h):
        first = first_of(a, h)
        total = gw[...]
        for k in range(8):
            total = total + dot(work[pl.ds(first + k, 1)][0], arr[pl.ds(first + k, 1)][0])
        gw[...] = total

    def relay(h):
        up, down = column(h, 1), column(h, 3)
        b1[h][0].wait_recv()
        add(up, 1, from_b1[h, pl.ds(0, 1)])
        b2[h].append(send(work.at[pl.ds(up, 1)], from_b2.at[h, 0, pl.ds(0, 1)], me.b_next))
        b1[h][1].wait_recv()
        add(down + 1, 1, from_b1[h, pl.ds(1, 1)])
        b2[h].append(send(work.at[pl.ds(down + 1, 1)], from_b2.at[h, 1, pl.ds(1, 1)], me.b_prev))

    along_a = []
    a_targets = (me.a_far, me.a_next, me.a_prev)

    def finish(h):
        here = column(h, 0)
        for copy in b2[h]:
            copy.wait_recv()
        if h < 3:
            add(here, 2, from_b2[h, 0], from_b2[h, 1])
            along_a.append(send(work.at[pl.ds(here, 2)], from_a.at[h], a_targets[h]))
        else:
            for copy in along_a:
                copy.wait_recv()
            add(here, 2, from_b2[h, 0], from_b2[h, 1], from_a[0], from_a[1], from_a[2])

    def ring_sum(buffer, index, targets):
        return [send(buffer.at[index], buffer.at[index], target) for target in targets]

    def take_sum(buffer, copies):
        for copy in copies:
            copy.wait_recv()
        return (buffer[0] + buffer[1]) + (buffer[2] + buffer[3])

    fold(0)
    small[0].wait()
    small[1].wait()
    fold(1)
    weigh(0)
    relay(0)
    fold(2)
    weigh(1)
    relay(1)
    fold(3)
    weigh(2)
    finish(0)
    weigh(3)
    sum_core[0] = jnp.transpose(gw[...])
    core_copy = send(sum_core.at[0], sum_core.at[1], me.sibling)
    relay(2)
    finish(1)
    relay(3)
    core_copy.wait_recv()
    sum_y[pl.ds(me.y, 1)] = (sum_core[0] + sum_core[1])[None]
    y_targets = [me.xy(me.x, me.y + k) for k in (1, 3, 2)]
    y_copies = ring_sum(sum_y, me.y, y_targets)
    finish(2)
    for copy in small[2:]:
        copy.wait()
    chosen = rows_by_refresh(refresh[pl.ds(me.dom, 1), :])
    own_columns, other_columns = column_block(f), column_block(1 - f)
    own_copy.wait_recv()
    base[...] = dot(weight[:, own_columns], own[...]) + dot(weight[:, other_columns], own_in[...])
    sum_x[pl.ds(me.x, 1)] = take_sum(sum_y, y_copies)[None]
    x_targets = [me.xy(me.x + k, me.y) for k in (1, 3, 2)]
    x_copies = ring_sum(sum_x, me.x, x_targets)
    finish(3)
    here = column(3, 0)
    mine, theirs = work.at[pl.ds(here + z, 1)], work.at[pl.ds(here + 1 - z, 1)]
    z_copies = (
        send(theirs, from_z.at[pl.ds(0, 1)], me.z_pair),
        send(mine, from_z.at[pl.ds(1, 1)], me.dom, 1 - f),
        send(theirs, from_z.at[pl.ds(2, 1)], me.z_pair, 1 - f),
    )
    sum_last[0] = take_sum(sum_x, x_copies)
    own_rows, other_rows = half_rows(f), half_rows(1 - f)
    last_copies = (
        send(sum_last.at[0, own_rows, :], sum_last.at[1, pl.ds(0, 64), :], me.z_pair),
        send(sum_last.at[0, other_rows, :], sum_last.at[1, pl.ds(64, 64), :], me.dom, 1 - f),
        send(sum_last.at[0, other_rows, :], sum_last.at[2, pl.ds(0, 64), :], me.z_pair, 1 - f),
    )
    for copy in z_copies:
        copy.wait_recv()
    carried = work[pl.ds(here + z, 1)][0].astype(F32) + from_z[0].astype(F32)
    carried_in = from_z[1].astype(F32) + from_z[2].astype(F32)
    short = dot(weight[:, own_columns], carried.astype(BF16)) + dot(
        weight[:, other_columns], carried_in.astype(BF16)
    )
    gf_out[...] = (base[...] + dot(short.astype(BF16), chosen)).astype(BF16)
    for copy in last_copies:
        copy.wait_recv()
    gw_out[:, own_columns] = sum_last[0, own_rows, :] + sum_last[1, pl.ds(0, 64), :]
    gw_out[:, other_columns] = sum_last[1, pl.ds(64, 64), :] + sum_last[2, pl.ds(0, 64), :]
    for copy in sends:
        copy.wait_send()


VMEM = pl.BlockSpec(memory_space=pltpu.VMEM)
SMEM = pl.BlockSpec(memory_space=pltpu.SMEM)
ANY = pl.BlockSpec(memory_space=pl.ANY)
DMA = pltpu.SemaphoreType.DMA


def shape(dims, kind):
    return jax.ShapeDtypeStruct(dims, kind)


def scratch(dims, kind):
    return pltpu.VMEM(dims, kind)


def params(**fields):
    return pltpu.CompilerParams(vmem_limit_bytes=62 * MIB, **fields)


def call_gather(features, weight, refresh, stale):
    return pl.pallas_call(
        gather_kernel,
        out_shape=(
            shape((CLASS, REF, TILE), BF16),
            shape((TILE, ROWS), BF16),
            shape((PARTS * ROWS, TILE), BF16),
        ),
        in_specs=[ANY] * 4,
        out_specs=(ANY, ANY, ANY),
        scratch_shapes=[
            scratch((PARTS, REF, TILE), BF16),
            scratch((CLASS * ROWS, TILE), BF16),
            scratch((ROWS, TILE), BF16),
            scratch((TILE, REF), BF16),
            scratch((TILE, ROWS), BF16),
            scratch((64, 2 * TILE), BF16),
            scratch((TILE, TILE), BF16),
            scratch((PARTS, REF), I32),
            DMA((6, PER + 1)),
            DMA((PARTS,)),
            DMA((3,)),
            DMA((3,)),
            DMA((PARTS,)),
            DMA((PARTS,)),
            DMA((3,)),
            DMA((PARTS,)),
            DMA((2,)),
            DMA((PARTS,)),
        ],
        compiler_params=params(collective_id=0, has_side_effects=True),
        name="gather_refreshed",
    )(features, weight, refresh, stale)


def call_forward(src, dst, count, mask, gh, source, tiles, name="forward_tiles"):
    return pl.pallas_call(
        forward_kernel,
        out_shape=(shape((ROWS, TILE), BF16), shape((PER, TILE, TILE), BF16)),
        in_specs=[SMEM] * 3 + [ANY] * 4,
        out_specs=(VMEM, VMEM),
        scratch_shapes=[
            scratch((PARTS * ROWS, TILE), BF16),
            scratch((NT, TILE, TILE), BF16),
            scratch((PER + 1, TILE, TILE), F32),
            scratch((PER, TILE), I32),
            scratch((ROWS, TILE), BF16),
            DMA,
            DMA((NT // CHUNK,)),
            DMA((2,)),
        ],
        compiler_params=params(),
        name=name,
    )(src, dst, count, mask, gh, source, tiles)


def call_backward(src, dst, count, refresh, fx, delta, tiles, name="backward_tiles"):
    return pl.pallas_call(
        backward_kernel,
        out_shape=(
            shape((PARTS, TILE, REF), BF16),
            shape((TILE, ROWS), BF16),
            shape((TILE, TILE), F32),
        ),
        in_specs=[SMEM] * 3 + [ANY] * 4,
        out_specs=(ANY, VMEM, VMEM),
        scratch_shapes=[
            scratch((BLOCKS + 1, TILE, TILE), F32),
            scratch((PARTS, REF), I32),
            scratch((TILE, ROWS), BF16),
            scratch((PER, TILE, TILE), BF16),
            scratch((B_RING, B_CHUNK, TILE, TILE), BF16),
            scratch((PARTS, TILE, REF), BF16),
            DMA((B_RING,)),
            DMA((3,)),
            DMA((PARTS,)),
        ],
        compiler_params=params(),
        name=name,
    )(src, dst, count, refresh, fx, delta, tiles)


def call_scatter(refresh, weight, own, gw, arr, picked):
    return pl.pallas_call(
        scatter_kernel,
        out_shape=(shape((64, ROWS), BF16), shape((64, 2 * TILE), F32)),
        in_specs=[ANY] * 6,
        out_specs=(VMEM, VMEM),
        scratch_shapes=[
            scratch((PARTS, REF), I32),
            scratch((64, 2 * TILE), BF16),
            scratch((TILE, ROWS), BF16),
            scratch((TILE, ROWS), BF16),
            scratch((64, ROWS), F32),
            scratch((TILE, TILE), F32),
            scratch((CLASS, REF, TILE), BF16),
            scratch((CLASS, TILE, REF), BF16),
            scratch((CLASS, TILE, REF), BF16),
            scratch((RING, 2, TILE, REF), BF16),
            scratch((RING, 2, 2, TILE, REF), BF16),
            scratch((3, 2, TILE, REF), BF16),
            scratch((3, TILE, REF), BF16),
            scratch((2, TILE, TILE), F32),
            scratch((RING, TILE, TILE), F32),
            scratch((RING, TILE, TILE), F32),
            scratch((3, TILE, TILE), F32),
            DMA((RING,)),
            DMA((5,)),
            DMA((48,)),
            DMA((48,)),
        ],
        compiler_params=params(collective_id=1, has_side_effects=True),
        name="scatter_gradients",
    )(refresh, weight, own, gw, arr, picked)


def shards(
    features,
    weight,
    stale_cache,
    adj_tiles,
    tile_src,
    tile_dst,
    tile_count,
    refresh,
    train_mask,
    grad_hidden,
):
    arr, fx, source = call_gather(features.T, weight, refresh, stale_cache)
    mask = train_mask.reshape(PER, TILE)
    hidden, delta = call_forward(
        tile_src, tile_dst, tile_count, mask, grad_hidden, source, adj_tiles
    )
    picked, own, gw = call_backward(
        tile_src, tile_dst, tile_count, refresh, fx, delta, adj_tiles
    )
    grad_features, grad_weight = call_scatter(refresh, weight, own, gw, arr, picked)
    return hidden, grad_features.T, grad_weight


def solution(mesh):
    placed = (
        P("dom", "feat"),
        P("feat", None),
        P(None, "feat"),
        P("dom", None, None),
        P("dom"),
        P("dom"),
        P("dom"),
        P(),
        P("dom"),
        P("dom", "feat"),
    )
    return jax.shard_map(
        shards,
        mesh=mesh,
        in_specs=placed,
        out_specs=(P("dom", "feat"), P("dom", "feat"), P("feat", None)),
        check_vma=False,
    )
```

```python
import jax
import jax.numpy as jnp
from jax import lax
from jax.experimental import pallas as pl
from jax.experimental.pallas import tpu as pltpu
from jax.sharding import PartitionSpec as P

MESH = pl.DeviceIdType.MESH
BF16 = jnp.bfloat16
F32 = jnp.float32
I32 = jnp.int32

ROWS = 1024
REF = 256
TILE = 128
NT = 768
PARTS = 64
BLOCKS = PARTS * ROWS // TILE
PER = ROWS // TILE
RING = 4
CLASS = PARTS // 2
MIB = 1024 * 1024


def dot(lhs, rhs):
    return jnp.dot(lhs, rhs, preferred_element_type=F32)


class Place:
    def __init__(self):
        self.dom = lax.axis_index("dom")
        self.feat = lax.axis_index("feat")
        self.core = self.dom % 2
        self.z = (self.dom // 2) % 2
        self.y = (self.dom // 4) % RING
        self.x = self.dom // 16
        self.a = self.x * (1 - self.core) + self.y * self.core
        self.b = self.y * (1 - self.core) + self.x * self.core
        self.sibling = self.dom + 1 - 2 * self.core
        self.z_pair = self.dom + 2 - 4 * self.z
        self.a_next = self.at(self.a + 1, self.b)
        self.a_prev = self.at(self.a + 3, self.b)
        self.b_next = self.at(self.a, self.b + 1)
        self.b_prev = self.at(self.a, self.b + 3)
        self.a_far = self.at(self.a + 2, self.b)
        self.b_far = self.at(self.a, self.b + 2)

    def at(self, a, b):
        a, b = a % RING, b % RING
        x = a * (1 - self.core) + b * self.core
        y = b * (1 - self.core) + a * self.core
        return ((x * RING + y) * 2 + self.z) * 2 + self.core

    def xy(self, x, y):
        return (((x % RING) * RING + y % RING) * 2 + self.z) * 2 + self.core

    def slot(self, a, b, z):
        return self.core * CLASS + (a % RING) * 8 + (b % RING) * 2 + z

    def greet(self, *more, cross=False):
        barrier = pltpu.get_barrier_semaphore()
        near = (self.sibling, self.z_pair, self.a_next, self.a_prev, self.b_next, self.b_prev)
        near = near + more
        for device in near:
            pl.semaphore_signal(barrier, inc=1, device_id=(device, self.feat), device_id_type=MESH)
        pairs = (self.dom, self.z_pair) if cross else (self.dom,)
        for device in pairs:
            pl.semaphore_signal(
                barrier, inc=1, device_id=(device, 1 - self.feat), device_id_type=MESH
            )
        return lambda: pl.semaphore_wait(barrier, len(near) + len(pairs))


def slot_part(slot):
    core, a, b, z = slot // CLASS, (slot // 8) % RING, (slot // 2) % RING, slot % 2
    x = a * (1 - core) + b * core
    y = b * (1 - core) + a * core
    return ((x * RING + y) * 2 + z) * 2 + core


def rows_by_refresh(row):
    column = jnp.transpose(jnp.broadcast_to(row, (TILE, REF)))
    lanes = lax.broadcasted_iota(I32, (REF, TILE), 1)
    parts = [(column == lanes + k * TILE).astype(F32).astype(BF16) for k in range(PER)]
    return jnp.concatenate(parts, axis=1)


def refresh_by_rows(row):
    rows = lax.broadcasted_iota(I32, (ROWS, REF), 0)
    return (rows == row).astype(F32).astype(BF16)


def fetch(sems, *pairs):
    copies = [pltpu.make_async_copy(src, dst, sems.at[k]) for k, (src, dst) in enumerate(pairs)]
    for copy in copies:
        copy.start()
    return copies


def half_rows(index):
    return pl.ds(pl.multiple_of(index * 64, 64), 64)


def column_block(index):
    return pl.ds(pl.multiple_of(index * TILE, TILE), TILE)


PLANE = ((0, 0), (0, 1), (3, 0), (1, 0), (3, 1), (1, 1), (2, 0), (2, 1))


def gather_kernel(
    feat_hbm,
    w_hbm,
    refresh_hbm,
    stale_hbm,
    arr_out,
    fx_out,
    source_out,
    arr,
    source,
    fresh_own,
    pick,
    fx,
    weight,
    wcol,
    refresh,
    send_sem,
    recv_sem,
    pair_send,
    pair_recv,
    give_sem,
    take_sem,
    load_sem,
    stale_sem,
    out_sem,
    row_sem,
):
    me = Place()
    f = me.feat
    own_rows, pair_rows = half_rows(f), half_rows(1 - f)
    own_columns, pair_columns = column_block(f), column_block(1 - f)
    loads = fetch(
        load_sem, (feat_hbm, fx.at[own_rows, :]), (w_hbm, weight), (refresh_hbm, refresh)
    )
    ready = me.greet(me.a_far)
    loads[2].wait()
    chosen = refresh_by_rows(refresh[pl.ds(me.dom, 1), :])
    loads[0].wait()
    pick[own_rows, :] = dot(fx[own_rows, :], chosen).astype(BF16)
    loads[1].wait()
    wcol[own_rows, :] = weight[:, own_columns]
    ready()

    def to_pair(k, src, dst):
        return pltpu.make_async_remote_copy(
            src_ref=src,
            dst_ref=dst,
            send_sem=pair_send.at[k],
            recv_sem=pair_recv.at[k],
            device_id=(me.dom, 1 - f),
            device_id_type=MESH,
        )

    pick_copy = to_pair(0, pick.at[own_rows, :], pick.at[own_rows, :])
    pick_copy.start()
    w_copy = to_pair(1, weight.at[:, pair_columns], wcol.at[own_rows, :])
    w_copy.start()
    fx_copy = to_pair(2, fx.at[own_rows, :], fx.at[own_rows, :])
    fx_copy.start()

    def shard(slot, target, kind, p):
        return pltpu.make_async_remote_copy(
            src_ref=arr.at[slot],
            dst_ref=arr.at[slot],
            send_sem=send_sem.at[kind, p],
            recv_sem=recv_sem.at[slot],
            device_id=(target, f),
            device_id_type=MESH,
        )

    def arrive(slot):
        shard(slot, me.sibling, 0, 0).wait_recv()

    def slot_of(p, b_offset):
        a_offset, pair = PLANE[p]
        return me.slot(me.a + a_offset, me.b + b_offset, (me.z + pair) % 2)

    def pass_on(p):
        slot = slot_of(p, 0)
        shard(slot, me.b_next, 0, p).start()
        shard(slot, me.b_prev, 1, p).start()

    def along_a(p):
        slot = slot_of(p, 0)
        shard(slot, me.a_next, 3, p).start()
        shard(slot, me.a_prev, 4, p).start()
        shard(slot, me.a_far, 5, p).start()

    def take_plane(p):
        slot = slot_of(p, 0)
        arrive(slot)
        if p == 1:
            along_a(p)
        pass_on(p)
        return slot

    def take_b(p):
        below, above = slot_of(p, 3), slot_of(p, 1)
        arrive(below)
        if PLANE[p][1] == 0:
            shard(below, me.b_next, 2, p).start()
        arrive(above)
        if PLANE[p][1] == 1:
            shard(above, me.b_prev, 2, p).start()
        return below, above

    def take_far(p):
        slot = slot_of(p, 2)
        arrive(slot)
        return slot

    ones = jnp.ones((REF, TILE), BF16)

    class_first = me.core * CLASS

    def held(slot):
        return pl.ds(pl.multiple_of((slot - class_first) * ROWS, ROWS), ROWS)

    def rows_of(part):
        return pl.ds(pl.multiple_of(part * ROWS, ROWS), ROWS)

    def load_rows(slot):
        return pltpu.make_async_copy(
            stale_hbm.at[rows_of(slot_part(slot))], source.at[held(slot)], stale_sem.at[slot]
        )

    def keep_rows(slot):
        return pltpu.make_async_copy(
            source.at[held(slot)], source_out.at[rows_of(slot_part(slot))], row_sem.at[slot]
        )

    def give_rows(slot, src):
        return pltpu.make_async_remote_copy(
            src_ref=src,
            dst_ref=source_out.at[rows_of(slot_part(slot))],
            send_sem=give_sem.at[slot],
            recv_sem=take_sem.at[slot],
            device_id=(me.sibling, f),
            device_id_type=MESH,
        )

    mine = slot_of(0, 0)

    def merge(*slots):
        fresh = [dot(arr[pl.ds(slot, 1)][0], wcol[...]).astype(BF16) for slot in slots]
        for slot, new in zip(slots, fresh):
            chosen = refresh_by_rows(refresh[pl.ds(slot_part(slot), 1), :])
            placed = dot(chosen, jnp.concatenate([new, ones], axis=1))
            rows = held(slot)
            old = source[rows, :].astype(F32)
            source[rows, :] = jnp.where(placed[:, TILE:] > 0, placed[:, :TILE], old).astype(BF16)
        for slot in slots:
            give_rows(slot, source.at[held(slot)]).start()
            if slot is not mine:
                keep_rows(slot).start()

    pick_copy.wait_recv()
    arr[pl.ds(mine, 1)] = jnp.transpose(pick[...].astype(F32)).astype(BF16)[None]
    pair_sent = shard(mine, me.z_pair, 2, PER)
    pair_sent.start()
    along_a(0)
    pass_on(0)

    def start_load(k, carry):
        load_rows(class_first + k).start()
        return carry

    def wait_load(k, carry):
        load_rows(class_first + k).wait()
        return carry

    lax.fori_loop(0, CLASS, start_load, 0)
    left, right = take_plane(2), take_plane(3)
    b0 = take_b(0)
    z_pair = take_plane(1)
    across = take_plane(6)
    w_copy.wait_recv()
    lax.fori_loop(0, CLASS, wait_load, 0)
    merge(left, right, *b0)
    merge(z_pair, across, mine)
    left, right = take_plane(4), take_plane(5)
    b2, b3 = take_b(2), take_b(3)
    merge(left, right, *b2)
    across = take_plane(7)
    b1, b6 = take_b(1), take_b(6)
    merge(*b3, *b1)
    b4, b5 = take_b(4), take_b(5)
    far0 = take_far(0)
    merge(*b6, across, far0)
    b7 = take_b(7)
    merge(*b4, *b5)
    merge(*b7, take_far(2), take_far(3))
    merge(take_far(1), take_far(6), take_far(4), take_far(5))
    merge(take_far(7))
    keep_arr = pltpu.make_async_copy(arr.at[pl.ds(class_first, CLASS)], arr_out, out_sem.at[0])
    keep_arr.start()
    fx_copy.wait_recv()
    keep_fx = pltpu.make_async_copy(fx, fx_out, out_sem.at[1])
    keep_fx.start()
    fresh_own[...] = lax.dot_general(
        fx[...], wcol[...], (((0,), (0,)), ((), ())), preferred_element_type=F32
    ).astype(BF16)
    keep_own = pltpu.make_async_copy(fresh_own, source_out.at[rows_of(me.dom)], row_sem.at[mine])
    keep_own.start()

    def settle(p, carry):
        for kind in range(3):
            shard(mine, me.sibling, kind, p).wait_send()
        return carry

    lax.fori_loop(0, PER, settle, 0)
    for p in range(2):
        for kind in range(3, 6):
            shard(mine, me.sibling, kind, p).wait_send()
    pair_sent.wait_send()
    pick_copy.wait_send()
    w_copy.wait_send()
    fx_copy.wait_send()

    def settle_rows(k, carry):
        given, taken = class_first + k, CLASS - class_first + k
        give_rows(given, source.at[held(given)]).wait_send()
        give_rows(taken, source_out.at[rows_of(slot_part(taken))]).wait_recv()
        keep_rows(class_first + k).wait()
        return carry

    lax.fori_loop(0, CLASS, settle_rows, 0)
    keep_fx.wait()
    keep_arr.wait()


GROUP = 8
CHUNK = 64
TILE_RING = 3
STAGED = 16


def tiles_kernel(
    src_ref,
    dst_ref,
    count_ref,
    refresh_hbm,
    fx_hbm,
    mask_hbm,
    gh_hbm,
    source_hbm,
    tiles_hbm,
    hidden_ref,
    picked_hbm,
    own_ref,
    gw_ref,
    source,
    tiles,
    pre,
    acc,
    delta,
    refresh,
    fx,
    mask,
    gh,
    picked,
    source_sem,
    tile_sem,
    load_sem,
    out_sem,
):
    me = lax.axis_index("dom")
    live = count_ref[0]
    chunks = (live + CHUNK - 1) // CHUNK
    source_copy = pltpu.make_async_copy(source_hbm, source, source_sem)
    source_copy.start()

    def tile_copy(turn):
        chunk = jnp.where(turn < chunks, turn, turn - chunks)
        place = turn % TILE_RING
        part = pl.ds(chunk * CHUNK, CHUNK)
        return pltpu.make_async_copy(tiles_hbm.at[part], tiles.at[place], tile_sem.at[place])

    for turn in range(TILE_RING):

        @pl.when(turn < 2 * chunks)
        def _():
            tile_copy(turn).start()

    loads = fetch(
        load_sem, (mask_hbm, mask), (gh_hbm, gh), (refresh_hbm, refresh), (fx_hbm, fx)
    )
    pre[...] = jnp.zeros_like(pre)

    def clear(index, carry):
        acc[pl.ds(index * PER, PER)] = jnp.zeros((PER, TILE, TILE), F32)
        return carry

    lax.fori_loop(0, BLOCKS // PER, clear, 0)
    acc[BLOCKS] = jnp.zeros((TILE, TILE), F32)
    source_copy.wait()

    def next_tiles(turn):
        @pl.when(turn + TILE_RING < 2 * chunks)
        def _():
            tile_copy(turn + TILE_RING).start()

    def forward(chunk, carry):
        tile_copy(chunk).wait()
        place = chunk % TILE_RING
        for k in range(CHUNK):
            t = chunk * CHUNK + k
            rows = pl.ds(pl.multiple_of(src_ref[t] * TILE, TILE), TILE)
            product = dot(tiles[place, k], source[rows, :])
            d = jnp.where(t < live, dst_ref[t], PER)
            pre[pl.ds(d, 1)] = pre[pl.ds(d, 1)] + product[None]
        next_tiles(chunk)
        return carry

    lax.fori_loop(0, chunks, forward, 0)
    for copy in loads:
        copy.wait()
    for d in range(PER):
        total = pre[d]
        rows = pl.ds(d * TILE, TILE)
        hidden_ref[rows, :] = jnp.maximum(total, 0.0).astype(BF16)
        passed = jnp.where(total > 0, gh[rows, :].astype(F32), 0.0)
        kept = mask[pl.ds(d, 1), :].astype(F32)
        delta[d] = (jnp.transpose(passed) * kept).astype(BF16)

    def backward(chunk, carry):
        turn = chunks + chunk
        tile_copy(turn).wait()
        place = turn % TILE_RING
        for k in range(CHUNK):
            t = chunk * CHUNK + k
            product = dot(delta[dst_ref[t]], tiles[place, k])
            s = jnp.where(t < live, src_ref[t], BLOCKS)
            acc[pl.ds(s, 1)] = acc[pl.ds(s, 1)] + product[None]
        next_tiles(turn)
        return carry

    lax.fori_loop(0, chunks, backward, 0)

    def out_copy(slot):
        place = slot % STAGED
        return pltpu.make_async_copy(picked.at[place], picked_hbm.at[slot], out_sem.at[place])

    def pick(group, carry):
        for k in range(GROUP):
            slot = group * GROUP + k

            @pl.when(slot >= STAGED)
            def _():
                out_copy(slot - STAGED).wait()

        for k in range(GROUP):
            slot = group * GROUP + k
            part = slot_part(slot)
            chosen = refresh_by_rows(refresh[pl.ds(part, 1), :])
            blocks = [acc[part * PER + i].astype(BF16) for i in range(PER)]
            grads = dot(jnp.concatenate(blocks, axis=1), chosen)
            grads = jnp.where(part == me, 0.0, grads).astype(BF16)
            picked[pl.ds(slot % STAGED, 1)] = grads[None]
        for k in range(GROUP):
            out_copy(group * GROUP + k).start()
        return carry

    lax.fori_loop(0, PARTS // GROUP, pick, 0)
    for k in range(PER):
        own_ref[:, pl.ds(k * TILE, TILE)] = acc[me * PER + k].astype(BF16)
    gw_ref[...] = lax.dot_general(
        own_ref[...], fx[...], (((1,), (1,)), ((), ())), preferred_element_type=F32
    )
    for slot in range(PARTS - STAGED, PARTS):
        out_copy(slot).wait()


def scatter_kernel(
    refresh_hbm,
    w_hbm,
    own_hbm,
    gw_hbm,
    arr_hbm,
    picked_hbm,
    gf_out,
    gw_out,
    refresh,
    weight,
    own,
    own_in,
    base,
    gw,
    arr,
    work,
    sib,
    from_b1,
    from_b2,
    from_a,
    from_z,
    sum_core,
    sum_y,
    sum_x,
    sum_last,
    load_sem,
    small_sem,
    send_sem,
    recv_sem,
):
    me = Place()
    ready = me.greet(me.a_far, me.b_far, cross=True)
    f, a, b, z = me.feat, me.a, me.b, me.z
    order = (2, 1, 3, 0)

    def first_of(center, h):
        return ((center + order[h]) % RING) * 8

    loads = []
    for h in range(RING):
        first = first_of(a, h)
        copy = pltpu.make_async_copy(
            picked_hbm.at[pl.ds(me.core * CLASS + first, 8)],
            work.at[pl.ds(first, 8)],
            load_sem.at[h],
        )
        copy.start()
        loads.append(copy)
    small = fetch(
        small_sem,
        (arr_hbm, arr),
        (gw_hbm, gw),
        (own_hbm, own),
        (w_hbm, weight),
        (refresh_hbm, refresh),
    )
    ready()
    sends = []

    def send(src, dst, target, feat=None):
        k = len(sends)
        copy = pltpu.make_async_remote_copy(
            src_ref=src,
            dst_ref=dst,
            send_sem=send_sem.at[k],
            recv_sem=recv_sem.at[k],
            device_id=(target, f if feat is None else feat),
            device_id_type=MESH,
        )
        copy.start()
        sends.append(copy)
        return copy

    def add(first, size, *others):
        part = pl.ds(first, size)
        total = work[part].astype(F32)
        for other in others:
            total = total + other.astype(F32)
        work[part] = total.astype(BF16)

    to_sib = []
    for h in range(RING):
        first = first_of(b, h)
        src = picked_hbm.at[pl.ds((1 - me.core) * CLASS + first, 8)]
        to_sib.append(send(src, sib.at[pl.ds(first, 8)], me.sibling))
    own_copy = send(own_hbm, own_in, me.dom, 1 - f)

    def column(h, offset):
        return first_of(a, h) + ((b + offset) % RING) * 2

    b1, b2 = [], []

    def fold(h):
        first = first_of(a, h)
        loads[h].wait()
        to_sib[h].wait_recv()
        add(first, 8, sib[pl.ds(first, 8)])
        far, up, down = column(h, 2), column(h, 1), column(h, 3)
        b1.append(
            (
                send(work.at[pl.ds(far, 1)], from_b1.at[h, pl.ds(0, 1)], me.b_next),
                send(work.at[pl.ds(far + 1, 1)], from_b1.at[h, pl.ds(1, 1)], me.b_prev),
            )
        )
        b2.append(
            [
                send(work.at[pl.ds(up + 1, 1)], from_b2.at[h, 0, pl.ds(1, 1)], me.b_next),
                send(work.at[pl.ds(down, 1)], from_b2.at[h, 1, pl.ds(0, 1)], me.b_prev),
            ]
        )

    def weigh(h):
        first = first_of(a, h)
        total = gw[...]
        for k in range(8):
            total = total + dot(work[pl.ds(first + k, 1)][0], arr[pl.ds(first + k, 1)][0])
        gw[...] = total

    def relay(h):
        up, down = column(h, 1), column(h, 3)
        b1[h][0].wait_recv()
        add(up, 1, from_b1[h, pl.ds(0, 1)])
        b2[h].append(send(work.at[pl.ds(up, 1)], from_b2.at[h, 0, pl.ds(0, 1)], me.b_next))
        b1[h][1].wait_recv()
        add(down + 1, 1, from_b1[h, pl.ds(1, 1)])
        b2[h].append(send(work.at[pl.ds(down + 1, 1)], from_b2.at[h, 1, pl.ds(1, 1)], me.b_prev))

    along_a = []
    a_targets = (me.a_far, me.a_next, me.a_prev)

    def finish(h):
        here = column(h, 0)
        for copy in b2[h]:
            copy.wait_recv()
        if h < 3:
            add(here, 2, from_b2[h, 0], from_b2[h, 1])
            along_a.append(send(work.at[pl.ds(here, 2)], from_a.at[h], a_targets[h]))
        else:
            for copy in along_a:
                copy.wait_recv()
            add(here, 2, from_b2[h, 0], from_b2[h, 1], from_a[0], from_a[1], from_a[2])

    def ring_sum(buffer, index, targets):
        return [send(buffer.at[index], buffer.at[index], target) for target in targets]

    def take_sum(buffer, copies):
        for copy in copies:
            copy.wait_recv()
        return (buffer[0] + buffer[1]) + (buffer[2] + buffer[3])

    fold(0)
    small[0].wait()
    small[1].wait()
    fold(1)
    weigh(0)
    relay(0)
    fold(2)
    weigh(1)
    relay(1)
    fold(3)
    weigh(2)
    finish(0)
    weigh(3)
    sum_core[0] = jnp.transpose(gw[...])
    core_copy = send(sum_core.at[0], sum_core.at[1], me.sibling)
    relay(2)
    finish(1)
    relay(3)
    core_copy.wait_recv()
    sum_y[pl.ds(me.y, 1)] = (sum_core[0] + sum_core[1])[None]
    y_targets = [me.xy(me.x, me.y + k) for k in (1, 3, 2)]
    y_copies = ring_sum(sum_y, me.y, y_targets)
    finish(2)
    for copy in small[2:]:
        copy.wait()
    chosen = rows_by_refresh(refresh[pl.ds(me.dom, 1), :])
    own_columns, other_columns = column_block(f), column_block(1 - f)
    own_copy.wait_recv()
    base[...] = dot(weight[:, own_columns], own[...]) + dot(weight[:, other_columns], own_in[...])
    sum_x[pl.ds(me.x, 1)] = take_sum(sum_y, y_copies)[None]
    x_targets = [me.xy(me.x + k, me.y) for k in (1, 3, 2)]
    x_copies = ring_sum(sum_x, me.x, x_targets)
    finish(3)
    here = column(3, 0)
    mine, theirs = work.at[pl.ds(here + z, 1)], work.at[pl.ds(here + 1 - z, 1)]
    z_copies = (
        send(theirs, from_z.at[pl.ds(0, 1)], me.z_pair),
        send(mine, from_z.at[pl.ds(1, 1)], me.dom, 1 - f),
        send(theirs, from_z.at[pl.ds(2, 1)], me.z_pair, 1 - f),
    )
    sum_last[0] = take_sum(sum_x, x_copies)
    own_rows, other_rows = half_rows(f), half_rows(1 - f)
    last_copies = (
        send(sum_last.at[0, own_rows, :], sum_last.at[1, pl.ds(0, 64), :], me.z_pair),
        send(sum_last.at[0, other_rows, :], sum_last.at[1, pl.ds(64, 64), :], me.dom, 1 - f),
        send(sum_last.at[0, other_rows, :], sum_last.at[2, pl.ds(0, 64), :], me.z_pair, 1 - f),
    )
    for copy in z_copies:
        copy.wait_recv()
    carried = work[pl.ds(here + z, 1)][0].astype(F32) + from_z[0].astype(F32)
    carried_in = from_z[1].astype(F32) + from_z[2].astype(F32)
    short = dot(weight[:, own_columns], carried.astype(BF16)) + dot(
        weight[:, other_columns], carried_in.astype(BF16)
    )
    gf_out[...] = (base[...] + dot(short.astype(BF16), chosen)).astype(BF16)
    for copy in last_copies:
        copy.wait_recv()
    gw_out[:, own_columns] = sum_last[0, own_rows, :] + sum_last[1, pl.ds(0, 64), :]
    gw_out[:, other_columns] = sum_last[1, pl.ds(64, 64), :] + sum_last[2, pl.ds(0, 64), :]
    for copy in sends:
        copy.wait_send()


VMEM = pl.BlockSpec(memory_space=pltpu.VMEM)
SMEM = pl.BlockSpec(memory_space=pltpu.SMEM)
ANY = pl.BlockSpec(memory_space=pl.ANY)
DMA = pltpu.SemaphoreType.DMA


def shape(dims, kind):
    return jax.ShapeDtypeStruct(dims, kind)


def scratch(dims, kind):
    return pltpu.VMEM(dims, kind)


def params(**fields):
    return pltpu.CompilerParams(vmem_limit_bytes=62 * MIB, **fields)


def call_gather(features, weight, refresh, stale):
    return pl.pallas_call(
        gather_kernel,
        out_shape=(
            shape((CLASS, REF, TILE), BF16),
            shape((TILE, ROWS), BF16),
            shape((PARTS * ROWS, TILE), BF16),
        ),
        in_specs=[ANY] * 4,
        out_specs=(ANY, ANY, ANY),
        scratch_shapes=[
            scratch((PARTS, REF, TILE), BF16),
            scratch((CLASS * ROWS, TILE), BF16),
            scratch((ROWS, TILE), BF16),
            scratch((TILE, REF), BF16),
            scratch((TILE, ROWS), BF16),
            scratch((64, 2 * TILE), BF16),
            scratch((TILE, TILE), BF16),
            scratch((PARTS, REF), I32),
            DMA((6, PER + 1)),
            DMA((PARTS,)),
            DMA((3,)),
            DMA((3,)),
            DMA((PARTS,)),
            DMA((PARTS,)),
            DMA((3,)),
            DMA((PARTS,)),
            DMA((2,)),
            DMA((PARTS,)),
        ],
        compiler_params=params(collective_id=0, has_side_effects=True),
        name="gather_refreshed",
    )(features, weight, refresh, stale)


def call_tiles(src, dst, count, refresh, fx, mask, gh, source, tiles, name="tiles"):
    return pl.pallas_call(
        tiles_kernel,
        out_shape=(
            shape((ROWS, TILE), BF16),
            shape((PARTS, TILE, REF), BF16),
            shape((TILE, ROWS), BF16),
            shape((TILE, TILE), F32),
        ),
        in_specs=[SMEM] * 3 + [ANY] * 6,
        out_specs=(VMEM, ANY, VMEM, VMEM),
        scratch_shapes=[
            scratch((PARTS * ROWS, TILE), BF16),
            scratch((TILE_RING, CHUNK, TILE, TILE), BF16),
            scratch((PER + 1, TILE, TILE), F32),
            scratch((BLOCKS + 1, TILE, TILE), F32),
            scratch((PER, TILE, TILE), BF16),
            scratch((PARTS, REF), I32),
            scratch((TILE, ROWS), BF16),
            scratch((PER, TILE), I32),
            scratch((ROWS, TILE), BF16),
            scratch((STAGED, TILE, REF), BF16),
            DMA,
            DMA((TILE_RING,)),
            DMA((4,)),
            DMA((STAGED,)),
        ],
        compiler_params=params(),
        name=name,
    )(src, dst, count, refresh, fx, mask, gh, source, tiles)


def call_scatter(refresh, weight, own, gw, arr, picked):
    return pl.pallas_call(
        scatter_kernel,
        out_shape=(shape((64, ROWS), BF16), shape((64, 2 * TILE), F32)),
        in_specs=[ANY] * 6,
        out_specs=(VMEM, VMEM),
        scratch_shapes=[
            scratch((PARTS, REF), I32),
            scratch((64, 2 * TILE), BF16),
            scratch((TILE, ROWS), BF16),
            scratch((TILE, ROWS), BF16),
            scratch((64, ROWS), F32),
            scratch((TILE, TILE), F32),
            scratch((CLASS, REF, TILE), BF16),
            scratch((CLASS, TILE, REF), BF16),
            scratch((CLASS, TILE, REF), BF16),
            scratch((RING, 2, TILE, REF), BF16),
            scratch((RING, 2, 2, TILE, REF), BF16),
            scratch((3, 2, TILE, REF), BF16),
            scratch((3, TILE, REF), BF16),
            scratch((2, TILE, TILE), F32),
            scratch((RING, TILE, TILE), F32),
            scratch((RING, TILE, TILE), F32),
            scratch((3, TILE, TILE), F32),
            DMA((RING,)),
            DMA((5,)),
            DMA((48,)),
            DMA((48,)),
        ],
        compiler_params=params(collective_id=1, has_side_effects=True),
        name="scatter_gradients",
    )(refresh, weight, own, gw, arr, picked)


def shards(
    features,
    weight,
    stale_cache,
    adj_tiles,
    tile_src,
    tile_dst,
    tile_count,
    refresh,
    train_mask,
    grad_hidden,
):
    arr, fx, source = call_gather(features.T, weight, refresh, stale_cache)
    mask = train_mask.reshape(PER, TILE)
    hidden, picked, own, gw = call_tiles(
        tile_src,
        tile_dst,
        tile_count,
        refresh,
        fx,
        mask,
        grad_hidden,
        source,
        adj_tiles,
    )
    grad_features, grad_weight = call_scatter(refresh, weight, own, gw, arr, picked)
    return hidden, grad_features.T, grad_weight


def solution(mesh):
    placed = (
        P("dom", "feat"),
        P("feat", None),
        P(None, "feat"),
        P("dom", None, None),
        P("dom"),
        P("dom"),
        P("dom"),
        P(),
        P("dom"),
        P("dom", "feat"),
    )
    return jax.shard_map(
        shards,
        mesh=mesh,
        in_specs=placed,
        out_specs=(P("dom", "feat"), P("dom", "feat"), P("feat", None)),
        check_vma=False,
    )
```

```python
import jax
import jax.numpy as jnp
from jax import lax
from jax.experimental import pallas as pl
from jax.experimental.pallas import tpu as pltpu
from jax.sharding import PartitionSpec as P

MESH = pl.DeviceIdType.MESH
BF16 = jnp.bfloat16
F32 = jnp.float32
I32 = jnp.int32

ROWS = 1024
REF = 256
TILE = 128
NT = 768
PARTS = 64
BLOCKS = PARTS * ROWS // TILE
PER = ROWS // TILE
RING = 4
CLASS = PARTS // 2
MIB = 1024 * 1024


def dot(lhs, rhs):
    return jnp.dot(lhs, rhs, preferred_element_type=F32)


class Place:
    def __init__(self):
        self.dom = lax.axis_index("dom")
        self.feat = lax.axis_index("feat")
        self.core = self.dom % 2
        self.z = (self.dom // 2) % 2
        self.y = (self.dom // 4) % RING
        self.x = self.dom // 16
        self.a = self.x * (1 - self.core) + self.y * self.core
        self.b = self.y * (1 - self.core) + self.x * self.core
        self.sibling = self.dom + 1 - 2 * self.core
        self.z_pair = self.dom + 2 - 4 * self.z
        self.cross = self.sibling + 2 - 4 * self.z
        self.a_next = self.at(self.a + 1, self.b)
        self.a_prev = self.at(self.a + 3, self.b)
        self.b_next = self.at(self.a, self.b + 1)
        self.b_prev = self.at(self.a, self.b + 3)
        self.a_far = self.at(self.a + 2, self.b)
        self.b_far = self.at(self.a, self.b + 2)

    def at(self, a, b):
        a, b = a % RING, b % RING
        x = a * (1 - self.core) + b * self.core
        y = b * (1 - self.core) + a * self.core
        return ((x * RING + y) * 2 + self.z) * 2 + self.core

    def xy(self, x, y):
        return (((x % RING) * RING + y % RING) * 2 + self.z) * 2 + self.core

    def slot(self, a, b, z):
        return self.core * CLASS + (a % RING) * 8 + (b % RING) * 2 + z

    def greet(self, *more, cross=False):
        barrier = pltpu.get_barrier_semaphore()
        near = (self.sibling, self.z_pair, self.a_next, self.a_prev, self.b_next, self.b_prev)
        near = near + more
        for device in near:
            pl.semaphore_signal(barrier, inc=1, device_id=(device, self.feat), device_id_type=MESH)
        pairs = (self.dom, self.sibling, self.z_pair, self.cross) if cross else (self.dom,)
        for device in pairs:
            pl.semaphore_signal(
                barrier, inc=1, device_id=(device, 1 - self.feat), device_id_type=MESH
            )
        return lambda: pl.semaphore_wait(barrier, len(near) + len(pairs))


def slot_part(slot):
    core, a, b, z = slot // CLASS, (slot // 8) % RING, (slot // 2) % RING, slot % 2
    x = a * (1 - core) + b * core
    y = b * (1 - core) + a * core
    return ((x * RING + y) * 2 + z) * 2 + core


def rows_by_refresh(row):
    column = jnp.transpose(jnp.broadcast_to(row, (TILE, REF)))
    lanes = lax.broadcasted_iota(I32, (REF, TILE), 1)
    parts = [(column == lanes + k * TILE).astype(F32).astype(BF16) for k in range(PER)]
    return jnp.concatenate(parts, axis=1)


def refresh_by_rows(row):
    rows = lax.broadcasted_iota(jnp.int16, (ROWS, REF), 0)
    one, zero = jnp.ones((), BF16), jnp.zeros((), BF16)
    return jnp.where(rows == row.astype(jnp.int16), one, zero)


def fetch(sems, *pairs):
    copies = [pltpu.make_async_copy(src, dst, sems.at[k]) for k, (src, dst) in enumerate(pairs)]
    for copy in copies:
        copy.start()
    return copies


def half_rows(index):
    return pl.ds(pl.multiple_of(index * 64, 64), 64)


def column_block(index):
    return pl.ds(pl.multiple_of(index * TILE, TILE), TILE)


PLANE = ((0, 0), (0, 1), (3, 0), (1, 0), (3, 1), (1, 1), (2, 0), (2, 1))


def gather_kernel(
    feat_hbm,
    w_hbm,
    refresh_hbm,
    stale_hbm,
    arr_out,
    fx_out,
    source_out,
    arr,
    source,
    fresh_own,
    pick,
    fx,
    weight,
    wcol,
    refresh,
    send_sem,
    recv_sem,
    pair_send,
    pair_recv,
    give_sem,
    take_sem,
    load_sem,
    stale_sem,
    out_sem,
    row_sem,
):
    me = Place()
    f = me.feat
    own_rows, pair_rows = half_rows(f), half_rows(1 - f)
    own_columns, pair_columns = column_block(f), column_block(1 - f)
    loads = fetch(
        load_sem, (feat_hbm, fx.at[own_rows, :]), (w_hbm, weight), (refresh_hbm, refresh)
    )
    ready = me.greet(me.a_far)
    loads[2].wait()
    chosen = refresh_by_rows(refresh[pl.ds(me.dom, 1), :])
    loads[0].wait()
    pick[own_rows, :] = dot(fx[own_rows, :], chosen).astype(BF16)
    loads[1].wait()
    wcol[own_rows, :] = weight[:, own_columns]
    ready()

    def to_pair(k, src, dst):
        return pltpu.make_async_remote_copy(
            src_ref=src,
            dst_ref=dst,
            send_sem=pair_send.at[k],
            recv_sem=pair_recv.at[k],
            device_id=(me.dom, 1 - f),
            device_id_type=MESH,
        )

    pick_copy = to_pair(0, pick.at[own_rows, :], pick.at[own_rows, :])
    pick_copy.start()
    w_copy = to_pair(1, weight.at[:, pair_columns], wcol.at[own_rows, :])
    w_copy.start()
    fx_copy = to_pair(2, fx.at[own_rows, :], fx.at[own_rows, :])

    def shard(slot, target, kind, p):
        return pltpu.make_async_remote_copy(
            src_ref=arr.at[slot],
            dst_ref=arr.at[slot],
            send_sem=send_sem.at[kind, p],
            recv_sem=recv_sem.at[slot],
            device_id=(target, f),
            device_id_type=MESH,
        )

    def arrive(slot):
        shard(slot, me.sibling, 0, 0).wait_recv()

    def slot_of(p, b_offset):
        a_offset, pair = PLANE[p]
        return me.slot(me.a + a_offset, me.b + b_offset, (me.z + pair) % 2)

    def pass_on(p):
        slot = slot_of(p, 0)
        shard(slot, me.b_next, 0, p).start()
        shard(slot, me.b_prev, 1, p).start()

    def along_a(p):
        slot = slot_of(p, 0)
        shard(slot, me.a_next, 3, p).start()
        shard(slot, me.a_prev, 4, p).start()
        shard(slot, me.a_far, 5, p).start()

    def take_plane(p):
        slot = slot_of(p, 0)
        arrive(slot)
        if p == 1:
            along_a(p)
        pass_on(p)
        return slot

    def take_b(p):
        below, above = slot_of(p, 3), slot_of(p, 1)
        arrive(below)
        if PLANE[p][1] == 0:
            shard(below, me.b_next, 2, p).start()
        arrive(above)
        if PLANE[p][1] == 1:
            shard(above, me.b_prev, 2, p).start()
        return below, above

    def take_far(p):
        slot = slot_of(p, 2)
        arrive(slot)
        return slot

    ones = jnp.ones((REF, TILE), BF16)

    class_first = me.core * CLASS

    def held(slot):
        return pl.ds(pl.multiple_of((slot - class_first) * ROWS, ROWS), ROWS)

    def rows_of(part):
        return pl.ds(pl.multiple_of(part * ROWS, ROWS), ROWS)

    def load_rows(slot):
        return pltpu.make_async_copy(
            stale_hbm.at[rows_of(slot_part(slot))], source.at[held(slot)], stale_sem.at[slot]
        )

    def keep_rows(slot):
        return pltpu.make_async_copy(
            source.at[held(slot)], source_out.at[rows_of(slot_part(slot))], row_sem.at[slot]
        )

    def give_rows(slot, src):
        return pltpu.make_async_remote_copy(
            src_ref=src,
            dst_ref=source_out.at[rows_of(slot_part(slot))],
            send_sem=give_sem.at[slot],
            recv_sem=take_sem.at[slot],
            device_id=(me.sibling, f),
            device_id_type=MESH,
        )

    mine = slot_of(0, 0)

    def merge(*slots):
        fresh = [dot(arr[pl.ds(slot, 1)][0], wcol[...]).astype(BF16) for slot in slots]
        for slot, new in zip(slots, fresh):
            chosen = refresh_by_rows(refresh[pl.ds(slot_part(slot), 1), :])
            placed = dot(chosen, jnp.concatenate([new, ones], axis=1))
            rows = held(slot)
            old = source[rows, :].astype(F32)
            source[rows, :] = jnp.where(placed[:, TILE:] > 0, placed[:, :TILE], old).astype(BF16)
        for slot in slots:
            give_rows(slot, source.at[held(slot)]).start()
            if slot is not mine:
                keep_rows(slot).start()

    pick_copy.wait_recv()
    arr[pl.ds(mine, 1)] = jnp.transpose(pick[...].astype(F32)).astype(BF16)[None]
    pair_sent = shard(mine, me.z_pair, 2, PER)
    pair_sent.start()
    along_a(0)
    pass_on(0)

    def start_load(k, carry):
        load_rows(class_first + k).start()
        return carry

    def wait_load(k, carry):
        load_rows(class_first + k).wait()
        return carry

    lax.fori_loop(0, CLASS, start_load, 0)
    left, right = take_plane(2), take_plane(3)
    b0 = take_b(0)
    z_pair = take_plane(1)
    across = take_plane(6)
    fx_copy.start()
    w_copy.wait_recv()
    lax.fori_loop(0, CLASS, wait_load, 0)
    merge(left, right, *b0)
    merge(z_pair, across, mine)
    left, right = take_plane(4), take_plane(5)
    b2, b3 = take_b(2), take_b(3)
    merge(left, right, *b2)
    across = take_plane(7)
    b1, b6 = take_b(1), take_b(6)
    merge(*b3, *b1)
    b4, b5 = take_b(4), take_b(5)
    far0 = take_far(0)
    merge(*b6, across, far0)
    b7 = take_b(7)
    merge(*b4, *b5)
    merge(*b7, take_far(2), take_far(3))
    merge(take_far(1), take_far(6), take_far(4), take_far(5))
    merge(take_far(7))
    keep_arr = pltpu.make_async_copy(arr.at[pl.ds(class_first, CLASS)], arr_out, out_sem.at[0])
    keep_arr.start()
    fx_copy.wait_recv()
    keep_fx = pltpu.make_async_copy(fx, fx_out, out_sem.at[1])
    keep_fx.start()
    fresh_own[...] = lax.dot_general(
        fx[...], wcol[...], (((0,), (0,)), ((), ())), preferred_element_type=F32
    ).astype(BF16)
    keep_own = pltpu.make_async_copy(fresh_own, source_out.at[rows_of(me.dom)], row_sem.at[mine])
    keep_own.start()

    def settle(p, carry):
        for kind in range(3):
            shard(mine, me.sibling, kind, p).wait_send()
        return carry

    lax.fori_loop(0, PER, settle, 0)
    for p in range(2):
        for kind in range(3, 6):
            shard(mine, me.sibling, kind, p).wait_send()
    pair_sent.wait_send()
    pick_copy.wait_send()
    w_copy.wait_send()
    fx_copy.wait_send()

    def settle_rows(k, carry):
        given, taken = class_first + k, CLASS - class_first + k
        give_rows(given, source.at[held(given)]).wait_send()
        give_rows(taken, source_out.at[rows_of(slot_part(taken))]).wait_recv()
        keep_rows(class_first + k).wait()
        return carry

    lax.fori_loop(0, CLASS, settle_rows, 0)
    keep_fx.wait()
    keep_arr.wait()


GROUP = 8
CHUNK = 64
TILE_RING = 3
STAGED = 16


def tiles_kernel(
    src_ref,
    dst_ref,
    count_ref,
    refresh_hbm,
    fx_hbm,
    mask_hbm,
    gh_hbm,
    source_hbm,
    tiles_hbm,
    hidden_ref,
    picked_hbm,
    own_ref,
    gw_ref,
    source,
    tiles,
    pre,
    acc,
    delta,
    refresh,
    fx,
    mask,
    gh,
    picked,
    source_sem,
    tile_sem,
    load_sem,
    out_sem,
):
    me = lax.axis_index("dom")
    live = count_ref[0]
    chunks = (live + CHUNK - 1) // CHUNK
    source_copy = pltpu.make_async_copy(source_hbm, source, source_sem)
    source_copy.start()

    def tile_copy(turn):
        chunk = jnp.where(turn < chunks, turn, turn - chunks)
        place = turn % TILE_RING
        part = pl.ds(chunk * CHUNK, CHUNK)
        return pltpu.make_async_copy(tiles_hbm.at[part], tiles.at[place], tile_sem.at[place])

    for turn in range(TILE_RING):

        @pl.when(turn < 2 * chunks)
        def _():
            tile_copy(turn).start()

    loads = fetch(
        load_sem, (mask_hbm, mask), (gh_hbm, gh), (refresh_hbm, refresh), (fx_hbm, fx)
    )
    pre[...] = jnp.zeros_like(pre)

    def clear(index, carry):
        acc[pl.ds(index * PER, PER)] = jnp.zeros((PER, TILE, TILE), F32)
        return carry

    lax.fori_loop(0, BLOCKS // PER, clear, 0)
    acc[BLOCKS] = jnp.zeros((TILE, TILE), F32)
    source_copy.wait()

    def next_tiles(turn):
        @pl.when(turn + TILE_RING < 2 * chunks)
        def _():
            tile_copy(turn + TILE_RING).start()

    def forward(chunk, carry):
        tile_copy(chunk).wait()
        place = chunk % TILE_RING
        for k in range(CHUNK):
            t = chunk * CHUNK + k
            rows = pl.ds(pl.multiple_of(src_ref[t] * TILE, TILE), TILE)
            product = dot(tiles[place, k], source[rows, :])
            d = jnp.where(t < live, dst_ref[t], PER)
            pre[pl.ds(d, 1)] = pre[pl.ds(d, 1)] + product[None]
        next_tiles(chunk)
        return carry

    lax.fori_loop(0, chunks, forward, 0)
    for copy in loads:
        copy.wait()
    for d in range(PER):
        total = pre[d]
        rows = pl.ds(d * TILE, TILE)
        hidden_ref[rows, :] = jnp.maximum(total, 0.0).astype(BF16)
        passed = jnp.where(total > 0, gh[rows, :].astype(F32), 0.0)
        kept = mask[pl.ds(d, 1), :].astype(F32)
        delta[d] = (jnp.transpose(passed) * kept).astype(BF16)

    def backward(chunk, carry):
        turn = chunks + chunk
        tile_copy(turn).wait()
        place = turn % TILE_RING
        for k in range(CHUNK):
            t = chunk * CHUNK + k
            product = dot(delta[dst_ref[t]], tiles[place, k])
            s = jnp.where(t < live, src_ref[t], BLOCKS)
            acc[pl.ds(s, 1)] = acc[pl.ds(s, 1)] + product[None]
        next_tiles(turn)
        return carry

    lax.fori_loop(0, chunks, backward, 0)

    def out_copy(slot):
        place = slot % STAGED
        return pltpu.make_async_copy(picked.at[place], picked_hbm.at[slot], out_sem.at[place])

    def pick(group, carry):
        for k in range(GROUP):
            slot = group * GROUP + k

            @pl.when(slot >= STAGED)
            def _():
                out_copy(slot - STAGED).wait()

        for k in range(GROUP):
            slot = group * GROUP + k
            part = slot_part(slot)
            chosen = refresh_by_rows(refresh[pl.ds(part, 1), :])
            blocks = [acc[part * PER + i].astype(BF16) for i in range(PER)]
            grads = dot(jnp.concatenate(blocks, axis=1), chosen)
            grads = jnp.where(part == me, 0.0, grads).astype(BF16)
            picked[pl.ds(slot % STAGED, 1)] = grads[None]
        for k in range(GROUP):
            out_copy(group * GROUP + k).start()
        return carry

    lax.fori_loop(0, PARTS // GROUP, pick, 0)
    for k in range(PER):
        own_ref[:, pl.ds(k * TILE, TILE)] = acc[me * PER + k].astype(BF16)
    gw_ref[...] = lax.dot_general(
        own_ref[...], fx[...], (((1,), (1,)), ((), ())), preferred_element_type=F32
    )
    for slot in range(PARTS - STAGED, PARTS):
        out_copy(slot).wait()


def scatter_kernel(
    refresh_hbm,
    w_hbm,
    own_hbm,
    gw_hbm,
    arr_hbm,
    picked_hbm,
    gf_out,
    gw_out,
    refresh,
    weight,
    own,
    own_in,
    base,
    gw,
    arr,
    work,
    sib,
    from_b1,
    from_b2,
    from_a,
    from_z,
    sum_y,
    sum_x,
    sum_out,
    sum_last,
    load_sem,
    small_sem,
    send_sem,
    recv_sem,
):
    me = Place()
    ready = me.greet(me.a_far, me.b_far, me.cross, cross=True)
    f, a, b, z = me.feat, me.a, me.b, me.z
    order = (2, 1, 3, 0)

    def first_of(center, h):
        return ((center + order[h]) % RING) * 8

    loads = []
    for h in range(RING):
        first = first_of(a, h)
        copy = pltpu.make_async_copy(
            picked_hbm.at[pl.ds(me.core * CLASS + first, 8)],
            work.at[pl.ds(first, 8)],
            load_sem.at[h],
        )
        copy.start()
        loads.append(copy)
    small = fetch(
        small_sem,
        (arr_hbm, arr),
        (gw_hbm, gw),
        (own_hbm, own),
        (w_hbm, weight),
        (refresh_hbm, refresh),
    )
    ready()
    sends = []

    def send(src, dst, target, feat=None):
        k = len(sends)
        copy = pltpu.make_async_remote_copy(
            src_ref=src,
            dst_ref=dst,
            send_sem=send_sem.at[k],
            recv_sem=recv_sem.at[k],
            device_id=(target, f if feat is None else feat),
            device_id_type=MESH,
        )
        copy.start()
        sends.append(copy)
        return copy

    def add(first, size, *others):
        part = pl.ds(first, size)
        total = work[part].astype(F32)
        for other in others:
            total = total + other.astype(F32)
        work[part] = total.astype(BF16)

    to_sib = []
    for h in range(RING):
        first = first_of(b, h)
        src = picked_hbm.at[pl.ds((1 - me.core) * CLASS + first, 8)]
        to_sib.append(send(src, sib.at[pl.ds(first, 8)], me.sibling))
    own_copy = send(own_hbm, own_in, me.dom, 1 - f)

    def column(h, offset):
        return first_of(a, h) + ((b + offset) % RING) * 2

    b1, b2 = [], []

    def fold(h):
        first = first_of(a, h)
        loads[h].wait()
        to_sib[h].wait_recv()
        add(first, 8, sib[pl.ds(first, 8)])

    def launch(h):
        far, up, down = column(h, 2), column(h, 1), column(h, 3)
        b1.append(
            (
                send(work.at[pl.ds(far, 1)], from_b1.at[h, pl.ds(0, 1)], me.b_next),
                send(work.at[pl.ds(far + 1, 1)], from_b1.at[h, pl.ds(1, 1)], me.b_prev),
            )
        )
        b2.append(
            [
                send(work.at[pl.ds(up + 1, 1)], from_b2.at[h, 0, pl.ds(1, 1)], me.b_next),
                send(work.at[pl.ds(down, 1)], from_b2.at[h, 1, pl.ds(0, 1)], me.b_prev),
            ]
        )

    def weigh(h):
        first = first_of(a, h)
        total = gw[...]
        for k in range(8):
            total = total + dot(work[pl.ds(first + k, 1)][0], arr[pl.ds(first + k, 1)][0])
        gw[...] = total

    def relay(h):
        up, down = column(h, 1), column(h, 3)
        b1[h][0].wait_recv()
        add(up, 1, from_b1[h, pl.ds(0, 1)])
        b2[h].append(send(work.at[pl.ds(up, 1)], from_b2.at[h, 0, pl.ds(0, 1)], me.b_next))
        b1[h][1].wait_recv()
        add(down + 1, 1, from_b1[h, pl.ds(1, 1)])
        b2[h].append(send(work.at[pl.ds(down + 1, 1)], from_b2.at[h, 1, pl.ds(1, 1)], me.b_prev))

    along_a = []
    a_targets = (me.a_far, me.a_next, me.a_prev)

    def finish(h):
        here = column(h, 0)
        for copy in b2[h]:
            copy.wait_recv()
        if h < 3:
            add(here, 2, from_b2[h, 0], from_b2[h, 1])
            along_a.append(send(work.at[pl.ds(here, 2)], from_a.at[h], a_targets[h]))
        else:
            for copy in along_a:
                copy.wait_recv()
            add(here, 2, from_b2[h, 0], from_b2[h, 1], from_a[0], from_a[1], from_a[2])

    def ring_sum(buffer, index, targets):
        return [send(buffer.at[index], buffer.at[index], target) for target in targets]

    def total_of(terms):
        one, two, three, four = [term.astype(F32) for term in terms]
        return (one + two) + (three + four)

    def take_sum(buffer, copies):
        for copy in copies:
            copy.wait_recv()
        return total_of([buffer[k] for k in range(RING)]).astype(BF16)

    fold(0)
    launch(0)
    small[0].wait()
    small[1].wait()
    fold(1)
    launch(1)
    fold(2)
    weigh(0)
    fold(3)
    weigh(1)
    weigh(2)
    weigh(3)
    sum_y[pl.ds(me.y, 1)] = jnp.transpose(gw[...]).astype(BF16)[None]
    y_targets = [me.xy(me.x, me.y + k) for k in (1, 3, 2)]
    y_copies = ring_sum(sum_y, me.y, y_targets)
    launch(2)
    relay(0)
    launch(3)
    relay(1)
    finish(0)
    relay(2)
    sum_x[pl.ds(me.x, 1)] = take_sum(sum_y, y_copies)[None]
    x_targets = [me.xy(me.x + k, me.y) for k in (1, 3, 2)]
    x_copies = ring_sum(sum_x, me.x, x_targets)
    finish(1)
    relay(3)
    for copy in small[2:]:
        copy.wait()
    chosen = rows_by_refresh(refresh[pl.ds(me.dom, 1), :])
    own_columns, other_columns = column_block(f), column_block(1 - f)
    own_rows, other_rows = half_rows(f), half_rows(1 - f)
    own_copy.wait_recv()
    base[...] = dot(weight[:, own_columns], own[...]) + dot(weight[:, other_columns], own_in[...])
    finish(2)
    sum_out[...] = take_sum(sum_x, x_copies)
    place = me.core * 2 + z
    sum_last[0, pl.ds(place, 1)] = sum_out[own_rows, :][None]
    last_copies = [
        send(sum_out.at[own_rows, :], sum_last.at[0, place], target)
        for target in (me.sibling, me.z_pair, me.cross)
    ]
    last_copies += [
        send(sum_out.at[other_rows, :], sum_last.at[1, place], target, 1 - f)
        for target in (me.dom, me.sibling, me.z_pair, me.cross)
    ]
    finish(3)
    here = column(3, 0)
    mine, theirs = work.at[pl.ds(here + z, 1)], work.at[pl.ds(here + 1 - z, 1)]
    z_copies = (
        send(theirs, from_z.at[pl.ds(0, 1)], me.z_pair),
        send(mine, from_z.at[pl.ds(1, 1)], me.dom, 1 - f),
        send(theirs, from_z.at[pl.ds(2, 1)], me.z_pair, 1 - f),
    )
    for copy in z_copies:
        copy.wait_recv()
    carried = work[pl.ds(here + z, 1)][0].astype(F32) + from_z[0].astype(F32)
    carried_in = from_z[1].astype(F32) + from_z[2].astype(F32)
    short = dot(weight[:, own_columns], carried.astype(BF16)) + dot(
        weight[:, other_columns], carried_in.astype(BF16)
    )
    gf_out[...] = (base[...] + dot(short.astype(BF16), chosen)).astype(BF16)
    for copy in last_copies:
        copy.wait_recv()
    gw_out[:, own_columns] = total_of([sum_last[0, k] for k in range(4)])
    gw_out[:, other_columns] = total_of([sum_last[1, k] for k in range(4)])
    for copy in sends:
        copy.wait_send()


def finish_kernel(gf_hbm, gw_hbm, gf_out, gw_out, sems):
    for copy in fetch(sems, (gf_hbm, gf_out), (gw_hbm, gw_out)):
        copy.wait()


VMEM = pl.BlockSpec(memory_space=pltpu.VMEM)
SMEM = pl.BlockSpec(memory_space=pltpu.SMEM)
ANY = pl.BlockSpec(memory_space=pl.ANY)
DMA = pltpu.SemaphoreType.DMA


def shape(dims, kind):
    return jax.ShapeDtypeStruct(dims, kind)


def scratch(dims, kind):
    return pltpu.VMEM(dims, kind)


def params(**fields):
    return pltpu.CompilerParams(vmem_limit_bytes=62 * MIB, **fields)


def call_gather(features, weight, refresh, stale):
    return pl.pallas_call(
        gather_kernel,
        out_shape=(
            shape((CLASS, REF, TILE), BF16),
            shape((TILE, ROWS), BF16),
            shape((PARTS * ROWS, TILE), BF16),
        ),
        in_specs=[ANY] * 4,
        out_specs=(ANY, ANY, ANY),
        scratch_shapes=[
            scratch((PARTS, REF, TILE), BF16),
            scratch((CLASS * ROWS, TILE), BF16),
            scratch((ROWS, TILE), BF16),
            scratch((TILE, REF), BF16),
            scratch((TILE, ROWS), BF16),
            scratch((64, 2 * TILE), BF16),
            scratch((TILE, TILE), BF16),
            scratch((PARTS, REF), I32),
            DMA((6, PER + 1)),
            DMA((PARTS,)),
            DMA((3,)),
            DMA((3,)),
            DMA((PARTS,)),
            DMA((PARTS,)),
            DMA((3,)),
            DMA((PARTS,)),
            DMA((2,)),
            DMA((PARTS,)),
        ],
        compiler_params=params(collective_id=0, has_side_effects=True),
        name="gather_refreshed",
    )(features, weight, refresh, stale)


def call_tiles(src, dst, count, refresh, fx, mask, gh, source, tiles, name="tiles"):
    return pl.pallas_call(
        tiles_kernel,
        out_shape=(
            shape((ROWS, TILE), BF16),
            shape((PARTS, TILE, REF), BF16),
            shape((TILE, ROWS), BF16),
            shape((TILE, TILE), F32),
        ),
        in_specs=[SMEM] * 3 + [ANY] * 6,
        out_specs=(VMEM, ANY, VMEM, VMEM),
        scratch_shapes=[
            scratch((PARTS * ROWS, TILE), BF16),
            scratch((TILE_RING, CHUNK, TILE, TILE), BF16),
            scratch((PER + 1, TILE, TILE), F32),
            scratch((BLOCKS + 1, TILE, TILE), F32),
            scratch((PER, TILE, TILE), BF16),
            scratch((PARTS, REF), I32),
            scratch((TILE, ROWS), BF16),
            scratch((PER, TILE), I32),
            scratch((ROWS, TILE), BF16),
            scratch((STAGED, TILE, REF), BF16),
            DMA,
            DMA((TILE_RING,)),
            DMA((4,)),
            DMA((STAGED,)),
        ],
        compiler_params=params(),
        name=name,
    )(src, dst, count, refresh, fx, mask, gh, source, tiles)


def call_scatter(refresh, weight, own, gw, arr, picked):
    return pl.pallas_call(
        scatter_kernel,
        out_shape=(shape((64, ROWS), BF16), shape((64, 2 * TILE), F32)),
        in_specs=[ANY] * 6,
        out_specs=(VMEM, VMEM),
        scratch_shapes=[
            scratch((PARTS, REF), I32),
            scratch((64, 2 * TILE), BF16),
            scratch((TILE, ROWS), BF16),
            scratch((TILE, ROWS), BF16),
            scratch((64, ROWS), F32),
            scratch((TILE, TILE), F32),
            scratch((CLASS, REF, TILE), BF16),
            scratch((CLASS, TILE, REF), BF16),
            scratch((CLASS, TILE, REF), BF16),
            scratch((RING, 2, TILE, REF), BF16),
            scratch((RING, 2, 2, TILE, REF), BF16),
            scratch((3, 2, TILE, REF), BF16),
            scratch((3, TILE, REF), BF16),
            scratch((RING, TILE, TILE), BF16),
            scratch((RING, TILE, TILE), BF16),
            scratch((TILE, TILE), BF16),
            scratch((2, 4, 64, TILE), BF16),
            DMA((RING,)),
            DMA((5,)),
            DMA((48,)),
            DMA((48,)),
        ],
        compiler_params=params(collective_id=1, has_side_effects=True),
        name="scatter_gradients",
    )(refresh, weight, own, gw, arr, picked)


def call_finish(gf, gw):
    return pl.pallas_call(
        finish_kernel,
        out_shape=(shape(gf.shape, gf.dtype), shape(gw.shape, gw.dtype)),
        in_specs=[ANY] * 2,
        out_specs=(ANY, ANY),
        scratch_shapes=[DMA((2,))],
        compiler_params=params(),
        name="finish",
    )(gf, gw)


def shards(
    features,
    weight,
    stale_cache,
    adj_tiles,
    tile_src,
    tile_dst,
    tile_count,
    refresh,
    train_mask,
    grad_hidden,
):
    arr, fx, source = call_gather(features.T, weight, refresh, stale_cache)
    mask = train_mask.reshape(PER, TILE)
    hidden, picked, own, gw = call_tiles(
        tile_src,
        tile_dst,
        tile_count,
        refresh,
        fx,
        mask,
        grad_hidden,
        source,
        adj_tiles,
    )
    grads = call_scatter(refresh, weight, own, gw, arr, picked)
    grad_features, grad_weight = call_finish(*grads)
    return hidden, grad_features.T, grad_weight


def solution(mesh):
    placed = (
        P("dom", "feat"),
        P("feat", None),
        P(None, "feat"),
        P("dom", None, None),
        P("dom"),
        P("dom"),
        P("dom"),
        P(),
        P("dom"),
        P("dom", "feat"),
    )
    return jax.shard_map(
        shards,
        mesh=mesh,
        in_specs=placed,
        out_specs=(P("dom", "feat"), P("dom", "feat"), P("feat", None)),
        check_vma=False,
    )
```

```python
import jax
import jax.numpy as jnp
from jax import lax
from jax.experimental import pallas as pl
from jax.experimental.pallas import tpu as pltpu
from jax.sharding import PartitionSpec as P

MESH = pl.DeviceIdType.MESH
BF16 = jnp.bfloat16
F32 = jnp.float32
I32 = jnp.int32

ROWS = 1024
REF = 256
TILE = 128
NT = 768
PARTS = 64
BLOCKS = PARTS * ROWS // TILE
PER = ROWS // TILE
RING = 4
CLASS = PARTS // 2
MIB = 1024 * 1024


def dot(lhs, rhs):
    return jnp.dot(lhs, rhs, preferred_element_type=F32)


class Place:
    def __init__(self):
        self.dom = lax.axis_index("dom")
        self.feat = lax.axis_index("feat")
        self.core = self.dom % 2
        self.z = (self.dom // 2) % 2
        self.y = (self.dom // 4) % RING
        self.x = self.dom // 16
        self.a = self.x * (1 - self.core) + self.y * self.core
        self.b = self.y * (1 - self.core) + self.x * self.core
        self.sibling = self.dom + 1 - 2 * self.core
        self.z_pair = self.dom + 2 - 4 * self.z
        self.cross = self.sibling + 2 - 4 * self.z
        self.a_next = self.at(self.a + 1, self.b)
        self.a_prev = self.at(self.a + 3, self.b)
        self.b_next = self.at(self.a, self.b + 1)
        self.b_prev = self.at(self.a, self.b + 3)
        self.a_far = self.at(self.a + 2, self.b)
        self.b_far = self.at(self.a, self.b + 2)

    def at(self, a, b):
        a, b = a % RING, b % RING
        x = a * (1 - self.core) + b * self.core
        y = b * (1 - self.core) + a * self.core
        return ((x * RING + y) * 2 + self.z) * 2 + self.core

    def xy(self, x, y):
        return (((x % RING) * RING + y % RING) * 2 + self.z) * 2 + self.core

    def slot(self, a, b, z):
        return self.core * CLASS + (a % RING) * 8 + (b % RING) * 2 + z

    def greet(self, *more, cross=False):
        barrier = pltpu.get_barrier_semaphore()
        near = (self.sibling, self.z_pair, self.a_next, self.a_prev, self.b_next, self.b_prev)
        near = near + more
        for device in near:
            pl.semaphore_signal(barrier, inc=1, device_id=(device, self.feat), device_id_type=MESH)
        pairs = (self.dom, self.sibling, self.z_pair, self.cross) if cross else (self.dom,)
        for device in pairs:
            pl.semaphore_signal(
                barrier, inc=1, device_id=(device, 1 - self.feat), device_id_type=MESH
            )
        return lambda: pl.semaphore_wait(barrier, len(near) + len(pairs))


def slot_part(slot):
    core, a, b, z = slot // CLASS, (slot // 8) % RING, (slot // 2) % RING, slot % 2
    x = a * (1 - core) + b * core
    y = b * (1 - core) + a * core
    return ((x * RING + y) * 2 + z) * 2 + core


def rows_by_refresh(row):
    column = jnp.transpose(jnp.broadcast_to(row, (TILE, REF)))
    lanes = lax.broadcasted_iota(I32, (REF, TILE), 1)
    parts = [(column == lanes + k * TILE).astype(F32).astype(BF16) for k in range(PER)]
    return jnp.concatenate(parts, axis=1)


def refresh_by_rows(row):
    rows = lax.broadcasted_iota(jnp.int16, (ROWS, REF), 0)
    one, zero = jnp.ones((), BF16), jnp.zeros((), BF16)
    return jnp.where(rows == row.astype(jnp.int16), one, zero)


def fetch(sems, *pairs):
    copies = [pltpu.make_async_copy(src, dst, sems.at[k]) for k, (src, dst) in enumerate(pairs)]
    for copy in copies:
        copy.start()
    return copies


def half_rows(index):
    return pl.ds(pl.multiple_of(index * 64, 64), 64)


def column_block(index):
    return pl.ds(pl.multiple_of(index * TILE, TILE), TILE)


PLANE = ((0, 0), (0, 1), (3, 0), (1, 0), (3, 1), (1, 1), (2, 0), (2, 1))


def gather_kernel(
    feat_hbm,
    w_hbm,
    refresh_hbm,
    stale_hbm,
    arr_out,
    fx_out,
    source_out,
    arr,
    source,
    fresh_own,
    pick,
    fx,
    weight,
    wcol,
    refresh,
    send_sem,
    recv_sem,
    pair_send,
    pair_recv,
    give_sem,
    take_sem,
    load_sem,
    stale_sem,
    out_sem,
    row_sem,
):
    me = Place()
    f = me.feat
    own_rows, pair_rows = half_rows(f), half_rows(1 - f)
    own_columns, pair_columns = column_block(f), column_block(1 - f)
    loads = fetch(
        load_sem, (feat_hbm, fx.at[own_rows, :]), (w_hbm, weight), (refresh_hbm, refresh)
    )
    ready = me.greet(me.a_far)
    loads[2].wait()
    chosen = refresh_by_rows(refresh[pl.ds(me.dom, 1), :])
    loads[0].wait()
    pick[own_rows, :] = dot(fx[own_rows, :], chosen).astype(BF16)
    loads[1].wait()
    wcol[own_rows, :] = weight[:, own_columns]
    ready()

    def to_pair(k, src, dst):
        return pltpu.make_async_remote_copy(
            src_ref=src,
            dst_ref=dst,
            send_sem=pair_send.at[k],
            recv_sem=pair_recv.at[k],
            device_id=(me.dom, 1 - f),
            device_id_type=MESH,
        )

    pick_copy = to_pair(0, pick.at[own_rows, :], pick.at[own_rows, :])
    pick_copy.start()
    w_copy = to_pair(1, weight.at[:, pair_columns], wcol.at[own_rows, :])
    w_copy.start()
    fx_copy = to_pair(2, fx.at[own_rows, :], fx.at[own_rows, :])

    def shard(slot, target, kind, p):
        return pltpu.make_async_remote_copy(
            src_ref=arr.at[slot],
            dst_ref=arr.at[slot],
            send_sem=send_sem.at[kind, p],
            recv_sem=recv_sem.at[slot],
            device_id=(target, f),
            device_id_type=MESH,
        )

    def arrive(slot):
        shard(slot, me.sibling, 0, 0).wait_recv()

    def slot_of(p, b_offset):
        a_offset, pair = PLANE[p]
        return me.slot(me.a + a_offset, me.b + b_offset, (me.z + pair) % 2)

    def pass_on(p):
        slot = slot_of(p, 0)
        shard(slot, me.b_next, 0, p).start()
        shard(slot, me.b_prev, 1, p).start()

    def along_a(p):
        slot = slot_of(p, 0)
        shard(slot, me.a_next, 3, p).start()
        shard(slot, me.a_prev, 4, p).start()
        shard(slot, me.a_far, 5, p).start()

    def take_plane(p):
        slot = slot_of(p, 0)
        arrive(slot)
        if p == 1:
            along_a(p)
        pass_on(p)
        return slot

    def take_b(p):
        below, above = slot_of(p, 3), slot_of(p, 1)
        arrive(below)
        if PLANE[p][1] == 0:
            shard(below, me.b_next, 2, p).start()
        arrive(above)
        if PLANE[p][1] == 1:
            shard(above, me.b_prev, 2, p).start()
        return below, above

    def take_far(p):
        slot = slot_of(p, 2)
        arrive(slot)
        return slot

    ones = jnp.ones((REF, TILE), BF16)

    class_first = me.core * CLASS

    def held(slot):
        return pl.ds(pl.multiple_of((slot - class_first) * ROWS, ROWS), ROWS)

    def rows_of(part):
        return pl.ds(pl.multiple_of(part * ROWS, ROWS), ROWS)

    def load_rows(slot):
        return pltpu.make_async_copy(
            stale_hbm.at[rows_of(slot_part(slot))], source.at[held(slot)], stale_sem.at[slot]
        )

    def keep_rows(slot):
        return pltpu.make_async_copy(
            source.at[held(slot)], source_out.at[rows_of(slot_part(slot))], row_sem.at[slot]
        )

    def give_rows(slot, src):
        return pltpu.make_async_remote_copy(
            src_ref=src,
            dst_ref=source_out.at[rows_of(slot_part(slot))],
            send_sem=give_sem.at[slot],
            recv_sem=take_sem.at[slot],
            device_id=(me.sibling, f),
            device_id_type=MESH,
        )

    mine = slot_of(0, 0)

    def merge(*slots):
        fresh = [dot(arr[pl.ds(slot, 1)][0], wcol[...]).astype(BF16) for slot in slots]
        for slot, new in zip(slots, fresh):
            chosen = refresh_by_rows(refresh[pl.ds(slot_part(slot), 1), :])
            placed = dot(chosen, jnp.concatenate([new, ones], axis=1))
            rows = held(slot)
            old = source[rows, :].astype(F32)
            source[rows, :] = jnp.where(placed[:, TILE:] > 0, placed[:, :TILE], old).astype(BF16)
        for slot in slots:
            give_rows(slot, source.at[held(slot)]).start()
            if slot is not mine:
                keep_rows(slot).start()

    pick_copy.wait_recv()
    arr[pl.ds(mine, 1)] = jnp.transpose(pick[...].astype(F32)).astype(BF16)[None]
    pair_sent = shard(mine, me.z_pair, 2, PER)
    pair_sent.start()
    along_a(0)
    pass_on(0)

    def start_load(k, carry):
        load_rows(class_first + k).start()
        return carry

    def wait_load(k, carry):
        load_rows(class_first + k).wait()
        return carry

    lax.fori_loop(0, CLASS, start_load, 0)
    left, right = take_plane(2), take_plane(3)
    b0 = take_b(0)
    z_pair = take_plane(1)
    across = take_plane(6)
    fx_copy.start()
    w_copy.wait_recv()
    lax.fori_loop(0, CLASS, wait_load, 0)
    merge(left, right, *b0)
    merge(z_pair, across, mine)
    left, right = take_plane(4), take_plane(5)
    b2, b3 = take_b(2), take_b(3)
    merge(left, right, *b2)
    across = take_plane(7)
    b1, b6 = take_b(1), take_b(6)
    merge(*b3, *b1)
    b4, b5 = take_b(4), take_b(5)
    far0 = take_far(0)
    merge(*b6, across, far0)
    b7 = take_b(7)
    merge(*b4, *b5)
    merge(*b7, take_far(2), take_far(3))
    merge(take_far(1), take_far(6), take_far(4), take_far(5))
    merge(take_far(7))
    keep_arr = pltpu.make_async_copy(arr.at[pl.ds(class_first, CLASS)], arr_out, out_sem.at[0])
    keep_arr.start()
    fx_copy.wait_recv()
    keep_fx = pltpu.make_async_copy(fx, fx_out, out_sem.at[1])
    keep_fx.start()
    fresh_own[...] = lax.dot_general(
        fx[...], wcol[...], (((0,), (0,)), ((), ())), preferred_element_type=F32
    ).astype(BF16)
    keep_own = pltpu.make_async_copy(fresh_own, source_out.at[rows_of(me.dom)], row_sem.at[mine])
    keep_own.start()

    def settle(p, carry):
        for kind in range(3):
            shard(mine, me.sibling, kind, p).wait_send()
        return carry

    lax.fori_loop(0, PER, settle, 0)
    for p in range(2):
        for kind in range(3, 6):
            shard(mine, me.sibling, kind, p).wait_send()
    pair_sent.wait_send()
    pick_copy.wait_send()
    w_copy.wait_send()
    fx_copy.wait_send()

    def settle_rows(k, carry):
        given, taken = class_first + k, CLASS - class_first + k
        give_rows(given, source.at[held(given)]).wait_send()
        give_rows(taken, source_out.at[rows_of(slot_part(taken))]).wait_recv()
        keep_rows(class_first + k).wait()
        return carry

    lax.fori_loop(0, CLASS, settle_rows, 0)
    keep_fx.wait()
    keep_arr.wait()


GROUP = 8
CHUNK = 64
TILE_RING = 3
STAGED = 16


def tiles_kernel(
    src_ref,
    dst_ref,
    count_ref,
    refresh_hbm,
    fx_hbm,
    mask_hbm,
    gh_hbm,
    source_hbm,
    tiles_hbm,
    hidden_ref,
    picked_hbm,
    own_ref,
    gw_ref,
    source,
    tiles,
    pre,
    acc,
    delta,
    refresh,
    fx,
    mask,
    gh,
    picked,
    source_sem,
    tile_sem,
    load_sem,
    out_sem,
):
    me = lax.axis_index("dom")
    live = count_ref[0]
    chunks = (live + CHUNK - 1) // CHUNK
    source_copy = pltpu.make_async_copy(source_hbm, source, source_sem)

    def tile_copy(turn):
        chunk = jnp.where(turn < chunks, turn, turn - chunks)
        place = turn % TILE_RING
        part = pl.ds(chunk * CHUNK, CHUNK)
        return pltpu.make_async_copy(tiles_hbm.at[part], tiles.at[place], tile_sem.at[place])

    tile_copy(0).start()
    source_copy.start()
    loads = fetch(
        load_sem, (mask_hbm, mask), (gh_hbm, gh), (refresh_hbm, refresh), (fx_hbm, fx)
    )
    pre[...] = jnp.zeros_like(pre)

    def clear(index, carry):
        acc[pl.ds(index * PER, PER)] = jnp.zeros((PER, TILE, TILE), F32)
        return carry

    lax.fori_loop(0, BLOCKS // PER, clear, 0)
    acc[BLOCKS] = jnp.zeros((TILE, TILE), F32)
    for turn in range(1, TILE_RING):

        @pl.when(turn < 2 * chunks)
        def _():
            tile_copy(turn).start()

    source_copy.wait()

    def next_tiles(turn):
        @pl.when(turn + TILE_RING < 2 * chunks)
        def _():
            tile_copy(turn + TILE_RING).start()

    def forward(chunk, carry):
        tile_copy(chunk).wait()
        place = chunk % TILE_RING
        for k in range(CHUNK):
            t = chunk * CHUNK + k
            rows = pl.ds(pl.multiple_of(src_ref[t] * TILE, TILE), TILE)
            product = dot(tiles[place, k], source[rows, :])
            d = jnp.where(t < live, dst_ref[t], PER)
            pre[pl.ds(d, 1)] = pre[pl.ds(d, 1)] + product[None]
        next_tiles(chunk)
        return carry

    lax.fori_loop(0, chunks, forward, 0)
    for copy in loads:
        copy.wait()
    for d in range(PER):
        total = pre[d]
        rows = pl.ds(d * TILE, TILE)
        hidden_ref[rows, :] = jnp.maximum(total, 0.0).astype(BF16)
        passed = jnp.where(total > 0, gh[rows, :].astype(F32), 0.0)
        kept = mask[pl.ds(d, 1), :].astype(F32)
        delta[d] = (jnp.transpose(passed) * kept).astype(BF16)

    def backward(chunk, carry):
        turn = chunks + chunk
        tile_copy(turn).wait()
        place = turn % TILE_RING
        for k in range(CHUNK):
            t = chunk * CHUNK + k
            product = dot(delta[dst_ref[t]], tiles[place, k])
            s = jnp.where(t < live, src_ref[t], BLOCKS)
            acc[pl.ds(s, 1)] = acc[pl.ds(s, 1)] + product[None]
        next_tiles(turn)
        return carry

    lax.fori_loop(0, chunks, backward, 0)

    def out_copy(slot):
        place = slot % STAGED
        return pltpu.make_async_copy(picked.at[place], picked_hbm.at[slot], out_sem.at[place])

    def pick(group, carry):
        for k in range(GROUP):
            slot = group * GROUP + k

            @pl.when(slot >= STAGED)
            def _():
                out_copy(slot - STAGED).wait()

        for k in range(GROUP):
            slot = group * GROUP + k
            part = slot_part(slot)
            chosen = refresh_by_rows(refresh[pl.ds(part, 1), :])
            blocks = [acc[part * PER + i].astype(BF16) for i in range(PER)]
            grads = dot(jnp.concatenate(blocks, axis=1), chosen)
            grads = jnp.where(part == me, 0.0, grads).astype(BF16)
            picked[pl.ds(slot % STAGED, 1)] = grads[None]
        for k in range(GROUP):
            out_copy(group * GROUP + k).start()
        return carry

    lax.fori_loop(0, PARTS // GROUP, pick, 0)
    for k in range(PER):
        own_ref[:, pl.ds(k * TILE, TILE)] = acc[me * PER + k].astype(BF16)
    gw_ref[...] = lax.dot_general(
        own_ref[...], fx[...], (((1,), (1,)), ((), ())), preferred_element_type=F32
    )
    for slot in range(PARTS - STAGED, PARTS):
        out_copy(slot).wait()


def scatter_kernel(
    refresh_hbm,
    w_hbm,
    own_hbm,
    gw_hbm,
    arr_hbm,
    picked_hbm,
    gf_out,
    gw_out,
    refresh,
    weight,
    own,
    own_in,
    base,
    gw,
    arr,
    work,
    sib,
    from_b1,
    from_b2,
    from_a,
    from_z,
    sum_y,
    sum_x,
    sum_out,
    sum_last,
    load_sem,
    small_sem,
    send_sem,
    recv_sem,
):
    me = Place()
    ready = me.greet(me.a_far, me.b_far, me.cross, cross=True)
    f, a, b, z = me.feat, me.a, me.b, me.z
    order = (2, 1, 3, 0)

    def first_of(center, h):
        return ((center + order[h]) % RING) * 8

    loads = []
    for h in range(RING):
        first = first_of(a, h)
        copy = pltpu.make_async_copy(
            picked_hbm.at[pl.ds(me.core * CLASS + first, 8)],
            work.at[pl.ds(first, 8)],
            load_sem.at[h],
        )
        copy.start()
        loads.append(copy)
    small = fetch(
        small_sem,
        (arr_hbm, arr),
        (gw_hbm, gw),
        (own_hbm, own),
        (w_hbm, weight),
        (refresh_hbm, refresh),
    )
    ready()
    sends = []

    def send(src, dst, target, feat=None):
        k = len(sends)
        copy = pltpu.make_async_remote_copy(
            src_ref=src,
            dst_ref=dst,
            send_sem=send_sem.at[k],
            recv_sem=recv_sem.at[k],
            device_id=(target, f if feat is None else feat),
            device_id_type=MESH,
        )
        copy.start()
        sends.append(copy)
        return copy

    def add(first, size, *others):
        part = pl.ds(first, size)
        total = work[part].astype(F32)
        for other in others:
            total = total + other.astype(F32)
        work[part] = total.astype(BF16)

    to_sib = []
    for h in range(RING):
        first = first_of(b, h)
        src = picked_hbm.at[pl.ds((1 - me.core) * CLASS + first, 8)]
        to_sib.append(send(src, sib.at[pl.ds(first, 8)], me.sibling))
    own_copy = send(own_hbm, own_in, me.dom, 1 - f)

    def column(h, offset):
        return first_of(a, h) + ((b + offset) % RING) * 2

    b1, b2 = [], []

    def fold(h):
        first = first_of(a, h)
        loads[h].wait()
        to_sib[h].wait_recv()
        add(first, 8, sib[pl.ds(first, 8)])

    def launch(h):
        far, up, down = column(h, 2), column(h, 1), column(h, 3)
        b1.append(
            (
                send(work.at[pl.ds(far, 1)], from_b1.at[h, pl.ds(0, 1)], me.b_next),
                send(work.at[pl.ds(far + 1, 1)], from_b1.at[h, pl.ds(1, 1)], me.b_prev),
            )
        )
        b2.append(
            [
                send(work.at[pl.ds(up + 1, 1)], from_b2.at[h, 0, pl.ds(1, 1)], me.b_next),
                send(work.at[pl.ds(down, 1)], from_b2.at[h, 1, pl.ds(0, 1)], me.b_prev),
            ]
        )

    def weigh(h):
        first = first_of(a, h)
        total = gw[...]
        for k in range(8):
            total = total + dot(work[pl.ds(first + k, 1)][0], arr[pl.ds(first + k, 1)][0])
        gw[...] = total

    def relay(h):
        up, down = column(h, 1), column(h, 3)
        b1[h][0].wait_recv()
        add(up, 1, from_b1[h, pl.ds(0, 1)])
        b2[h].append(send(work.at[pl.ds(up, 1)], from_b2.at[h, 0, pl.ds(0, 1)], me.b_next))
        b1[h][1].wait_recv()
        add(down + 1, 1, from_b1[h, pl.ds(1, 1)])
        b2[h].append(send(work.at[pl.ds(down + 1, 1)], from_b2.at[h, 1, pl.ds(1, 1)], me.b_prev))

    along_a = []
    a_targets = (me.a_far, me.a_next, me.a_prev)

    def finish(h):
        here = column(h, 0)
        for copy in b2[h]:
            copy.wait_recv()
        if h < 3:
            add(here, 2, from_b2[h, 0], from_b2[h, 1])
            along_a.append(send(work.at[pl.ds(here, 2)], from_a.at[h], a_targets[h]))
        else:
            for copy in along_a:
                copy.wait_recv()
            add(here, 2, from_b2[h, 0], from_b2[h, 1], from_a[0], from_a[1], from_a[2])

    def ring_sum(buffer, index, targets):
        return [send(buffer.at[index], buffer.at[index], target) for target in targets]

    def total_of(terms):
        one, two, three, four = [term.astype(F32) for term in terms]
        return (one + two) + (three + four)

    def take_sum(buffer, copies):
        for copy in copies:
            copy.wait_recv()
        return total_of([buffer[k] for k in range(RING)]).astype(BF16)

    fold(0)
    launch(0)
    small[0].wait()
    small[1].wait()
    fold(1)
    launch(1)
    fold(2)
    weigh(0)
    fold(3)
    weigh(1)
    weigh(2)
    weigh(3)
    sum_y[pl.ds(me.y, 1)] = jnp.transpose(gw[...]).astype(BF16)[None]
    y_targets = [me.xy(me.x, me.y + k) for k in (1, 3, 2)]
    y_copies = ring_sum(sum_y, me.y, y_targets)
    launch(2)
    relay(0)
    launch(3)
    relay(1)
    finish(0)
    relay(2)
    sum_x[pl.ds(me.x, 1)] = take_sum(sum_y, y_copies)[None]
    x_targets = [me.xy(me.x + k, me.y) for k in (1, 3, 2)]
    x_copies = ring_sum(sum_x, me.x, x_targets)
    finish(1)
    relay(3)
    for copy in small[2:]:
        copy.wait()
    chosen = rows_by_refresh(refresh[pl.ds(me.dom, 1), :])
    own_columns, other_columns = column_block(f), column_block(1 - f)
    own_rows, other_rows = half_rows(f), half_rows(1 - f)
    own_copy.wait_recv()
    base[...] = dot(weight[:, own_columns], own[...]) + dot(weight[:, other_columns], own_in[...])
    finish(2)
    sum_out[...] = take_sum(sum_x, x_copies)
    place = me.core * 2 + z
    sum_last[0, pl.ds(place, 1)] = sum_out[own_rows, :][None]
    last_copies = [
        send(sum_out.at[own_rows, :], sum_last.at[0, place], target)
        for target in (me.sibling, me.z_pair, me.cross)
    ]
    last_copies += [
        send(sum_out.at[other_rows, :], sum_last.at[1, place], target, 1 - f)
        for target in (me.dom, me.sibling, me.z_pair, me.cross)
    ]
    finish(3)
    here = column(3, 0)
    mine, theirs = work.at[pl.ds(here + z, 1)], work.at[pl.ds(here + 1 - z, 1)]
    z_copies = (
        send(theirs, from_z.at[pl.ds(0, 1)], me.z_pair),
        send(mine, from_z.at[pl.ds(1, 1)], me.dom, 1 - f),
        send(theirs, from_z.at[pl.ds(2, 1)], me.z_pair, 1 - f),
    )
    for copy in z_copies:
        copy.wait_recv()
    carried = work[pl.ds(here + z, 1)][0].astype(F32) + from_z[0].astype(F32)
    carried_in = from_z[1].astype(F32) + from_z[2].astype(F32)
    short = dot(weight[:, own_columns], carried.astype(BF16)) + dot(
        weight[:, other_columns], carried_in.astype(BF16)
    )
    gf_out[...] = (base[...] + dot(short.astype(BF16), chosen)).astype(BF16)
    for copy in last_copies:
        copy.wait_recv()
    gw_out[:, own_columns] = total_of([sum_last[0, k] for k in range(4)])
    gw_out[:, other_columns] = total_of([sum_last[1, k] for k in range(4)])
    for copy in sends:
        copy.wait_send()


def finish_kernel(gf_ref, gw_ref, gf_out, gw_out):
    gf_out[...] = gf_ref[...]
    gw_out[...] = gw_ref[...]


VMEM = pl.BlockSpec(memory_space=pltpu.VMEM)
SMEM = pl.BlockSpec(memory_space=pltpu.SMEM)
ANY = pl.BlockSpec(memory_space=pl.ANY)
DMA = pltpu.SemaphoreType.DMA


def shape(dims, kind):
    return jax.ShapeDtypeStruct(dims, kind)


def scratch(dims, kind):
    return pltpu.VMEM(dims, kind)


def params(**fields):
    return pltpu.CompilerParams(vmem_limit_bytes=62 * MIB, **fields)


def call_gather(features, weight, refresh, stale):
    return pl.pallas_call(
        gather_kernel,
        out_shape=(
            shape((CLASS, REF, TILE), BF16),
            shape((TILE, ROWS), BF16),
            shape((PARTS * ROWS, TILE), BF16),
        ),
        in_specs=[ANY] * 4,
        out_specs=(ANY, ANY, ANY),
        scratch_shapes=[
            scratch((PARTS, REF, TILE), BF16),
            scratch((CLASS * ROWS, TILE), BF16),
            scratch((ROWS, TILE), BF16),
            scratch((TILE, REF), BF16),
            scratch((TILE, ROWS), BF16),
            scratch((64, 2 * TILE), BF16),
            scratch((TILE, TILE), BF16),
            scratch((PARTS, REF), I32),
            DMA((6, PER + 1)),
            DMA((PARTS,)),
            DMA((3,)),
            DMA((3,)),
            DMA((PARTS,)),
            DMA((PARTS,)),
            DMA((3,)),
            DMA((PARTS,)),
            DMA((2,)),
            DMA((PARTS,)),
        ],
        compiler_params=params(collective_id=0, has_side_effects=True),
        name="gather_refreshed",
    )(features, weight, refresh, stale)


def call_tiles(src, dst, count, refresh, fx, mask, gh, source, tiles, name="tiles"):
    return pl.pallas_call(
        tiles_kernel,
        out_shape=(
            shape((ROWS, TILE), BF16),
            shape((PARTS, TILE, REF), BF16),
            shape((TILE, ROWS), BF16),
            shape((TILE, TILE), F32),
        ),
        in_specs=[SMEM] * 3 + [ANY] * 6,
        out_specs=(VMEM, ANY, VMEM, VMEM),
        scratch_shapes=[
            scratch((PARTS * ROWS, TILE), BF16),
            scratch((TILE_RING, CHUNK, TILE, TILE), BF16),
            scratch((PER + 1, TILE, TILE), F32),
            scratch((BLOCKS + 1, TILE, TILE), F32),
            scratch((PER, TILE, TILE), BF16),
            scratch((PARTS, REF), I32),
            scratch((TILE, ROWS), BF16),
            scratch((PER, TILE), I32),
            scratch((ROWS, TILE), BF16),
            scratch((STAGED, TILE, REF), BF16),
            DMA,
            DMA((TILE_RING,)),
            DMA((4,)),
            DMA((STAGED,)),
        ],
        compiler_params=params(),
        name=name,
    )(src, dst, count, refresh, fx, mask, gh, source, tiles)


def call_scatter(refresh, weight, own, gw, arr, picked):
    return pl.pallas_call(
        scatter_kernel,
        out_shape=(shape((64, ROWS), BF16), shape((64, 2 * TILE), F32)),
        in_specs=[ANY] * 6,
        out_specs=(VMEM, VMEM),
        scratch_shapes=[
            scratch((PARTS, REF), I32),
            scratch((64, 2 * TILE), BF16),
            scratch((TILE, ROWS), BF16),
            scratch((TILE, ROWS), BF16),
            scratch((64, ROWS), F32),
            scratch((TILE, TILE), F32),
            scratch((CLASS, REF, TILE), BF16),
            scratch((CLASS, TILE, REF), BF16),
            scratch((CLASS, TILE, REF), BF16),
            scratch((RING, 2, TILE, REF), BF16),
            scratch((RING, 2, 2, TILE, REF), BF16),
            scratch((3, 2, TILE, REF), BF16),
            scratch((3, TILE, REF), BF16),
            scratch((RING, TILE, TILE), BF16),
            scratch((RING, TILE, TILE), BF16),
            scratch((TILE, TILE), BF16),
            scratch((2, 4, 64, TILE), BF16),
            DMA((RING,)),
            DMA((5,)),
            DMA((48,)),
            DMA((48,)),
        ],
        compiler_params=params(collective_id=1, has_side_effects=True),
        name="scatter_gradients",
    )(refresh, weight, own, gw, arr, picked)


def call_finish(gf, gw):
    return pl.pallas_call(
        finish_kernel,
        out_shape=(shape(gf.shape, gf.dtype), shape(gw.shape, gw.dtype)),
        in_specs=[VMEM] * 2,
        out_specs=(VMEM, VMEM),
        compiler_params=params(),
        name="finish",
    )(gf, gw)


def shards(
    features,
    weight,
    stale_cache,
    adj_tiles,
    tile_src,
    tile_dst,
    tile_count,
    refresh,
    train_mask,
    grad_hidden,
):
    arr, fx, source = call_gather(features.T, weight, refresh, stale_cache)
    mask = train_mask.reshape(PER, TILE)
    hidden, picked, own, gw = call_tiles(
        tile_src,
        tile_dst,
        tile_count,
        refresh,
        fx,
        mask,
        grad_hidden,
        source,
        adj_tiles,
    )
    grads = call_scatter(refresh, weight, own, gw, arr, picked)
    grad_features, grad_weight = call_finish(*grads)
    return hidden, grad_features.T, grad_weight


def solution(mesh):
    placed = (
        P("dom", "feat"),
        P("feat", None),
        P(None, "feat"),
        P("dom", None, None),
        P("dom"),
        P("dom"),
        P("dom"),
        P(),
        P("dom"),
        P("dom", "feat"),
    )
    return jax.shard_map(
        shards,
        mesh=mesh,
        in_specs=placed,
        out_specs=(P("dom", "feat"), P("dom", "feat"), P("feat", None)),
        check_vma=False,
    )
```

```python
import jax
import jax.numpy as jnp
from jax import lax
from jax.experimental import pallas as pl
from jax.experimental.pallas import tpu as pltpu
from jax.sharding import PartitionSpec as P

MESH = pl.DeviceIdType.MESH
BF16 = jnp.bfloat16
F32 = jnp.float32
I32 = jnp.int32

ROWS = 1024
REF = 256
TILE = 128
NT = 768
PARTS = 64
BLOCKS = PARTS * ROWS // TILE
PER = ROWS // TILE
RING = 4
CLASS = PARTS // 2
MIB = 1024 * 1024


def dot(lhs, rhs):
    return jnp.dot(lhs, rhs, preferred_element_type=F32)


class Place:
    def __init__(self):
        self.dom = lax.axis_index("dom")
        self.feat = lax.axis_index("feat")
        self.core = self.dom % 2
        self.z = (self.dom // 2) % 2
        self.y = (self.dom // 4) % RING
        self.x = self.dom // 16
        self.a = self.x * (1 - self.core) + self.y * self.core
        self.b = self.y * (1 - self.core) + self.x * self.core
        self.sibling = self.dom + 1 - 2 * self.core
        self.z_pair = self.dom + 2 - 4 * self.z
        self.cross = self.sibling + 2 - 4 * self.z
        self.a_next = self.at(self.a + 1, self.b)
        self.a_prev = self.at(self.a + 3, self.b)
        self.b_next = self.at(self.a, self.b + 1)
        self.b_prev = self.at(self.a, self.b + 3)
        self.a_far = self.at(self.a + 2, self.b)
        self.b_far = self.at(self.a, self.b + 2)

    def at(self, a, b):
        a, b = a % RING, b % RING
        x = a * (1 - self.core) + b * self.core
        y = b * (1 - self.core) + a * self.core
        return ((x * RING + y) * 2 + self.z) * 2 + self.core

    def xy(self, x, y):
        return (((x % RING) * RING + y % RING) * 2 + self.z) * 2 + self.core

    def slot(self, a, b, z):
        return self.core * CLASS + (a % RING) * 8 + (b % RING) * 2 + z

    def greet(self, *more, cross=False):
        barrier = pltpu.get_barrier_semaphore()
        near = (self.sibling, self.z_pair, self.a_next, self.a_prev, self.b_next, self.b_prev)
        near = near + more
        for device in near:
            pl.semaphore_signal(barrier, inc=1, device_id=(device, self.feat), device_id_type=MESH)
        pairs = (self.dom, self.sibling, self.z_pair, self.cross) if cross else (self.dom,)
        for device in pairs:
            pl.semaphore_signal(
                barrier, inc=1, device_id=(device, 1 - self.feat), device_id_type=MESH
            )
        return lambda: pl.semaphore_wait(barrier, len(near) + len(pairs))


def slot_part(slot):
    core, a, b, z = slot // CLASS, (slot // 8) % RING, (slot // 2) % RING, slot % 2
    x = a * (1 - core) + b * core
    y = b * (1 - core) + a * core
    return ((x * RING + y) * 2 + z) * 2 + core


def rows_by_refresh(row):
    column = jnp.transpose(jnp.broadcast_to(row, (TILE, REF)))
    lanes = lax.broadcasted_iota(I32, (REF, TILE), 1)
    parts = [(column == lanes + k * TILE).astype(F32).astype(BF16) for k in range(PER)]
    return jnp.concatenate(parts, axis=1)


def refresh_by_rows(row):
    rows = lax.broadcasted_iota(jnp.int16, (ROWS, REF), 0)
    one, zero = jnp.ones((), BF16), jnp.zeros((), BF16)
    return jnp.where(rows == row.astype(jnp.int16), one, zero)


def fetch(sems, *pairs):
    copies = [pltpu.make_async_copy(src, dst, sems.at[k]) for k, (src, dst) in enumerate(pairs)]
    for copy in copies:
        copy.start()
    return copies


def half_rows(index):
    return pl.ds(pl.multiple_of(index * 64, 64), 64)


def column_block(index):
    return pl.ds(pl.multiple_of(index * TILE, TILE), TILE)


PLANE = ((0, 0), (0, 1), (3, 0), (1, 0), (3, 1), (1, 1), (2, 0), (2, 1))


def gather_kernel(
    feat_hbm,
    w_hbm,
    refresh_hbm,
    stale_hbm,
    arr_out,
    fx_out,
    source_out,
    arr,
    source,
    fresh_own,
    pick,
    fx,
    weight,
    wcol,
    refresh,
    send_sem,
    recv_sem,
    pair_send,
    pair_recv,
    give_sem,
    take_sem,
    load_sem,
    stale_sem,
    out_sem,
    row_sem,
):
    me = Place()
    f = me.feat
    own_rows, pair_rows = half_rows(f), half_rows(1 - f)
    own_columns, pair_columns = column_block(f), column_block(1 - f)
    loads = fetch(
        load_sem, (feat_hbm, fx.at[own_rows, :]), (w_hbm, weight), (refresh_hbm, refresh)
    )
    ready = me.greet(me.a_far)
    loads[2].wait()
    chosen = refresh_by_rows(refresh[pl.ds(me.dom, 1), :])
    loads[0].wait()
    pick[own_rows, :] = dot(fx[own_rows, :], chosen).astype(BF16)
    loads[1].wait()
    wcol[own_rows, :] = weight[:, own_columns]
    ready()

    def to_pair(k, src, dst):
        return pltpu.make_async_remote_copy(
            src_ref=src,
            dst_ref=dst,
            send_sem=pair_send.at[k],
            recv_sem=pair_recv.at[k],
            device_id=(me.dom, 1 - f),
            device_id_type=MESH,
        )

    pick_copy = to_pair(0, pick.at[own_rows, :], pick.at[own_rows, :])
    pick_copy.start()
    w_copy = to_pair(1, weight.at[:, pair_columns], wcol.at[own_rows, :])
    w_copy.start()
    fx_copy = to_pair(2, fx.at[own_rows, :], fx.at[own_rows, :])

    def shard(slot, target, kind, p):
        return pltpu.make_async_remote_copy(
            src_ref=arr.at[slot],
            dst_ref=arr.at[slot],
            send_sem=send_sem.at[kind, p],
            recv_sem=recv_sem.at[slot],
            device_id=(target, f),
            device_id_type=MESH,
        )

    def arrive(slot):
        shard(slot, me.sibling, 0, 0).wait_recv()

    def slot_of(p, b_offset):
        a_offset, pair = PLANE[p]
        return me.slot(me.a + a_offset, me.b + b_offset, (me.z + pair) % 2)

    def pass_on(p):
        slot = slot_of(p, 0)
        shard(slot, me.b_next, 0, p).start()
        shard(slot, me.b_prev, 1, p).start()

    def along_a(p):
        slot = slot_of(p, 0)
        shard(slot, me.a_next, 3, p).start()
        shard(slot, me.a_prev, 4, p).start()
        shard(slot, me.a_far, 5, p).start()

    def take_plane(p):
        slot = slot_of(p, 0)
        arrive(slot)
        if p == 1:
            along_a(p)
        pass_on(p)
        return slot

    def take_b(p):
        below, above = slot_of(p, 3), slot_of(p, 1)
        arrive(below)
        if PLANE[p][1] == 0:
            shard(below, me.b_next, 2, p).start()
        arrive(above)
        if PLANE[p][1] == 1:
            shard(above, me.b_prev, 2, p).start()
        return below, above

    def take_far(p):
        slot = slot_of(p, 2)
        arrive(slot)
        return slot

    ones = jnp.ones((REF, TILE), BF16)

    class_first = me.core * CLASS

    def held(slot):
        return pl.ds(pl.multiple_of((slot - class_first) * ROWS, ROWS), ROWS)

    def rows_of(part):
        return pl.ds(pl.multiple_of(part * ROWS, ROWS), ROWS)

    def load_rows(slot):
        return pltpu.make_async_copy(
            stale_hbm.at[rows_of(slot_part(slot))], source.at[held(slot)], stale_sem.at[slot]
        )

    def keep_rows(slot):
        return pltpu.make_async_copy(
            source.at[held(slot)], source_out.at[rows_of(slot_part(slot))], row_sem.at[slot]
        )

    def give_rows(slot, src):
        return pltpu.make_async_remote_copy(
            src_ref=src,
            dst_ref=source_out.at[rows_of(slot_part(slot))],
            send_sem=give_sem.at[slot],
            recv_sem=take_sem.at[slot],
            device_id=(me.sibling, f),
            device_id_type=MESH,
        )

    mine = slot_of(0, 0)

    def merge(*slots):
        fresh = [dot(arr[pl.ds(slot, 1)][0], wcol[...]).astype(BF16) for slot in slots]
        for slot, new in zip(slots, fresh):
            chosen = refresh_by_rows(refresh[pl.ds(slot_part(slot), 1), :])
            placed = dot(chosen, jnp.concatenate([new, ones], axis=1))
            rows = held(slot)
            old = source[rows, :].astype(F32)
            source[rows, :] = jnp.where(placed[:, TILE:] > 0, placed[:, :TILE], old).astype(BF16)
        for slot in slots:
            give_rows(slot, source.at[held(slot)]).start()
            if slot is not mine:
                keep_rows(slot).start()

    pick_copy.wait_recv()
    arr[pl.ds(mine, 1)] = jnp.transpose(pick[...].astype(F32)).astype(BF16)[None]
    pair_sent = shard(mine, me.z_pair, 2, PER)
    pair_sent.start()
    along_a(0)
    pass_on(0)

    def start_load(k, carry):
        load_rows(class_first + k).start()
        return carry

    def wait_load(k, carry):
        @pl.when(class_first + k != mine)
        def _():
            load_rows(class_first + k).wait()

        return carry

    lax.fori_loop(0, CLASS, start_load, 0)
    w_copy.wait_recv()
    load_rows(mine).wait()
    merge(mine)
    left, right = take_plane(2), take_plane(3)
    b0 = take_b(0)
    z_pair = take_plane(1)
    across = take_plane(6)
    fx_copy.start()
    lax.fori_loop(0, CLASS, wait_load, 0)
    merge(left, right, *b0)
    merge(z_pair, across)
    left, right = take_plane(4), take_plane(5)
    b2, b3 = take_b(2), take_b(3)
    merge(left, right, *b2)
    across = take_plane(7)
    b1, b6 = take_b(1), take_b(6)
    merge(*b3, *b1)
    b4, b5 = take_b(4), take_b(5)
    far0 = take_far(0)
    merge(*b6, across, far0)
    b7 = take_b(7)
    merge(*b4, *b5)
    merge(*b7, take_far(2), take_far(3))
    merge(take_far(1), take_far(6), take_far(4), take_far(5))
    merge(take_far(7))
    keep_arr = pltpu.make_async_copy(arr.at[pl.ds(class_first, CLASS)], arr_out, out_sem.at[0])
    keep_arr.start()
    fx_copy.wait_recv()
    keep_fx = pltpu.make_async_copy(fx, fx_out, out_sem.at[1])
    keep_fx.start()
    fresh_own[...] = lax.dot_general(
        fx[...], wcol[...], (((0,), (0,)), ((), ())), preferred_element_type=F32
    ).astype(BF16)
    keep_own = pltpu.make_async_copy(fresh_own, source_out.at[rows_of(me.dom)], row_sem.at[mine])
    keep_own.start()

    def settle(p, carry):
        for kind in range(3):
            shard(mine, me.sibling, kind, p).wait_send()
        return carry

    lax.fori_loop(0, PER, settle, 0)
    for p in range(2):
        for kind in range(3, 6):
            shard(mine, me.sibling, kind, p).wait_send()
    pair_sent.wait_send()
    pick_copy.wait_send()
    w_copy.wait_send()
    fx_copy.wait_send()

    def settle_rows(k, carry):
        given, taken = class_first + k, CLASS - class_first + k
        give_rows(given, source.at[held(given)]).wait_send()
        give_rows(taken, source_out.at[rows_of(slot_part(taken))]).wait_recv()
        keep_rows(class_first + k).wait()
        return carry

    lax.fori_loop(0, CLASS, settle_rows, 0)
    keep_fx.wait()
    keep_arr.wait()


GROUP = 8
CHUNK = 96
TILE_RING = 3
STAGED = 16


def tiles_kernel(
    src_ref,
    dst_ref,
    count_ref,
    refresh_hbm,
    fx_hbm,
    mask_hbm,
    gh_hbm,
    source_hbm,
    tiles_hbm,
    hidden_hbm,
    picked_hbm,
    own_hbm,
    gw_hbm,
    hidden,
    own,
    gw,
    source,
    tiles,
    pre,
    acc,
    delta,
    refresh,
    fx,
    mask,
    gh,
    picked,
    source_sem,
    tile_sem,
    load_sem,
    out_sem,
    early_sem,
):
    me = lax.axis_index("dom")
    live = count_ref[0]
    chunks = (live + CHUNK - 1) // CHUNK
    source_copy = pltpu.make_async_copy(source_hbm, source, source_sem)

    def tile_copy(turn):
        chunk = jnp.where(turn < chunks, turn, turn - chunks)
        place = turn % TILE_RING
        part = pl.ds(chunk * CHUNK, CHUNK)
        return pltpu.make_async_copy(tiles_hbm.at[part], tiles.at[place], tile_sem.at[place])

    tile_copy(0).start()
    source_copy.start()
    loads = fetch(
        load_sem, (mask_hbm, mask), (gh_hbm, gh), (refresh_hbm, refresh), (fx_hbm, fx)
    )
    pre[...] = jnp.zeros_like(pre)

    def clear(index, carry):
        acc[pl.ds(index * PER, PER)] = jnp.zeros((PER, TILE, TILE), F32)
        return carry

    lax.fori_loop(0, BLOCKS // PER, clear, 0)
    acc[BLOCKS] = jnp.zeros((TILE, TILE), F32)
    for turn in range(1, TILE_RING):

        @pl.when(turn < 2 * chunks)
        def _():
            tile_copy(turn).start()

    source_copy.wait()

    def next_tiles(turn):
        @pl.when(turn + TILE_RING < 2 * chunks)
        def _():
            tile_copy(turn + TILE_RING).start()

    def forward(chunk, carry):
        tile_copy(chunk).wait()
        place = chunk % TILE_RING
        for k in range(CHUNK):
            t = chunk * CHUNK + k
            rows = pl.ds(pl.multiple_of(src_ref[t] * TILE, TILE), TILE)
            product = dot(tiles[place, k], source[rows, :])
            d = jnp.where(t < live, dst_ref[t], PER)
            pre[pl.ds(d, 1)] = pre[pl.ds(d, 1)] + product[None]
        next_tiles(chunk)
        return carry

    lax.fori_loop(0, chunks, forward, 0)
    for copy in loads:
        copy.wait()
    for d in range(PER):
        total = pre[d]
        rows = pl.ds(d * TILE, TILE)
        hidden[rows, :] = jnp.maximum(total, 0.0).astype(BF16)
        passed = jnp.where(total > 0, gh[rows, :].astype(F32), 0.0)
        kept = mask[pl.ds(d, 1), :].astype(F32)
        delta[d] = (jnp.transpose(passed) * kept).astype(BF16)

    hidden_copy = pltpu.make_async_copy(hidden, hidden_hbm, early_sem.at[0])
    hidden_copy.start()

    def backward(chunk, carry):
        turn = chunks + chunk
        tile_copy(turn).wait()
        place = turn % TILE_RING
        for k in range(CHUNK):
            t = chunk * CHUNK + k
            product = dot(delta[dst_ref[t]], tiles[place, k])
            s = jnp.where(t < live, src_ref[t], BLOCKS)
            acc[pl.ds(s, 1)] = acc[pl.ds(s, 1)] + product[None]
        next_tiles(turn)
        return carry

    lax.fori_loop(0, chunks, backward, 0)
    for k in range(PER):
        own[:, pl.ds(k * TILE, TILE)] = acc[me * PER + k].astype(BF16)
    gw[...] = lax.dot_general(
        own[...], fx[...], (((1,), (1,)), ((), ())), preferred_element_type=F32
    )
    own_copy = pltpu.make_async_copy(own, own_hbm, early_sem.at[1])
    own_copy.start()
    gw_copy = pltpu.make_async_copy(gw, gw_hbm, early_sem.at[2])
    gw_copy.start()

    def out_copy(slot):
        place = slot % STAGED
        return pltpu.make_async_copy(picked.at[place], picked_hbm.at[slot], out_sem.at[place])

    def pick(group, carry):
        for k in range(GROUP):
            slot = group * GROUP + k

            @pl.when(slot >= STAGED)
            def _():
                out_copy(slot - STAGED).wait()

        for k in range(GROUP):
            slot = group * GROUP + k
            part = slot_part(slot)
            chosen = refresh_by_rows(refresh[pl.ds(part, 1), :])
            blocks = [acc[part * PER + i].astype(BF16) for i in range(PER)]
            grads = dot(jnp.concatenate(blocks, axis=1), chosen)
            grads = jnp.where(part == me, 0.0, grads).astype(BF16)
            picked[pl.ds(slot % STAGED, 1)] = grads[None]
        for k in range(GROUP):
            out_copy(group * GROUP + k).start()
        return carry

    lax.fori_loop(0, PARTS // GROUP, pick, 0)
    hidden_copy.wait()
    own_copy.wait()
    gw_copy.wait()
    for slot in range(PARTS - STAGED, PARTS):
        out_copy(slot).wait()


def scatter_kernel(
    refresh_hbm,
    w_hbm,
    own_hbm,
    gw_hbm,
    arr_hbm,
    picked_hbm,
    gf_out,
    gw_out,
    refresh,
    weight,
    own,
    own_in,
    base,
    gw,
    arr,
    work,
    sib,
    from_b1,
    from_b2,
    from_a,
    from_z,
    sum_y,
    sum_x,
    sum_out,
    sum_last,
    load_sem,
    small_sem,
    send_sem,
    recv_sem,
):
    me = Place()
    ready = me.greet(me.a_far, me.b_far, me.cross, cross=True)
    f, a, b, z = me.feat, me.a, me.b, me.z
    order = (2, 1, 3, 0)

    def first_of(center, h):
        return ((center + order[h]) % RING) * 8

    loads = []
    for h in range(RING):
        first = first_of(a, h)
        copy = pltpu.make_async_copy(
            picked_hbm.at[pl.ds(me.core * CLASS + first, 8)],
            work.at[pl.ds(first, 8)],
            load_sem.at[h],
        )
        copy.start()
        loads.append(copy)
    small = fetch(
        small_sem,
        (arr_hbm, arr),
        (gw_hbm, gw),
        (own_hbm, own),
        (w_hbm, weight),
        (refresh_hbm, refresh),
    )
    ready()
    sends = []

    def send(src, dst, target, feat=None):
        k = len(sends)
        copy = pltpu.make_async_remote_copy(
            src_ref=src,
            dst_ref=dst,
            send_sem=send_sem.at[k],
            recv_sem=recv_sem.at[k],
            device_id=(target, f if feat is None else feat),
            device_id_type=MESH,
        )
        copy.start()
        sends.append(copy)
        return copy

    def add(first, size, *others):
        part = pl.ds(first, size)
        total = work[part].astype(F32)
        for other in others:
            total = total + other.astype(F32)
        work[part] = total.astype(BF16)

    to_sib = []
    for h in range(RING):
        first = first_of(b, h)
        src = picked_hbm.at[pl.ds((1 - me.core) * CLASS + first, 8)]
        to_sib.append(send(src, sib.at[pl.ds(first, 8)], me.sibling))
    own_copy = send(own_hbm, own_in, me.dom, 1 - f)

    def column(h, offset):
        return first_of(a, h) + ((b + offset) % RING) * 2

    b1, b2 = [], []

    def fold(h):
        first = first_of(a, h)
        loads[h].wait()
        to_sib[h].wait_recv()
        add(first, 8, sib[pl.ds(first, 8)])

    def launch(h):
        far, up, down = column(h, 2), column(h, 1), column(h, 3)
        b1.append(
            (
                send(work.at[pl.ds(far, 1)], from_b1.at[h, pl.ds(0, 1)], me.b_next),
                send(work.at[pl.ds(far + 1, 1)], from_b1.at[h, pl.ds(1, 1)], me.b_prev),
            )
        )
        b2.append(
            [
                send(work.at[pl.ds(up + 1, 1)], from_b2.at[h, 0, pl.ds(1, 1)], me.b_next),
                send(work.at[pl.ds(down, 1)], from_b2.at[h, 1, pl.ds(0, 1)], me.b_prev),
            ]
        )

    def weigh(h):
        first = first_of(a, h)
        total = gw[...]
        for k in range(8):
            total = total + dot(work[pl.ds(first + k, 1)][0], arr[pl.ds(first + k, 1)][0])
        gw[...] = total

    def relay(h):
        up, down = column(h, 1), column(h, 3)
        b1[h][0].wait_recv()
        add(up, 1, from_b1[h, pl.ds(0, 1)])
        b2[h].append(send(work.at[pl.ds(up, 1)], from_b2.at[h, 0, pl.ds(0, 1)], me.b_next))
        b1[h][1].wait_recv()
        add(down + 1, 1, from_b1[h, pl.ds(1, 1)])
        b2[h].append(send(work.at[pl.ds(down + 1, 1)], from_b2.at[h, 1, pl.ds(1, 1)], me.b_prev))

    along_a = []
    a_targets = (me.a_far, me.a_next, me.a_prev)

    def finish(h):
        here = column(h, 0)
        for copy in b2[h]:
            copy.wait_recv()
        if h < 3:
            add(here, 2, from_b2[h, 0], from_b2[h, 1])
            along_a.append(send(work.at[pl.ds(here, 2)], from_a.at[h], a_targets[h]))
        else:
            for copy in along_a:
                copy.wait_recv()
            add(here, 2, from_b2[h, 0], from_b2[h, 1], from_a[0], from_a[1], from_a[2])

    def ring_sum(buffer, index, targets):
        return [send(buffer.at[index], buffer.at[index], target) for target in targets]

    def total_of(terms):
        one, two, three, four = [term.astype(F32) for term in terms]
        return (one + two) + (three + four)

    def take_sum(buffer, copies):
        for copy in copies:
            copy.wait_recv()
        return total_of([buffer[k] for k in range(RING)]).astype(BF16)

    fold(0)
    launch(0)
    small[0].wait()
    small[1].wait()
    fold(1)
    launch(1)
    fold(2)
    weigh(0)
    fold(3)
    weigh(1)
    weigh(2)
    weigh(3)
    sum_y[pl.ds(me.y, 1)] = jnp.transpose(gw[...]).astype(BF16)[None]
    y_targets = [me.xy(me.x, me.y + k) for k in (1, 3, 2)]
    y_copies = ring_sum(sum_y, me.y, y_targets)
    launch(2)
    relay(0)
    launch(3)
    relay(1)
    finish(0)
    relay(2)
    sum_x[pl.ds(me.x, 1)] = take_sum(sum_y, y_copies)[None]
    x_targets = [me.xy(me.x + k, me.y) for k in (1, 3, 2)]
    x_copies = ring_sum(sum_x, me.x, x_targets)
    finish(1)
    relay(3)
    own_rows, other_rows = half_rows(f), half_rows(1 - f)
    finish(2)
    sum_out[...] = take_sum(sum_x, x_copies)
    place = me.core * 2 + z
    sum_last[0, pl.ds(place, 1)] = sum_out[own_rows, :][None]
    last_copies = [
        send(sum_out.at[own_rows, :], sum_last.at[0, place], target)
        for target in (me.sibling, me.z_pair, me.cross)
    ]
    last_copies += [
        send(sum_out.at[other_rows, :], sum_last.at[1, place], target, 1 - f)
        for target in (me.dom, me.sibling, me.z_pair, me.cross)
    ]
    finish(3)
    here = column(3, 0)
    mine, theirs = work.at[pl.ds(here + z, 1)], work.at[pl.ds(here + 1 - z, 1)]
    z_copies = (
        send(theirs, from_z.at[pl.ds(0, 1)], me.z_pair),
        send(mine, from_z.at[pl.ds(1, 1)], me.dom, 1 - f),
        send(theirs, from_z.at[pl.ds(2, 1)], me.z_pair, 1 - f),
    )
    for copy in small[2:]:
        copy.wait()
    chosen = rows_by_refresh(refresh[pl.ds(me.dom, 1), :])
    own_columns, other_columns = column_block(f), column_block(1 - f)
    own_copy.wait_recv()
    base[...] = dot(weight[:, own_columns], own[...]) + dot(weight[:, other_columns], own_in[...])
    for copy in last_copies:
        copy.wait_recv()
    gw_out[:, own_columns] = total_of([sum_last[0, k] for k in range(4)])
    gw_out[:, other_columns] = total_of([sum_last[1, k] for k in range(4)])
    for copy in z_copies:
        copy.wait_recv()
    carried = work[pl.ds(here + z, 1)][0].astype(F32) + from_z[0].astype(F32)
    carried_in = from_z[1].astype(F32) + from_z[2].astype(F32)
    short = dot(weight[:, own_columns], carried.astype(BF16)) + dot(
        weight[:, other_columns], carried_in.astype(BF16)
    )
    gf_out[...] = (base[...] + dot(short.astype(BF16), chosen)).astype(BF16)
    for copy in sends:
        copy.wait_send()


def finish_kernel(gf_ref, gw_ref, gf_out, gw_out):
    gf_out[...] = gf_ref[...]
    gw_out[...] = gw_ref[...]


VMEM = pl.BlockSpec(memory_space=pltpu.VMEM)
SMEM = pl.BlockSpec(memory_space=pltpu.SMEM)
ANY = pl.BlockSpec(memory_space=pl.ANY)
DMA = pltpu.SemaphoreType.DMA


def shape(dims, kind):
    return jax.ShapeDtypeStruct(dims, kind)


def scratch(dims, kind):
    return pltpu.VMEM(dims, kind)


def params(**fields):
    return pltpu.CompilerParams(vmem_limit_bytes=62 * MIB, **fields)


def call_gather(features, weight, refresh, stale):
    return pl.pallas_call(
        gather_kernel,
        out_shape=(
            shape((CLASS, REF, TILE), BF16),
            shape((TILE, ROWS), BF16),
            shape((PARTS * ROWS, TILE), BF16),
        ),
        in_specs=[ANY] * 4,
        out_specs=(ANY, ANY, ANY),
        scratch_shapes=[
            scratch((PARTS, REF, TILE), BF16),
            scratch((CLASS * ROWS, TILE), BF16),
            scratch((ROWS, TILE), BF16),
            scratch((TILE, REF), BF16),
            scratch((TILE, ROWS), BF16),
            scratch((64, 2 * TILE), BF16),
            scratch((TILE, TILE), BF16),
            scratch((PARTS, REF), I32),
            DMA((6, PER + 1)),
            DMA((PARTS,)),
            DMA((3,)),
            DMA((3,)),
            DMA((PARTS,)),
            DMA((PARTS,)),
            DMA((3,)),
            DMA((PARTS,)),
            DMA((2,)),
            DMA((PARTS,)),
        ],
        compiler_params=params(collective_id=0, has_side_effects=True),
        name="gather_refreshed",
    )(features, weight, refresh, stale)


def call_tiles(src, dst, count, refresh, fx, mask, gh, source, tiles, name="tiles"):
    return pl.pallas_call(
        tiles_kernel,
        out_shape=(
            shape((ROWS, TILE), BF16),
            shape((PARTS, TILE, REF), BF16),
            shape((TILE, ROWS), BF16),
            shape((TILE, TILE), F32),
        ),
        in_specs=[SMEM] * 3 + [ANY] * 6,
        out_specs=(ANY, ANY, ANY, ANY),
        scratch_shapes=[
            scratch((ROWS, TILE), BF16),
            scratch((TILE, ROWS), BF16),
            scratch((TILE, TILE), F32),
            scratch((PARTS * ROWS, TILE), BF16),
            scratch((TILE_RING, CHUNK, TILE, TILE), BF16),
            scratch((PER + 1, TILE, TILE), F32),
            scratch((BLOCKS + 1, TILE, TILE), F32),
            scratch((PER, TILE, TILE), BF16),
            scratch((PARTS, REF), I32),
            scratch((TILE, ROWS), BF16),
            scratch((PER, TILE), I32),
            scratch((ROWS, TILE), BF16),
            scratch((STAGED, TILE, REF), BF16),
            DMA,
            DMA((TILE_RING,)),
            DMA((4,)),
            DMA((STAGED,)),
            DMA((3,)),
        ],
        compiler_params=params(),
        name=name,
    )(src, dst, count, refresh, fx, mask, gh, source, tiles)


def call_scatter(refresh, weight, own, gw, arr, picked):
    return pl.pallas_call(
        scatter_kernel,
        out_shape=(shape((64, ROWS), BF16), shape((64, 2 * TILE), F32)),
        in_specs=[ANY] * 6,
        out_specs=(VMEM, VMEM),
        scratch_shapes=[
            scratch((PARTS, REF), I32),
            scratch((64, 2 * TILE), BF16),
            scratch((TILE, ROWS), BF16),
            scratch((TILE, ROWS), BF16),
            scratch((64, ROWS), F32),
            scratch((TILE, TILE), F32),
            scratch((CLASS, REF, TILE), BF16),
            scratch((CLASS, TILE, REF), BF16),
            scratch((CLASS, TILE, REF), BF16),
            scratch((RING, 2, TILE, REF), BF16),
            scratch((RING, 2, 2, TILE, REF), BF16),
            scratch((3, 2, TILE, REF), BF16),
            scratch((3, TILE, REF), BF16),
            scratch((RING, TILE, TILE), BF16),
            scratch((RING, TILE, TILE), BF16),
            scratch((TILE, TILE), BF16),
            scratch((2, 4, 64, TILE), BF16),
            DMA((RING,)),
            DMA((5,)),
            DMA((48,)),
            DMA((48,)),
        ],
        compiler_params=params(collective_id=1, has_side_effects=True),
        name="scatter_gradients",
    )(refresh, weight, own, gw, arr, picked)


def call_finish(gf, gw):
    return pl.pallas_call(
        finish_kernel,
        out_shape=(shape(gf.shape, gf.dtype), shape(gw.shape, gw.dtype)),
        in_specs=[VMEM] * 2,
        out_specs=(VMEM, VMEM),
        compiler_params=params(),
        name="finish",
    )(gf, gw)


def shards(
    features,
    weight,
    stale_cache,
    adj_tiles,
    tile_src,
    tile_dst,
    tile_count,
    refresh,
    train_mask,
    grad_hidden,
):
    arr, fx, source = call_gather(features.T, weight, refresh, stale_cache)
    mask = train_mask.reshape(PER, TILE)
    hidden, picked, own, gw = call_tiles(
        tile_src,
        tile_dst,
        tile_count,
        refresh,
        fx,
        mask,
        grad_hidden,
        source,
        adj_tiles,
    )
    grads = call_scatter(refresh, weight, own, gw, arr, picked)
    grad_features, grad_weight = call_finish(*grads)
    return hidden, grad_features.T, grad_weight


def solution(mesh):
    placed = (
        P("dom", "feat"),
        P("feat", None),
        P(None, "feat"),
        P("dom", None, None),
        P("dom"),
        P("dom"),
        P("dom"),
        P(),
        P("dom"),
        P("dom", "feat"),
    )
    return jax.shard_map(
        shards,
        mesh=mesh,
        in_specs=placed,
        out_specs=(P("dom", "feat"), P("dom", "feat"), P("feat", None)),
        check_vma=False,
    )
```
